256 devices in a mesh: dp: 128 (over z, y, x_hi, core), seq: 2 (over x_lo).
Axes of the slice: x: 4 (x_hi: 2, x_lo: 2; x = x_hi * 2 + x_lo), y: 4, z: 8, core: 2. Of those that a mesh axis runs over, the one named last changes fastest.
Arguments:
- hidden: bfloat16 [49152, 4096], P('dp'), may hold values from -6 to 6
- queries: bfloat16 [49152, 4096], P('dp', 'seq')
- keys: bfloat16 [49152, 1024], P('dp', 'seq')
- value_codes: bfloat16 [4096, 1024], P('dp', 'seq'), may hold values from -127 to 127, as said below
- value_scale: float32 [1024], P('seq'), may hold values from 0.0001 to 0.0004
- upstream: bfloat16 [49152, 4096], P('dp', 'seq'), may hold values from -6 to 6
- lengths: int32 [128, 4], P('dp'), may hold values from 1 to 288, 384 in all within a row
Outputs:
- grad_queries: bfloat16 [49152, 4096], P('dp', 'seq')
- grad_keys: bfloat16 [49152, 1024], P('dp', 'seq')
- grad_hidden: bfloat16 [49152, 4096], P('dp', 'seq')
- grad_log_scale: float32 [1024], P('seq')
The draws below stay inside these ranges and needn't reach their ends.
Inputs may be any that keep to these rules, and one draw needn't show every extreme that they name: Each row holds the lengths of a pack's documents; the longest document of every pack has exactly 288 tokens. `value_codes`: whole numbers.
All inputs are finite; a program needn't handle non-finite values.
Results may differ from the reference program's by a relative error of at most 0.0076.
Values may be sent and summed in bfloat16 or wider, within the bound.
No kernel may reach another device: no remote copies, remote signals or barrier semaphores. Data moves between devices by JAX's collectives and lax.ppermute only.
A program may use at most 128 MiB of HBM per device.

```python
import math
import jax
import jax.numpy as jnp
import numpy as np
from jax import lax

D = 4096
HEADS = 32
KV_HEADS = 8
KVD = 1024
PACK = 384
DOCS = 4
LONGEST = 288
TOKENS = 49152
N_DP = 128


def shared_keys(key):
    return jnp.clip(jax.random.normal(key, (TOKENS, KVD), jnp.float32), -4.0, 4.0)


def draw_keys(key, part):
    base = shared_keys(key)
    return base.astype(jnp.bfloat16)


def draw_queries(key, part):
    key = jax.random.fold_in(key, 2)
    fresh = jnp.clip(jax.random.normal(key, (TOKENS, D), jnp.float32), -4.0, 4.0)
    return fresh.astype(jnp.bfloat16)


def draw_value_codes(key, part):
    key = jax.random.fold_in(key, 3)
    codes = jax.random.randint(key, (D, KVD), -127, 128)
    return codes.astype(jnp.float32).astype(jnp.bfloat16)


def block_levels(rng, shape, shards, least, top_value):
    def one(axis_at, parts):
        heights = jax.random.uniform(jax.random.fold_in(jax.random.fold_in(rng, 6), axis_at), (parts,), jnp.float32, least / len(shards), top_value / len(shards))
        return jnp.repeat(jnp.exp(heights), shape[axis_at] // parts).reshape((-1,) + (1,) * (len(shape) - axis_at - 1))

    gain = one(*shards[0])
    for cut in shards[1:]:
        gain = gain * one(*cut)
    return gain


def split_up(count, total, limit, slope):
    loads = [(1 << 20) // math.isqrt(grade ** slope) + 1 for grade in range(2, count + 1)]
    spare, holding = total - limit - (count - 1), [1] * (count - 1)
    while spare > 0:
        movable = [i for i in range(count - 1) if holding[i] < limit]
        mass, budget = sum([loads[i] for i in movable]), spare
        for i in movable:
            extra = min(limit - holding[i], max(1, budget * loads[i] // mass), spare)
            holding[i] = holding[i] + extra
            spare = spare - extra
    return np.array([limit] + holding)


def ragged_sizes(key, count, total, reach, slope):
    if count == 2:
        one = jax.random.randint(key, (), max(1, total - reach), min(reach, total - 1) + 1)
        return jnp.stack([one, total - one])
    sizes = jnp.asarray(split_up(count, total, reach, slope), jnp.int32)
    pairs = (count - 1) // 2
    source_of, taker = sizes[1:1 + 2 * pairs:2], sizes[2:2 + 2 * pairs:2]
    margin = jnp.minimum(source_of - 1, reach - taker)
    moved = jax.random.randint(jax.random.fold_in(key, 1), (pairs,), 0, 1 << 20) % (margin + 1)
    sizes = sizes.at[1:1 + 2 * pairs:2].set(source_of - moved).at[2:2 + 2 * pairs:2].set(taker + moved)
    return sizes[jax.random.permutation(jax.random.fold_in(key, 2), count)]


def gaussian(stream_key, extent, width, limit, split=(), held_as=jnp.bfloat16):
    factor_of = block_levels(stream_key, extent, split, -0.22, 0.18) if split else 1.0
    result = jax.random.normal(stream_key, extent, jnp.float32) * width * factor_of
    return jnp.minimum(jnp.maximum(result, -limit), limit).astype(held_as)


def setup_inputs(seed: int = 0) -> dict:
    streams_of = jax.random.split(jax.random.key(seed), 8)
    return {
        "hidden": gaussian(streams_of[0], (TOKENS, D), 1.0, 6.0, ((0, 128),)),
        "queries": draw_queries(jax.random.fold_in(streams_of[7], 71), 0),
        "keys": draw_keys(jax.random.fold_in(streams_of[7], 71), 0),
        "value_codes": draw_value_codes(jax.random.fold_in(streams_of[7], 71), 0),
        "value_scale": jnp.clip(jnp.exp(math.log(0.0004) - 1.3862944 * jax.random.uniform(streams_of[4], (KVD,), jnp.float32) ** block_levels(streams_of[4], (KVD,), ((0, 2),), -0.2, 0.2)), 0.0001, 0.0004),
        "upstream": gaussian(streams_of[5], (TOKENS, D), 1.0, 6.0, ((0, 128), (1, 2))),
        "lengths": jax.vmap(lambda own: ragged_sizes(own, DOCS, PACK, LONGEST, 2))(jax.random.split(streams_of[6], N_DP)).reshape((N_DP, DOCS)).astype(jnp.int32),
    }


def documents(lengths_row, count):
    ends = jnp.cumsum(lengths_row.astype(jnp.int32))
    positions = jnp.arange(count).astype(jnp.int32)
    return jnp.sum((positions[:, None] >= ends[None, :]).astype(jnp.int32), axis=1).astype(jnp.int32)


def attend(query_rows, cotangent, key_rows, value_rows, positions, doc):
    count = query_rows.shape[0]
    head_dim = D // HEADS
    group = HEADS // KV_HEADS
    kv_count = key_rows.shape[1] // head_dim
    factor = 1.0 / (head_dim ** 0.5)
    qs = query_rows.astype(jnp.float32).reshape(count, kv_count, group, head_dim)
    dos = cotangent.astype(jnp.float32).reshape(count, kv_count, group, head_dim)
    ks = key_rows.astype(jnp.float32).reshape(count, kv_count, head_dim)
    vs = value_rows.astype(jnp.float32).reshape(count, kv_count, head_dim)
    scores = jnp.einsum("qgmd,kgd->gmqk", qs, ks) * factor
    keep = (positions[None, :] <= positions[:, None]) & (doc[None, :] == doc[:, None])
    scores = jnp.where(keep[None, None], scores, -1e30)
    top = jnp.max(scores, axis=-1, keepdims=True)
    expo = jnp.exp(scores - top)
    probs = expo / jnp.sum(expo, axis=-1, keepdims=True)
    probs_low = probs.astype(jnp.bfloat16).astype(jnp.float32)
    out = jnp.einsum("gmqk,kgd->qgmd", probs_low, vs)
    dprobs = jnp.einsum("qgmd,kgd->gmqk", dos, vs)
    delta = jnp.transpose(jnp.sum(dos * out, axis=-1), (1, 2, 0))
    dscores = (probs * (dprobs - delta[..., None])).astype(jnp.bfloat16).astype(jnp.float32)
    dquery = jnp.einsum("gmqk,kgd->qgmd", dscores, ks) * factor
    dkey = jnp.einsum("gmqk,qgmd->kgd", dscores, qs) * factor
    dvalue = jnp.einsum("gmqk,qgmd->kgd", probs_low, dos)
    return dquery.reshape(count, -1), dkey.reshape(count, kv_count * head_dim), dvalue.reshape(count, kv_count * head_dim)


def reference(hidden, queries, keys, value_codes, value_scale, upstream, lengths):
    packs = hidden.shape[0] // PACK
    width_kv = keys.shape[1]
    raw = jnp.dot(hidden, value_codes, preferred_element_type=jnp.float32)
    values = (raw * value_scale[None, :]).astype(jnp.bfloat16)

    def one_pack(items):
        query_rows, cotangent, key_rows, value_rows, lengths_row = items
        doc = documents(lengths_row, PACK)
        positions = jnp.arange(PACK).astype(jnp.int32)
        return attend(query_rows, cotangent, key_rows, value_rows, positions, doc)

    dquery, dkey, dvalue = lax.map(one_pack, (queries.reshape(packs, PACK, D), upstream.reshape(packs, PACK, D), keys.reshape(packs, PACK, width_kv), values.reshape(packs, PACK, width_kv), lengths))
    dvalue = dvalue.reshape(packs * PACK, width_kv)
    grad_queries = dquery.reshape(packs * PACK, D).astype(jnp.bfloat16)
    grad_keys = dkey.reshape(packs * PACK, width_kv).astype(jnp.bfloat16)
    grad_log_scale = value_scale * jnp.sum(dvalue * raw, axis=0)
    scaled = (dvalue * value_scale[None, :]).astype(jnp.bfloat16)
    grad_hidden = lax.dot_general(scaled, value_codes, (((1,), (1,)), ((), ())), preferred_element_type=jnp.float32).astype(jnp.bfloat16)
    return grad_queries, grad_keys, grad_hidden, grad_log_scale
```

```python
import functools
import math

import jax
import jax.numpy as jnp
from jax import lax
from jax.experimental import pallas as pl
from jax.experimental.pallas import tpu as pltpu
from jax.sharding import PartitionSpec as P

COUNT = 384
HEAD = 128
GROUP = 4
BLOCK = 128
BLOCKS = COUNT // BLOCK
FACTOR = 1.0 / math.sqrt(HEAD)
LOG2E = math.log2(math.e)
BF16 = jnp.bfloat16
F32 = jnp.float32
VMEM_LIMIT = 40 * 1024 * 1024


def dot(a, b, dims):
    return lax.dot_general(a, b, ((dims[:1], dims[1:]), ((), ())), preferred_element_type=F32)


def probs_kernel(lengths_ref, q_ref, k_ref, up_ref, scale_ref, p_ref, dv_ref, scaled_ref, bias_ref, dv_acc):
    @pl.when(pl.program_id(0) == 0)
    def _():
        rows = lax.broadcasted_iota(jnp.int32, (COUNT, COUNT), 0)
        cols = lax.broadcasted_iota(jnp.int32, (COUNT, COUNT), 1)
        start = jnp.zeros((COUNT, COUNT), jnp.int32)
        end = jnp.int32(0)
        for doc in range(3):
            end = end + lengths_ref[0, doc]
            start = jnp.where(rows >= end, end, start)
        bias_ref[...] = jnp.where((cols <= rows) & (cols >= start), 0.0, -1e30).astype(F32)

    dv_acc[...] = jnp.zeros_like(dv_acc)
    for i in range(BLOCKS):
        width = BLOCK * (i + 1)
        at = pl.ds(BLOCK * i, BLOCK)
        keys = k_ref[:width, :]
        for h in range(GROUP):
            head = pl.ds(HEAD * h, HEAD)
            scores = dot(q_ref[at, head], keys, (1, 1)) * (FACTOR * LOG2E) + bias_ref[at, :width]
            expo = jnp.exp2(scores - jnp.max(scores, axis=1, keepdims=True))
            probs = expo * (1.0 / jnp.sum(expo, axis=1, keepdims=True))
            p_ref[h, at, :width] = probs.astype(BF16)
        low = jnp.concatenate([p_ref[h, at, :width] for h in range(GROUP)], axis=0)
        ups = jnp.concatenate([up_ref[at, pl.ds(HEAD * h, HEAD)] for h in range(GROUP)], axis=0)
        dv_acc[:width, :] += dot(low, ups, (0, 0))
    dv_ref[...] = dv_acc[...]
    scaled_ref[...] = (dv_acc[...] * scale_ref[...]).astype(BF16)


def probs_part(lengths, queries, keys, upstream, scale):
    wide = pl.BlockSpec((COUNT, GROUP * HEAD), lambda g: (0, g))
    narrow = pl.BlockSpec((COUNT, HEAD), lambda g: (0, g))
    kv = keys.shape[1] // HEAD
    return pl.pallas_call(
        probs_kernel,
        grid=(kv,),
        in_specs=[pl.BlockSpec(memory_space=pltpu.SMEM), wide, narrow, wide, pl.BlockSpec((1, HEAD), lambda g: (0, g))],
        out_specs=[pl.BlockSpec((GROUP, COUNT, COUNT), lambda g: (g, 0, 0)), narrow, narrow],
        out_shape=[
            jax.ShapeDtypeStruct((kv * GROUP, COUNT, COUNT), BF16),
            jax.ShapeDtypeStruct(keys.shape, F32),
            jax.ShapeDtypeStruct(keys.shape, BF16),
        ],
        scratch_shapes=[pltpu.VMEM((COUNT, COUNT), F32), pltpu.VMEM((COUNT, HEAD), F32)],
        compiler_params=pltpu.CompilerParams(vmem_limit_bytes=VMEM_LIMIT),
        cost_estimate=pl.CostEstimate(flops=2_400_000_000, bytes_accessed=9_000_000, transcendentals=1_600_000),
        name="probs_part",
    )(lengths, queries, keys, upstream, scale)


def grads_kernel(q_ref, k_ref, up_ref, v_ref, p_ref, gq_ref, gk_ref, ds_ref, dk_acc):
    dk_acc[...] = jnp.zeros_like(dk_acc)
    for i in range(BLOCKS):
        width = BLOCK * (i + 1)
        at = pl.ds(BLOCK * i, BLOCK)
        keys = k_ref[:width, :]
        values = v_ref[:width, :]
        for h in range(GROUP):
            head = pl.ds(HEAD * h, HEAD)
            dprobs = dot(up_ref[at, head], values, (1, 1))
            probs = p_ref[h, at, :width].astype(F32)
            delta = jnp.sum(probs * dprobs, axis=1, keepdims=True)
            dscores = (probs * (dprobs - delta)).astype(BF16)
            ds_ref[pl.ds(BLOCK * h, BLOCK), :width] = dscores
            gq_ref[at, head] = (dot(dscores, keys, (1, 0)) * FACTOR).astype(BF16)
        qs = jnp.concatenate([q_ref[at, pl.ds(HEAD * h, HEAD)] for h in range(GROUP)], axis=0)
        dk_acc[:width, :] += dot(ds_ref[:, :width], qs, (0, 0))
    gk_ref[...] = (dk_acc[...] * FACTOR).astype(BF16)


def grads_part(queries, keys, upstream, values, probs):
    wide = pl.BlockSpec((COUNT, GROUP * HEAD), lambda g: (0, g))
    narrow = pl.BlockSpec((COUNT, HEAD), lambda g: (0, g))
    kv = keys.shape[1] // HEAD
    return pl.pallas_call(
        grads_kernel,
        grid=(kv,),
        in_specs=[wide, narrow, wide, narrow, pl.BlockSpec((GROUP, COUNT, COUNT), lambda g: (g, 0, 0))],
        out_specs=[wide, narrow],
        out_shape=[jax.ShapeDtypeStruct(queries.shape, BF16), jax.ShapeDtypeStruct(keys.shape, BF16)],
        scratch_shapes=[pltpu.VMEM((GROUP * BLOCK, COUNT), BF16), pltpu.VMEM((COUNT, HEAD), F32)],
        compiler_params=pltpu.CompilerParams(vmem_limit_bytes=VMEM_LIMIT),
        cost_estimate=pl.CostEstimate(flops=2_400_000_000, bytes_accessed=9_000_000, transcendentals=0),
        name="grads_part",
    )(queries, keys, upstream, values, probs)


Z_ORDER = (0, 4, 2, 6, 1, 5, 3, 7)
SHARD = 32
HALF = 256


def raw_kernel(at_ref, hidden_ref, dv_ref, scale_ref, *refs):
    pieces, (codes_ref, values_ref, sums_ref, raw_ref) = refs[:-4], refs[-4:]
    z, y, x, c = at_ref[0], at_ref[1], at_ref[2], at_ref[3]

    def place(piece, row, zi, k, xi, ci, col):
        to = (((z ^ Z_ORDER[zi]) * 4 + ((y + 4 - k) & 3)) * 2 + (x ^ xi)) * 2 + (c ^ ci)
        rows = pl.ds(pl.multiple_of(to * SHARD, SHARD), SHARD)
        codes_ref[rows, pl.ds(col, HALF)] = piece[pl.ds(row, SHARD), :]

    for ci in range(2):
        for k in range(4):
            piece = pieces[6 * ci + k]
            for xi in range(2):
                for zi in range(8):
                    place(piece, (xi * 8 + zi) * SHARD, zi, k, xi, ci, 0)
        for xi in range(2):
            piece = pieces[6 * ci + 4 + xi]
            for k in range(4):
                for zi in range(8):
                    place(piece, (k * 8 + zi) * SHARD, zi, k, xi, ci, HALF)
    raw_ref[...] = jnp.zeros_like(raw_ref)
    step = 512

    @pl.loop(0, hidden_ref.shape[1] // step)
    def _(i):
        depth = pl.ds(pl.multiple_of(i * step, step), step)
        raw_ref[...] += dot(hidden_ref[:, depth], codes_ref[depth, :], (1, 0))

    values_ref[...] = (raw_ref[...] * scale_ref[...]).astype(BF16)
    sums_ref[...] = jnp.sum(raw_ref[...] * dv_ref[...], axis=0, keepdims=True)


def raw_part(at, hidden, dv, scale, pieces):
    depth, width = hidden.shape[1], dv.shape[1]
    vmem = pl.BlockSpec(memory_space=pltpu.VMEM)
    return pl.pallas_call(
        raw_kernel,
        in_specs=[pl.BlockSpec(memory_space=pltpu.SMEM)] + [vmem] * (3 + len(pieces)),
        out_specs=[vmem] * 3,
        out_shape=[
            jax.ShapeDtypeStruct((depth, width), BF16),
            jax.ShapeDtypeStruct(dv.shape, BF16),
            jax.ShapeDtypeStruct((1, width), F32),
        ],
        scratch_shapes=[pltpu.VMEM(dv.shape, F32)],
        compiler_params=pltpu.CompilerParams(vmem_limit_bytes=VMEM_LIMIT),
        cost_estimate=pl.CostEstimate(flops=1_700_000_000, bytes_accessed=13_000_000, transcendentals=0),
        name="raw_part",
    )(at, hidden, dv, scale, *pieces)


QUARTER = 512


def hidden_kernel(at_ref, own_ref, other_ref, codes_ref, near0, near1, far0, far1, out_ref):
    c = at_ref[3]
    for other, quarters in enumerate(((near0, near1), (far0, far1))):
        for i, quarter in enumerate(quarters):
            rows = pl.ds(pl.multiple_of(((c ^ other) * 2 + i) * QUARTER, QUARTER), QUARTER)
            total = dot(own_ref[...], codes_ref[rows, :], (1, 1)) + dot(other_ref[...], quarter[...], (1, 1))
            out_ref[:, rows] = total.astype(BF16)


def hidden_part(at, own, other, codes, quarters):
    vmem = pl.BlockSpec(memory_space=pltpu.VMEM)
    return pl.pallas_call(
        hidden_kernel,
        in_specs=[pl.BlockSpec(memory_space=pltpu.SMEM)] + [vmem] * 7,
        out_specs=vmem,
        out_shape=jax.ShapeDtypeStruct((own.shape[0], 4 * QUARTER), BF16),
        compiler_params=pltpu.CompilerParams(vmem_limit_bytes=VMEM_LIMIT),
        cost_estimate=pl.CostEstimate(flops=1_700_000_000, bytes_accessed=8_000_000, transcendentals=0),
        name="hidden_part",
    )(at, own, other, codes, *quarters)


def pairs(move):
    out = []
    for i in range(128):
        z, y, x, c = move(i // 16, i // 4 % 4, i // 2 % 2, i % 2)
        out.append((i, ((z * 4 + y) * 2 + x) * 2 + c))
    return out


def z_swap(bit):
    return pairs(lambda z, y, x, c: (z ^ bit, y, x, c))


def y_shift(k):
    return pairs(lambda z, y, x, c: (z, (y + k) % 4, x, c))


def y_swap(bit):
    return pairs(lambda z, y, x, c: (z, y ^ bit, x, c))


X_SWAP = pairs(lambda z, y, x, c: (z, y, x ^ 1, c))
C_SWAP = pairs(lambda z, y, x, c: (z, y, x, c ^ 1))
BESIDE = [(2 * a + s, 2 * b + 1 - s) for a, b in X_SWAP for s in range(2)]


def send(x, perm):
    return lax.ppermute(x, "dp", perm)


def gather(shard):
    rows = shard
    for bit in (4, 2, 1):
        rows = jnp.concatenate([rows, send(rows, z_swap(bit))], axis=0)
    first, second = rows[:, :HALF], rows[:, HALF:]
    first_x = send(first, X_SWAP)
    second_y = [send(second, y_shift(k)) for k in (1, 2, 3)]
    first = jnp.concatenate([first, first_x], axis=0)
    second = jnp.concatenate([second] + second_y, axis=0)
    firsts = [first] + [send(first, y_shift(k)) for k in (1, 2, 3)]
    seconds = [second, send(second, X_SWAP)]
    mine = firsts + seconds
    return mine + [send(piece, C_SWAP) for piece in mine]


def shards(hidden, queries, keys, value_codes, value_scale, upstream, lengths):
    me, s = lax.axis_index("dp"), lax.axis_index("seq")
    at = jnp.stack([me // 16, me // 4 % 4, me // 2 % 2, me % 2]).astype(jnp.int32)
    scale = value_scale.reshape(1, -1)
    pieces = gather(value_codes)
    probs, dv, scaled = probs_part(lengths, queries, keys, upstream, scale)
    scaled_other = lax.ppermute(scaled, "seq", [(0, 1), (1, 0)])
    codes, values, sums = raw_part(at, hidden, dv, scale, pieces)
    base = 2048 * (1 - s) + 1024 * at[3]
    near0 = lax.ppermute(lax.dynamic_slice_in_dim(codes, base, QUARTER, 0), "seq", [(0, 1), (1, 0)])
    near1 = lax.ppermute(lax.dynamic_slice_in_dim(codes, base + QUARTER, QUARTER, 0), ("dp", "seq"), BESIDE)
    far0, far1 = send(near0, C_SWAP), send(near1, C_SWAP)
    for perm in (z_swap(4), z_swap(2), z_swap(1), y_swap(2), y_swap(1), X_SWAP, C_SWAP):
        sums = sums + send(sums, perm)
    grad_log_scale = (scale * sums).reshape(-1)
    grad_queries, grad_keys = grads_part(queries, keys, upstream, values, probs)
    own_codes = lax.dynamic_slice_in_dim(codes, 2048 * s, 2048, 0)
    grad_hidden = hidden_part(at, scaled, scaled_other, own_codes, (near0, near1, far0, far1))
    return grad_queries, grad_keys, grad_hidden, grad_log_scale


def solution(mesh):
    placed = (
        P("dp", None),
        P("dp", "seq"),
        P("dp", "seq"),
        P("dp", "seq"),
        P("seq"),
        P("dp", "seq"),
        P("dp", None),
    )
    return jax.shard_map(
        shards,
        mesh=mesh,
        in_specs=placed,
        out_specs=(P("dp", "seq"), P("dp", "seq"), P("dp", "seq"), P("seq")),
        check_vma=False,
    )
```

```python
import functools
import math

import jax
import jax.numpy as jnp
from jax import lax
from jax.experimental import pallas as pl
from jax.experimental.pallas import tpu as pltpu
from jax.sharding import PartitionSpec as P

COUNT = 384
HEAD = 128
GROUP = 4
BLOCK = 128
BLOCKS = COUNT // BLOCK
FACTOR = 1.0 / math.sqrt(HEAD)
LOG2E = math.log2(math.e)
BF16 = jnp.bfloat16
F32 = jnp.float32
VMEM_LIMIT = 20 * 1024 * 1024


def dot(a, b, dims):
    return lax.dot_general(a, b, ((dims[:1], dims[1:]), ((), ())), preferred_element_type=F32)

VMEM = pl.BlockSpec(memory_space=pltpu.VMEM)
SMEM = pl.BlockSpec(memory_space=pltpu.SMEM)
ANY = pl.BlockSpec(memory_space=pl.ANY)
TOKEN = jax.ShapeDtypeStruct((8, 128), F32)
WIDE = GROUP * HEAD


def call(kernel, name, out_shape, ins, after=(), through=(), **kw):
    specs, args = zip(*ins)
    n_in = len(args) + len(after)
    single = not isinstance(out_shape, (list, tuple))
    outs = [out_shape] if single else list(out_shape)
    kw.setdefault("out_specs", [VMEM] * len(outs))

    n_out = len(outs)
    if through:
        kw["input_output_aliases"] = {n_in + j: n_out + j for j in range(len(through))}
        outs += [jax.ShapeDtypeStruct(a.shape, a.dtype) for a in through]
        kw["out_specs"] = list(kw["out_specs"]) + [ANY] * len(through)
        single = False

    def run(*refs):
        first = n_in + len(through)
        kernel(*refs[: len(args)], *refs[first : first + n_out], *refs[first + n_out + len(through) :])

    got = pl.pallas_call(
        run,
        in_specs=list(specs) + [ANY] * (len(after) + len(through)),
        out_shape=outs,
        compiler_params=pltpu.CompilerParams(vmem_limit_bytes=VMEM_LIMIT),
        cost_estimate=pl.CostEstimate(flops=1000, bytes_accessed=1000, transcendentals=0),
        name=name,
        **kw,
    )(*args, *after, *through)
    return got[0] if single else got


def shape(*dims, dtype=BF16):
    return jax.ShapeDtypeStruct(dims, dtype)


def probs_kernel(lengths_ref, q_ref, k_ref, up_ref, p_ref, dv_ref, bias_ref, s_ref, dv_acc):
    rows = lax.broadcasted_iota(jnp.int32, (COUNT, COUNT), 0)
    cols = lax.broadcasted_iota(jnp.int32, (COUNT, COUNT), 1)
    start = jnp.zeros((COUNT, COUNT), jnp.int32)
    end = jnp.int32(0)
    for doc in range(3):
        end = end + lengths_ref[0, doc]
        start = jnp.where(rows >= end, end, start)
    bias_ref[...] = jnp.where((cols <= rows) & (cols >= start), 0.0, -1e30).astype(F32)
    dv_acc[...] = jnp.zeros_like(dv_acc)
    for i in range(BLOCKS):
        width = BLOCK * (i + 1)
        at = pl.ds(BLOCK * i, BLOCK)
        qs = jnp.concatenate([q_ref[at, pl.ds(HEAD * h, HEAD)] for h in range(GROUP)], axis=0)
        s_ref[:, :width] = dot(qs, k_ref[:width, :], (1, 1))
        for h in range(GROUP):
            scores = s_ref[pl.ds(BLOCK * h, BLOCK), :width] * (FACTOR * LOG2E) + bias_ref[at, :width]
            expo = jnp.exp2(scores - jnp.max(scores, axis=1, keepdims=True))
            probs = expo * (1.0 / jnp.sum(expo, axis=1, keepdims=True))
            p_ref[h, at, :width] = probs.astype(BF16)
        low = jnp.concatenate([p_ref[h, at, :width] for h in range(GROUP)], axis=0)
        ups = jnp.concatenate([up_ref[at, pl.ds(HEAD * h, HEAD)] for h in range(GROUP)], axis=0)
        dv_acc[:, :width] += dot(ups, low, (0, 0))
    dv_ref[...] = dv_acc[...].T


def probs_part(g, lengths, queries, keys, upstream, dv, after):
    wide = pl.BlockSpec((COUNT, WIDE), lambda i: (0, g))
    narrow = pl.BlockSpec((COUNT, HEAD), lambda i: (0, g))
    ins = [(SMEM, lengths), (wide, queries), (narrow, keys), (wide, upstream)]

    def kernel(*refs):
        probs_kernel(*refs[:4], *refs[len(refs) - 5 :])

    extra = {}
    if dv is not None:
        ins.append((ANY, dv))
        extra["input_output_aliases"] = {4: 1}
    return call(
        kernel, "probs_part", [shape(GROUP, COUNT, COUNT), shape(COUNT, 4 * HEAD, dtype=F32)], ins, after,
        out_specs=[VMEM, narrow], grid=(1,),
        scratch_shapes=[pltpu.VMEM((COUNT, COUNT), F32), pltpu.VMEM((GROUP * BLOCK, COUNT), F32), pltpu.VMEM((HEAD, COUNT), F32)], **extra,
    )


def grads_kernel(g, at_ref, q_ref, k_ref, up_ref, mine_ref, theirs_ref, p_ref, gq_ref, gk_ref, token_ref, dp_ref, ds_ref, dk_acc):
    token_ref[...] = jnp.zeros_like(token_ref)
    dk_acc[...] = jnp.zeros_like(dk_acc)
    col = pl.ds(HEAD * (g % 2), HEAD)
    all_values = jnp.where(at_ref[3] == g // 2, mine_ref[:, col], theirs_ref[:, col])
    for i in range(BLOCKS):
        width = BLOCK * (i + 1)
        at = pl.ds(BLOCK * i, BLOCK)
        ups = jnp.concatenate([up_ref[at, pl.ds(HEAD * h, HEAD)] for h in range(GROUP)], axis=0)
        dp_ref[:, :width] = dot(ups, all_values[:width], (1, 1))
        for h in range(GROUP):
            rows = pl.ds(BLOCK * h, BLOCK)
            dprobs = dp_ref[rows, :width]
            probs = p_ref[h, at, :width].astype(F32)
            delta = jnp.sum(probs * dprobs, axis=1, keepdims=True)
            ds_ref[rows, :width] = (probs * (dprobs - delta)).astype(BF16)
        dscores = ds_ref[:, :width]
        gq = dot(dscores, k_ref[:width, :], (1, 0)) * FACTOR
        for h in range(GROUP):
            gq_ref[at, pl.ds(HEAD * h, HEAD)] = gq[BLOCK * h : BLOCK * (h + 1)].astype(BF16)
        qs = jnp.concatenate([q_ref[at, pl.ds(HEAD * h, HEAD)] for h in range(GROUP)], axis=0)
        dk_acc[:, :width] += dot(qs, dscores, (0, 0))
    gk_ref[...] = (dk_acc[...] * FACTOR).T.astype(BF16)


def grads_part(g, at, queries, keys, upstream, mine, theirs, probs, held, after):
    wide = pl.BlockSpec((COUNT, WIDE), lambda i: (0, g))
    narrow = pl.BlockSpec((COUNT, HEAD), lambda i: (0, g))
    ins = [(SMEM, at), (wide, queries), (narrow, keys), (wide, upstream), (VMEM, mine), (VMEM, theirs), (VMEM, probs)]

    def kernel(*refs):
        grads_kernel(g, *refs[:7], *refs[len(refs) - 6 :])

    extra = {}
    if held is not None:
        ins += [(ANY, held[0]), (ANY, held[1])]
        extra["input_output_aliases"] = {7: 0, 8: 1}
    return call(
        kernel, "grads_part", [shape(*queries.shape), shape(*keys.shape), TOKEN], ins, after,
        out_specs=[wide, narrow, VMEM], grid=(1,),
        scratch_shapes=[pltpu.VMEM((GROUP * BLOCK, COUNT), F32), pltpu.VMEM((GROUP * BLOCK, COUNT), BF16), pltpu.VMEM((HEAD, COUNT), F32)], **extra,
    )


Z_ORDER = (0, 4, 2, 6, 1, 5, 3, 7)
SHARD = 32
CHIP = 2 * SHARD
HALF = 256
DEPTH = 4096


def own_columns(at_ref):
    return pl.ds(pl.multiple_of(at_ref[3] * HALF, HALF), HALF)


def first_join(at_ref, own_ref, other_ref, out_ref):
    c, cols = at_ref[3], own_columns(at_ref)
    out_ref[pl.ds(pl.multiple_of(c * SHARD, SHARD), SHARD), :] = own_ref[:, cols]
    out_ref[pl.ds(pl.multiple_of((1 - c) * SHARD, SHARD), SHARD), :] = other_ref[:, cols]


def copy_kernel(in_ref, out_ref, sem):
    copy = pltpu.make_async_copy(in_ref, out_ref, sem)
    copy.start()
    copy.wait()


def join_kernel(own_ref, other_ref, out_ref):
    n = own_ref.shape[0]
    out_ref[:n, :] = own_ref[...]
    out_ref[n:, :] = other_ref[...]


def join_split_kernel(own_ref, other_ref, first_ref, second_ref):
    n = own_ref.shape[0]
    for j, out_ref in enumerate((first_ref, second_ref)):
        out_ref[:n, :] = own_ref[:, HEAD * j : HEAD * (j + 1)]
        out_ref[n:, :] = other_ref[:, HEAD * j : HEAD * (j + 1)]


def two_joins_kernel(a0, a1, b0, b1, b2, b3, first_ref, second_ref):
    n = a0.shape[0]
    for j, part in enumerate((a0, a1)):
        first_ref[n * j : n * (j + 1), :] = part[...]
    for j, part in enumerate((b0, b1, b2, b3)):
        second_ref[n * j : n * (j + 1), :] = part[...]


def put_in_order(at_ref, pieces, codes_ref):
    z, y, x = at_ref[0], at_ref[1], at_ref[2]

    def place(piece, row, zi, k, xi, col):
        to = ((z ^ Z_ORDER[zi]) * 4 + ((y + 4 - k) & 3)) * 2 + (x ^ xi)
        rows = pl.ds(pl.multiple_of(to * CHIP, CHIP), CHIP)
        codes_ref[rows, pl.ds(col, HEAD)] = piece[pl.ds(row, CHIP), :]

    for k in range(4):
        for xi in range(2):
            for zi in range(8):
                place(pieces[k], (xi * 8 + zi) * CHIP, zi, k, xi, 0)
                place(pieces[4 + xi], (k * 8 + zi) * CHIP, zi, k, xi, HEAD)


STEP = 512


def raw_kernel(at_ref, own_ref, other_ref, dv_own, dv_other, scale_ref, *refs):
    pieces, (mine_ref, theirs_ref, sums_ref, codes_ref, raw_own, raw_other) = refs[:6], refs[6:]
    i = pl.program_id(0)

    @pl.when(i == 0)
    def _():
        put_in_order(at_ref, pieces, codes_ref)
        raw_own[...] = jnp.zeros_like(raw_own)
        raw_other[...] = jnp.zeros_like(raw_other)

    codes = codes_ref[pl.ds(pl.multiple_of(i * STEP, STEP), STEP), :]
    raw_own[...] += dot(own_ref[...], codes, (1, 0))
    raw_other[...] += dot(other_ref[...], codes, (1, 0))

    @pl.when(i == pl.num_programs(0) - 1)
    def _():
        cols = own_columns(at_ref)
        scale = scale_ref[:, cols]
        mine_ref[...] = (raw_own[...] * scale).astype(BF16)
        theirs_ref[...] = (raw_other[...] * scale).astype(BF16)
        products = raw_own[...] * dv_own[:, cols] + raw_other[...] * dv_other[:, cols]
        sums_ref[...] = jnp.sum(products, axis=0, keepdims=True)


def raw_part(at, hidden, hidden_other, dv, dv_other, scale, pieces):
    block = pl.BlockSpec((COUNT, STEP), lambda i: (0, i))
    return call(
        raw_kernel, "raw_part", [shape(COUNT, HALF), shape(COUNT, HALF), shape(1, HALF, dtype=F32)],
        [(SMEM, at), (block, hidden), (block, hidden_other), (VMEM, dv), (VMEM, dv_other), (VMEM, scale)] + [(VMEM, p) for p in pieces],
        grid=(DEPTH // STEP,),
        scratch_shapes=[pltpu.VMEM((DEPTH, HALF), BF16), pltpu.VMEM((COUNT, HALF), F32), pltpu.VMEM((COUNT, HALF), F32)],
    )


def split_kernel(at_ref, dv_ref, scale_ref, *refs):
    pieces, (kept_ref, near_ref, beside_ref, scaled_ref, codes_ref) = refs[:6], refs[6:]
    put_in_order(at_ref, pieces, codes_ref)
    s, half = at_ref[4], DEPTH // 2
    kept_ref[...] = codes_ref[pl.ds(pl.multiple_of(s * half, half), half), :]
    base = (1 - s) * half
    near_ref[...] = codes_ref[pl.ds(pl.multiple_of(base, half), half // 2), :]
    beside_ref[...] = codes_ref[pl.ds(pl.multiple_of(base + half // 2, half // 2), half // 2), :]
    scaled_ref[...] = (dv_ref[...] * scale_ref[...]).astype(BF16)


def split_part(at, dv, scale, pieces, after):
    return call(
        split_kernel, "split_part", [shape(DEPTH // 2, HALF), shape(DEPTH // 4, HALF), shape(DEPTH // 4, HALF), shape(COUNT, 2 * HALF)],
        [(SMEM, at), (VMEM, dv), (VMEM, scale)] + [(VMEM, p) for p in pieces], after,
        scratch_shapes=[pltpu.VMEM((DEPTH, HALF), BF16)],
    )


def hidden_kernel(at_ref, own_ref, other_ref, kept_ref, kept_far, near_ref, near_far, out_ref, token_ref):
    mine = own_columns(at_ref)
    rest = pl.ds(pl.multiple_of((1 - at_ref[3]) * HALF, HALF), HALF)
    total = dot(own_ref[:, mine], kept_ref[...], (1, 1)) + dot(own_ref[:, rest], kept_far[...], (1, 1))
    total += dot(other_ref[:, mine], near_ref[...], (1, 1)) + dot(other_ref[:, rest], near_far[...], (1, 1))
    out_ref[...] = total.astype(BF16)
    token_ref[...] = jnp.zeros_like(token_ref)


def hidden_part(at, own, other, kept, kept_far, near, near_far, after):
    block = pl.BlockSpec((STEP, HALF), lambda i: (i, 0))
    return call(
        hidden_kernel, "hidden_part", [shape(COUNT, DEPTH // 2), TOKEN],
        [(SMEM, at), (VMEM, own), (VMEM, other), (block, kept), (block, kept_far), (block, near), (block, near_far)], after,
        grid=(DEPTH // 2 // STEP,),
        out_specs=[pl.BlockSpec((COUNT, STEP), lambda i: (0, i)), VMEM],
    )


def add_kernel(a_ref, b_ref, out_ref):
    out_ref[...] = a_ref[...] + b_ref[...]


def last_kernel(at_ref, own_ref, other_ref, scale_ref, out_ref):
    c = at_ref[3]
    low = jnp.where(c == 0, own_ref[...], other_ref[...])
    high = jnp.where(c == 0, other_ref[...], own_ref[...])
    out_ref[:, :HALF] = low * scale_ref[:, :HALF]
    out_ref[:, HALF:] = high * scale_ref[:, HALF:]


def pairs(move):
    out = []
    for i in range(128):
        z, y, x, c = move(i // 16, i // 4 % 4, i // 2 % 2, i % 2)
        out.append((i, ((z * 4 + y) * 2 + x) * 2 + c))
    return out


def z_swap(bit):
    return pairs(lambda z, y, x, c: (z ^ bit, y, x, c))


def y_shift(k):
    return pairs(lambda z, y, x, c: (z, (y + k) % 4, x, c))


def y_swap(bit):
    return pairs(lambda z, y, x, c: (z, y ^ bit, x, c))


X_SWAP = pairs(lambda z, y, x, c: (z, y, x ^ 1, c))
C_SWAP = pairs(lambda z, y, x, c: (z, y, x, c ^ 1))
SEQ_SWAP = [(0, 1), (1, 0)]
BESIDE = [(2 * a + s, 2 * b + 1 - s) for a, b in X_SWAP for s in range(2)]


def send(x, perm):
    return lax.ppermute(x, "dp", perm)


def shards(hidden, queries, keys, value_codes, value_scale, upstream, lengths):
    me, s = lax.axis_index("dp"), lax.axis_index("seq")
    at = jnp.stack([me // 16, me // 4 % 4, me // 2 % 2, me % 2, s]).astype(jnp.int32)
    scale = value_scale.reshape(1, -1)

    rows = call(first_join, "join", shape(CHIP, HALF), [(SMEM, at), (VMEM, value_codes), (VMEM, send(value_codes, C_SWAP))])
    hidden = call(
        copy_kernel, "copy", shape(*hidden.shape), [(ANY, hidden)], (rows,),
        out_specs=[ANY], scratch_shapes=[pltpu.SemaphoreType.DMA],
    )
    probs, dv = [], None
    for bit, heads in ((4, (0,)), (2, (1,)), (1, (2, 3))):
        got = send(rows, z_swap(bit))
        for g in heads:
            p, dv = probs_part(g, lengths, queries, keys, upstream, dv, (rows,))
            probs.append(p)
        n = rows.shape[0]
        ins = [(VMEM, rows), (VMEM, got)]
        if bit == 4:
            rows, hidden = call(join_kernel, "join", shape(2 * n, HALF), ins, (p,), (hidden,))
            hidden_other = send(hidden, C_SWAP)
        elif bit == 2:
            rows = call(join_kernel, "join", shape(2 * n, HALF), ins, (p,))
        else:
            first, second, dv = call(join_split_kernel, "join", [shape(2 * n, HEAD)] * 2, ins, (p,), (dv,))
    dv_other = send(dv, C_SWAP)
    first_x = send(first, X_SWAP)
    second_y = [send(second, y_shift(k)) for k in (1, 2, 3)]
    n = first.shape[0]
    first, second = call(
        two_joins_kernel, "join", [shape(2 * n, HEAD), shape(4 * n, HEAD)],
        [(VMEM, a) for a in [first, first_x, second] + second_y], (hidden_other, dv_other),
    )
    pieces = [first] + [send(first, y_shift(k)) for k in (1, 2, 3)] + [second, send(second, X_SWAP)]

    mine, theirs, sums = raw_part(at, hidden, hidden_other, dv, dv_other, scale, pieces)

    got = send(sums, X_SWAP)
    values_far = send(theirs, C_SWAP)
    kept, near, beside, scaled = split_part(at, dv, scale, pieces, (values_far,))
    sums, kept, near, beside, scaled = call(
        add_kernel, "add", shape(1, HALF, dtype=F32), [(VMEM, sums), (VMEM, got)], (), (kept, near, beside, scaled)
    )
    kept_far = send(kept, C_SWAP)
    scaled_other = lax.ppermute(scaled, "seq", SEQ_SWAP)
    near = lax.ppermute(near, "seq", SEQ_SWAP)
    beside = lax.ppermute(beside, ("dp", "seq"), BESIDE)
    held = None
    for g, perm in enumerate((y_swap(1), y_swap(2), z_swap(1), z_swap(2))):
        got = send(sums, perm)
        *held, token = grads_part(g, at, queries, keys, upstream, mine, values_far, probs[g], held, (sums,))
        after = (token,)
        if g == 3:
            near = call(join_kernel, "join", shape(DEPTH // 2, HALF), [(VMEM, near), (VMEM, beside)], (sums,))
            near_far = send(near, C_SWAP)
            after += (near,)
        sums = call(add_kernel, "add", shape(1, HALF, dtype=F32), [(VMEM, sums), (VMEM, got)], after)
    got = send(sums, z_swap(4))
    grad_hidden, token = hidden_part(at, scaled, scaled_other, kept, kept_far, near, near_far, (sums,))
    sums = call(add_kernel, "add", shape(1, HALF, dtype=F32), [(VMEM, sums), (VMEM, got)], (token,))
    last = call(
        last_kernel, "last", shape(1, 2 * HALF, dtype=F32),
        [(SMEM, at), (VMEM, sums), (VMEM, send(sums, C_SWAP)), (VMEM, scale)],
    )
    return held[0], held[1], grad_hidden, last.reshape(-1)


def solution(mesh):
    placed = (
        P("dp", None),
        P("dp", "seq"),
        P("dp", "seq"),
        P("dp", "seq"),
        P("seq"),
        P("dp", "seq"),
        P("dp", None),
    )
    return jax.shard_map(
        shards,
        mesh=mesh,
        in_specs=placed,
        out_specs=(P("dp", "seq"), P("dp", "seq"), P("dp", "seq"), P("seq")),
        check_vma=False,
    )
```

```python
import functools
import math

import jax
import jax.numpy as jnp
from jax import lax
from jax.experimental import pallas as pl
from jax.experimental.pallas import tpu as pltpu
from jax.sharding import PartitionSpec as P

COUNT = 384
HEAD = 128
GROUP = 4
BLOCK = 128
BLOCKS = COUNT // BLOCK
FACTOR = 1.0 / math.sqrt(HEAD)
LOG2E = math.log2(math.e)
BF16 = jnp.bfloat16
F32 = jnp.float32
VMEM_LIMIT = 20 * 1024 * 1024


def dot(a, b, dims):
    return lax.dot_general(a, b, ((dims[:1], dims[1:]), ((), ())), preferred_element_type=F32)

VMEM = pl.BlockSpec(memory_space=pltpu.VMEM)
SMEM = pl.BlockSpec(memory_space=pltpu.SMEM)
ANY = pl.BlockSpec(memory_space=pl.ANY)
TOKEN = jax.ShapeDtypeStruct((8, 128), F32)
WIDE = GROUP * HEAD


def call(kernel, name, out_shape, ins, after=(), through=(), **kw):
    specs, args = zip(*ins)
    n_in = len(args) + len(after)
    single = not isinstance(out_shape, (list, tuple))
    outs = [out_shape] if single else list(out_shape)
    kw.setdefault("out_specs", [VMEM] * len(outs))

    n_out = len(outs)
    if through:
        kw["input_output_aliases"] = {n_in + j: n_out + j for j in range(len(through))}
        outs += [jax.ShapeDtypeStruct(a.shape, a.dtype) for a in through]
        kw["out_specs"] = list(kw["out_specs"]) + [ANY] * len(through)
        single = False

    def run(*refs):
        first = n_in + len(through)
        kernel(*refs[: len(args)], *refs[first : first + n_out], *refs[first + n_out + len(through) :])

    got = pl.pallas_call(
        run,
        in_specs=list(specs) + [ANY] * (len(after) + len(through)),
        out_shape=outs,
        compiler_params=pltpu.CompilerParams(vmem_limit_bytes=VMEM_LIMIT),
        cost_estimate=pl.CostEstimate(flops=1000, bytes_accessed=1000, transcendentals=0),
        name=name,
        **kw,
    )(*args, *after, *through)
    return got[0] if single else got


def shape(*dims, dtype=BF16):
    return jax.ShapeDtypeStruct(dims, dtype)


def probs_kernel(lengths_ref, q_ref, k_ref, up_ref, p_ref, dv_ref, bias_ref, s_ref, dv_acc):
    rows = lax.broadcasted_iota(jnp.int32, (COUNT, COUNT), 0)
    cols = lax.broadcasted_iota(jnp.int32, (COUNT, COUNT), 1)
    start = jnp.zeros((COUNT, COUNT), jnp.int32)
    end = jnp.int32(0)
    for doc in range(3):
        end = end + lengths_ref[0, doc]
        start = jnp.where(rows >= end, end, start)
    bias_ref[...] = jnp.where((cols <= rows) & (cols >= start), 0.0, -1e30).astype(F32)
    dv_acc[...] = jnp.zeros_like(dv_acc)
    for i in range(BLOCKS):
        width = BLOCK * (i + 1)
        at = pl.ds(BLOCK * i, BLOCK)
        qs = jnp.concatenate([q_ref[at, pl.ds(HEAD * h, HEAD)] for h in range(GROUP)], axis=0)
        s_ref[:, :width] = dot(qs, k_ref[:width, :], (1, 1))
        for h in range(GROUP):
            scores = s_ref[pl.ds(BLOCK * h, BLOCK), :width] * (FACTOR * LOG2E) + bias_ref[at, :width]
            expo = jnp.exp2(scores - jnp.max(scores, axis=1, keepdims=True))
            probs = expo * (1.0 / jnp.sum(expo, axis=1, keepdims=True))
            p_ref[h, at, :width] = probs.astype(BF16)
        low = jnp.concatenate([p_ref[h, at, :width] for h in range(GROUP)], axis=0)
        ups = jnp.concatenate([up_ref[at, pl.ds(HEAD * h, HEAD)] for h in range(GROUP)], axis=0)
        dv_acc[:, :width] += dot(ups, low, (0, 0))
    dv_ref[...] = dv_acc[...].T


def probs_part(g, lengths, queries, keys, upstream, dv, after):
    wide = pl.BlockSpec((COUNT, WIDE), lambda i: (0, g))
    narrow = pl.BlockSpec((COUNT, HEAD), lambda i: (0, g))
    ins = [(SMEM, lengths), (wide, queries), (narrow, keys), (wide, upstream)]

    def kernel(*refs):
        probs_kernel(*refs[:4], *refs[len(refs) - 5 :])

    extra = {}
    if dv is not None:
        ins.append((ANY, dv))
        extra["input_output_aliases"] = {4: 1}
    return call(
        kernel, "probs_part", [shape(GROUP, COUNT, COUNT), shape(COUNT, 4 * HEAD, dtype=F32)], ins, after,
        out_specs=[VMEM, narrow], grid=(1,),
        scratch_shapes=[pltpu.VMEM((COUNT, COUNT), F32), pltpu.VMEM((GROUP * BLOCK, COUNT), F32), pltpu.VMEM((HEAD, COUNT), F32)], **extra,
    )


def grads_kernel(g, at_ref, q_ref, k_ref, up_ref, mine_ref, theirs_ref, p_ref, gq_ref, gk_ref, token_ref, dp_ref, ds_ref, dk_acc):
    token_ref[...] = jnp.zeros_like(token_ref)
    dk_acc[...] = jnp.zeros_like(dk_acc)
    col = pl.ds(HEAD * (g % 2), HEAD)
    all_values = jnp.where(at_ref[3] == g // 2, mine_ref[:, col], theirs_ref[:, col])
    for i in range(BLOCKS):
        width = BLOCK * (i + 1)
        at = pl.ds(BLOCK * i, BLOCK)
        ups = jnp.concatenate([up_ref[at, pl.ds(HEAD * h, HEAD)] for h in range(GROUP)], axis=0)
        dp_ref[:, :width] = dot(ups, all_values[:width], (1, 1))
        for h in range(GROUP):
            rows = pl.ds(BLOCK * h, BLOCK)
            dprobs = dp_ref[rows, :width]
            probs = p_ref[h, at, :width].astype(F32)
            delta = jnp.sum(probs * dprobs, axis=1, keepdims=True)
            ds_ref[rows, :width] = (probs * (dprobs - delta)).astype(BF16)
        dscores = ds_ref[:, :width]
        gq = dot(dscores, k_ref[:width, :], (1, 0)) * FACTOR
        for h in range(GROUP):
            gq_ref[at, pl.ds(HEAD * h, HEAD)] = gq[BLOCK * h : BLOCK * (h + 1)].astype(BF16)
        qs = jnp.concatenate([q_ref[at, pl.ds(HEAD * h, HEAD)] for h in range(GROUP)], axis=0)
        dk_acc[:, :width] += dot(qs, dscores, (0, 0))
    gk_ref[...] = (dk_acc[...] * FACTOR).T.astype(BF16)


def grads_part(g, at, queries, keys, upstream, mine, theirs, probs, held, after):
    wide = pl.BlockSpec((COUNT, WIDE), lambda i: (0, g))
    narrow = pl.BlockSpec((COUNT, HEAD), lambda i: (0, g))
    ins = [(SMEM, at), (wide, queries), (narrow, keys), (wide, upstream), (VMEM, mine), (VMEM, theirs), (VMEM, probs)]

    def kernel(*refs):
        grads_kernel(g, *refs[:7], *refs[len(refs) - 6 :])

    extra = {}
    if held is not None:
        ins += [(ANY, held[0]), (ANY, held[1])]
        extra["input_output_aliases"] = {7: 0, 8: 1}
    return call(
        kernel, "grads_part", [shape(*queries.shape), shape(*keys.shape), TOKEN], ins, after,
        out_specs=[wide, narrow, VMEM], grid=(1,),
        scratch_shapes=[pltpu.VMEM((GROUP * BLOCK, COUNT), F32), pltpu.VMEM((GROUP * BLOCK, COUNT), BF16), pltpu.VMEM((HEAD, COUNT), F32)], **extra,
    )


Z_ORDER = (0, 4, 2, 6, 1, 5, 3, 7)
SHARD = 32
CHIP = 2 * SHARD
HALF = 256
DEPTH = 4096


def own_columns(at_ref):
    return pl.ds(pl.multiple_of(at_ref[3] * HALF, HALF), HALF)


def first_join(at_ref, own_ref, other_ref, out_ref):
    c, cols = at_ref[3], own_columns(at_ref)
    out_ref[pl.ds(pl.multiple_of(c * SHARD, SHARD), SHARD), :] = own_ref[:, cols]
    out_ref[pl.ds(pl.multiple_of((1 - c) * SHARD, SHARD), SHARD), :] = other_ref[:, cols]


def copy_kernel(in_ref, out_ref, sem):
    copy = pltpu.make_async_copy(in_ref, out_ref, sem)
    copy.start()
    copy.wait()


def join_kernel(own_ref, other_ref, out_ref):
    n = own_ref.shape[0]
    out_ref[:n, :] = own_ref[...]
    out_ref[n:, :] = other_ref[...]


def join_split_kernel(own_ref, other_ref, first_ref, second_ref):
    n = own_ref.shape[0]
    for j, out_ref in enumerate((first_ref, second_ref)):
        out_ref[:n, :] = own_ref[:, HEAD * j : HEAD * (j + 1)]
        out_ref[n:, :] = other_ref[:, HEAD * j : HEAD * (j + 1)]


def two_joins_kernel(a0, a1, b0, b1, b2, b3, first_ref, second_ref):
    n = a0.shape[0]
    for j, part in enumerate((a0, a1)):
        first_ref[n * j : n * (j + 1), :] = part[...]
    for j, part in enumerate((b0, b1, b2, b3)):
        second_ref[n * j : n * (j + 1), :] = part[...]


def put_in_order(at_ref, pieces, codes_ref):
    z, y, x = at_ref[0], at_ref[1], at_ref[2]

    def place(piece, row, zi, k, xi, col):
        to = ((z ^ Z_ORDER[zi]) * 4 + ((y + 4 - k) & 3)) * 2 + (x ^ xi)
        rows = pl.ds(pl.multiple_of(to * CHIP, CHIP), CHIP)
        codes_ref[rows, pl.ds(col, HEAD)] = piece[pl.ds(row, CHIP), :]

    for k in range(4):
        for xi in range(2):
            for zi in range(8):
                place(pieces[k], (xi * 8 + zi) * CHIP, zi, k, xi, 0)
                place(pieces[4 + xi], (k * 8 + zi) * CHIP, zi, k, xi, HEAD)


def raw_kernel(at_ref, own_ref, other_ref, dv_own, dv_other, scale_ref, *refs):
    pieces, (mine_ref, theirs_ref, sums_ref, codes_ref) = refs[:6], refs[6:]
    put_in_order(at_ref, pieces, codes_ref)
    cols = own_columns(at_ref)
    scale = scale_ref[:, cols]
    sums = jnp.zeros((1, HALF), F32)
    for hidden_ref, dv_ref, values_ref in ((other_ref, dv_other, theirs_ref), (own_ref, dv_own, mine_ref)):
        raw = dot(hidden_ref[...], codes_ref[...], (1, 0))
        values_ref[...] = (raw * scale).astype(BF16)
        sums += jnp.sum(raw * dv_ref[:, cols], axis=0, keepdims=True)
    sums_ref[...] = sums


def raw_part(at, hidden, hidden_other, dv, dv_other, scale, pieces):
    return call(
        raw_kernel, "raw_part", [shape(COUNT, HALF), shape(COUNT, HALF), shape(1, HALF, dtype=F32)],
        [(SMEM, at)] + [(VMEM, a) for a in [hidden, hidden_other, dv, dv_other, scale] + pieces],
        scratch_shapes=[pltpu.VMEM((DEPTH, HALF), BF16)],
    )


NEAR = 640


def split_kernel(at_ref, dv_ref, scale_ref, *refs):
    pieces, (kept_ref, near_ref, beside_ref, scaled_ref, codes_ref) = refs[:6], refs[6:]
    put_in_order(at_ref, pieces, codes_ref)
    s, half = at_ref[4], DEPTH // 2
    kept_ref[...] = codes_ref[pl.ds(pl.multiple_of(s * half, half), half), :]
    base = (1 - s) * half
    near_ref[...] = codes_ref[pl.ds(pl.multiple_of(base, half), NEAR), :]
    beside_ref[...] = codes_ref[pl.ds(pl.multiple_of(base + NEAR, 128), half - NEAR), :]
    scaled_ref[...] = (dv_ref[...] * scale_ref[...]).astype(BF16)


def split_part(at, dv, scale, pieces, after):
    return call(
        split_kernel, "split_part", [shape(DEPTH // 2, HALF), shape(NEAR, HALF), shape(DEPTH // 2 - NEAR, HALF), shape(COUNT, 2 * HALF)],
        [(SMEM, at), (VMEM, dv), (VMEM, scale)] + [(VMEM, p) for p in pieces], after,
        scratch_shapes=[pltpu.VMEM((DEPTH, HALF), BF16)],
    )


BATCH = 512


def hidden_kernel(at_ref, own_ref, other_ref, kept_ref, kept_far, near_ref, near_far, out_ref, token_ref):
    mine = own_columns(at_ref)
    rest = pl.ds(pl.multiple_of((1 - at_ref[3]) * HALF, HALF), HALF)
    terms = ((own_ref, mine, kept_ref), (own_ref, rest, kept_far), (other_ref, mine, near_ref), (other_ref, rest, near_far))
    for i in range(0, DEPTH // 2, BATCH):
        rows = pl.ds(i, BATCH)
        out_ref[:, rows] = sum(dot(a[:, cols], b[rows, :], (1, 1)) for a, cols, b in terms).astype(BF16)
    token_ref[...] = jnp.zeros_like(token_ref)


def hidden_part(at, *arrays, after):
    return call(
        hidden_kernel, "hidden_part", [shape(COUNT, DEPTH // 2), TOKEN],
        [(SMEM, at)] + [(VMEM, a) for a in arrays], after,
    )


def add_kernel(a_ref, b_ref, out_ref):
    out_ref[...] = a_ref[...] + b_ref[...]


def last_kernel(at_ref, own_ref, other_ref, scale_ref, out_ref):
    c = at_ref[3]
    low = jnp.where(c == 0, own_ref[...], other_ref[...])
    high = jnp.where(c == 0, other_ref[...], own_ref[...])
    out_ref[:, :HALF] = low * scale_ref[:, :HALF]
    out_ref[:, HALF:] = high * scale_ref[:, HALF:]


def pairs(move):
    out = []
    for i in range(128):
        z, y, x, c = move(i // 16, i // 4 % 4, i // 2 % 2, i % 2)
        out.append((i, ((z * 4 + y) * 2 + x) * 2 + c))
    return out


def z_swap(bit):
    return pairs(lambda z, y, x, c: (z ^ bit, y, x, c))


def y_shift(k):
    return pairs(lambda z, y, x, c: (z, (y + k) % 4, x, c))


def y_swap(bit):
    return pairs(lambda z, y, x, c: (z, y ^ bit, x, c))


X_SWAP = pairs(lambda z, y, x, c: (z, y, x ^ 1, c))
C_SWAP = pairs(lambda z, y, x, c: (z, y, x, c ^ 1))
SEQ_SWAP = [(0, 1), (1, 0)]
BESIDE = [(2 * a + s, 2 * b + 1 - s) for a, b in X_SWAP for s in range(2)]


def send(x, perm):
    return lax.ppermute(x, "dp", perm)


def shards(hidden, queries, keys, value_codes, value_scale, upstream, lengths):
    me, s = lax.axis_index("dp"), lax.axis_index("seq")
    at = jnp.stack([me // 16, me // 4 % 4, me // 2 % 2, me % 2, s]).astype(jnp.int32)
    scale = value_scale.reshape(1, -1)

    rows = call(first_join, "join", shape(CHIP, HALF), [(SMEM, at), (VMEM, value_codes), (VMEM, send(value_codes, C_SWAP))])
    probs, dv = [], None
    for g, bit in enumerate((4, 2, 1)):
        got = send(rows, z_swap(bit))
        p, dv = probs_part(g, lengths, queries, keys, upstream, dv, (rows,))
        probs.append(p)
        n = rows.shape[0]
        ins = [(VMEM, rows), (VMEM, got)]
        if bit > 1:
            rows = call(join_kernel, "join", shape(2 * n, HALF), ins, (p,))
        else:
            hidden = call(
                copy_kernel, "copy", shape(*hidden.shape), [(ANY, hidden)], (rows,),
                out_specs=[ANY], scratch_shapes=[pltpu.SemaphoreType.DMA],
            )
            first, second, hidden = call(join_split_kernel, "join", [shape(2 * n, HEAD)] * 2, ins, (p,), (hidden,))
    first_x = send(first, X_SWAP)
    second_y = [send(second, y_shift(k)) for k in (1, 2, 3)]
    hidden_other = send(hidden, C_SWAP)
    p, dv = probs_part(3, lengths, queries, keys, upstream, dv, (first,))
    probs.append(p)
    n = first.shape[0]
    first, second, dv = call(
        two_joins_kernel, "join", [shape(2 * n, HEAD), shape(4 * n, HEAD)],
        [(VMEM, a) for a in [first, first_x, second] + second_y], (hidden_other,), (dv,),
    )
    pieces = [first] + [send(first, y_shift(k)) for k in (1, 2, 3)] + [second, send(second, X_SWAP)]
    mine, theirs, sums = raw_part(at, hidden, hidden_other, dv, send(dv, C_SWAP), scale, pieces)

    got = send(sums, X_SWAP)
    values_far = send(theirs, C_SWAP)
    kept, near, beside, scaled = split_part(at, dv, scale, pieces, (values_far,))
    sums, kept, near, beside, scaled = call(
        add_kernel, "add", shape(1, HALF, dtype=F32), [(VMEM, sums), (VMEM, got)], (), (kept, near, beside, scaled)
    )
    kept_far = send(kept, C_SWAP)
    scaled_other = lax.ppermute(scaled, "seq", SEQ_SWAP)
    near = lax.ppermute(near, "seq", SEQ_SWAP)
    beside = lax.ppermute(beside, ("dp", "seq"), BESIDE)
    held = None
    for g, perm in enumerate((y_swap(1), y_swap(2), z_swap(1), z_swap(2))):
        got = send(sums, perm)
        *held, token = grads_part(g, at, queries, keys, upstream, mine, values_far, probs[g], held, (sums, scaled_other) if g == 2 else (sums,))
        after = (token,)
        if g == 3:
            near = call(join_kernel, "join", shape(DEPTH // 2, HALF), [(VMEM, near), (VMEM, beside)], (sums,))
            near_far = send(near, C_SWAP)
            after += (near,)
        sums = call(add_kernel, "add", shape(1, HALF, dtype=F32), [(VMEM, sums), (VMEM, got)], after)
    got = send(sums, z_swap(4))
    grad_hidden, token = hidden_part(at, scaled, scaled_other, kept, kept_far, near, near_far, after=(sums,))
    sums = call(add_kernel, "add", shape(1, HALF, dtype=F32), [(VMEM, sums), (VMEM, got)], (token,))
    last = call(
        last_kernel, "last", shape(1, 2 * HALF, dtype=F32),
        [(SMEM, at), (VMEM, sums), (VMEM, send(sums, C_SWAP)), (VMEM, scale)],
    )
    return held[0], held[1], grad_hidden, last.reshape(-1)


def solution(mesh):
    placed = (
        P("dp", None),
        P("dp", "seq"),
        P("dp", "seq"),
        P("dp", "seq"),
        P("seq"),
        P("dp", "seq"),
        P("dp", None),
    )
    return jax.shard_map(
        shards,
        mesh=mesh,
        in_specs=placed,
        out_specs=(P("dp", "seq"), P("dp", "seq"), P("dp", "seq"), P("seq")),
        check_vma=False,
    )
```

```python
import functools
import math

import jax
import jax.numpy as jnp
from jax import lax
from jax.experimental import pallas as pl
from jax.experimental.pallas import tpu as pltpu
from jax.sharding import PartitionSpec as P

COUNT = 384
HEAD = 128
GROUP = 4
BLOCK = 128
BLOCKS = COUNT // BLOCK
FACTOR = 1.0 / math.sqrt(HEAD)
LOG2E = math.log2(math.e)
BF16 = jnp.bfloat16
F32 = jnp.float32
VMEM_LIMIT = 20 * 1024 * 1024


def dot(a, b, dims):
    return lax.dot_general(a, b, ((dims[:1], dims[1:]), ((), ())), preferred_element_type=F32)

VMEM = pl.BlockSpec(memory_space=pltpu.VMEM)
SMEM = pl.BlockSpec(memory_space=pltpu.SMEM)
ANY = pl.BlockSpec(memory_space=pl.ANY)
HBM = pl.BlockSpec(memory_space=pltpu.HBM)
TOKEN = jax.ShapeDtypeStruct((8, 128), F32)
WIDE = GROUP * HEAD


def call(kernel, name, out_shape, ins, after=(), through=(), **kw):
    specs, args = zip(*ins)
    args = tuple(pltpu.with_memory_space_constraint(a, pltpu.HBM) if spec is HBM else a for spec, a in ins)
    n_in = len(args) + len(after)
    single = not isinstance(out_shape, (list, tuple))
    outs = [out_shape] if single else list(out_shape)
    kw.setdefault("out_specs", [VMEM] * len(outs))

    n_out = len(outs)
    if through:
        kw["input_output_aliases"] = {n_in + j: n_out + j for j in range(len(through))}
        outs += [jax.ShapeDtypeStruct(a.shape, a.dtype) for a in through]
        kw["out_specs"] = list(kw["out_specs"]) + [ANY] * len(through)
        single = False

    def run(*refs):
        first = n_in + len(through)
        kernel(*refs[: len(args)], *refs[first : first + n_out], *refs[first + n_out + len(through) :])

    got = pl.pallas_call(
        run,
        in_specs=list(specs) + [ANY] * (len(after) + len(through)),
        out_shape=outs,
        compiler_params=pltpu.CompilerParams(vmem_limit_bytes=VMEM_LIMIT),
        cost_estimate=pl.CostEstimate(flops=1000, bytes_accessed=1000, transcendentals=0),
        name=name,
        **kw,
    )(*args, *after, *through)
    return got[0] if single else got


def shape(*dims, dtype=BF16):
    return jax.ShapeDtypeStruct(dims, dtype)


def probs_kernel(at_ref, q_ref, k_ref, up_ref, p_ref, dv_ref, bias_ref, s_ref, dv_acc):
    rows = lax.broadcasted_iota(jnp.int32, (COUNT, COUNT), 0)
    cols = lax.broadcasted_iota(jnp.int32, (COUNT, COUNT), 1)
    start = jnp.zeros((COUNT, COUNT), jnp.int32)
    end = jnp.int32(0)
    for doc in range(3):
        end = end + at_ref[5 + doc]
        start = jnp.where(rows >= end, end, start)
    bias_ref[...] = jnp.where((cols <= rows) & (cols >= start), 0.0, -1e30).astype(F32)
    dv_acc[...] = jnp.zeros_like(dv_acc)
    for i in range(BLOCKS):
        width = BLOCK * (i + 1)
        at = pl.ds(BLOCK * i, BLOCK)
        qs = jnp.concatenate([q_ref[at, pl.ds(HEAD * h, HEAD)] for h in range(GROUP)], axis=0)
        s_ref[:, :width] = dot(qs, k_ref[:width, :], (1, 1))
        for h in range(GROUP):
            scores = s_ref[pl.ds(BLOCK * h, BLOCK), :width] * (FACTOR * LOG2E) + bias_ref[at, :width]
            expo = jnp.exp2(scores - jnp.max(scores, axis=1, keepdims=True))
            probs = expo * (1.0 / jnp.sum(expo, axis=1, keepdims=True))
            p_ref[h, at, :width] = probs.astype(BF16)
        low = jnp.concatenate([p_ref[h, at, :width] for h in range(GROUP)], axis=0)
        ups = jnp.concatenate([up_ref[at, pl.ds(HEAD * h, HEAD)] for h in range(GROUP)], axis=0)
        dv_acc[:, :width] += dot(ups, low, (0, 0))
    dv_ref[...] = dv_acc[...].T


PROBS_SCRATCH = [pltpu.VMEM((COUNT, COUNT), F32), pltpu.VMEM((GROUP * BLOCK, COUNT), F32), pltpu.VMEM((HEAD, COUNT), F32)]


def first_probs_kernel(at_ref, q_hbm, k_hbm, up_hbm, p_ref, dv_ref, q_ref, k_ref, up_ref, sems, *scratch):
    copies = [
        pltpu.make_async_copy(a.at[:, pl.ds(0, b.shape[1])], b, sems.at[j])
        for j, (a, b) in enumerate(((q_hbm, q_ref), (k_hbm, k_ref), (up_hbm, up_ref)))
    ]
    for copy in copies:
        copy.start()
    for copy in copies:
        copy.wait()
    probs_kernel(at_ref, q_ref, k_ref, up_ref, p_ref, dv_ref, *scratch)


def probs_part(g, at, queries, keys, upstream, dv, after):
    wide = pl.BlockSpec((COUNT, WIDE), lambda i: (0, g))
    narrow = pl.BlockSpec((COUNT, HEAD), lambda i: (0, g))
    outs = [shape(GROUP, COUNT, COUNT), shape(COUNT, 4 * HEAD, dtype=F32)]
    if g == 0:
        blocks = [pltpu.VMEM((COUNT, WIDE), BF16), pltpu.VMEM((COUNT, HEAD), BF16), pltpu.VMEM((COUNT, WIDE), BF16)]
        return call(
            first_probs_kernel, "probs_part", outs, [(SMEM, at), (HBM, queries), (HBM, keys), (HBM, upstream)], after,
            out_specs=[VMEM, narrow], grid=(1,), scratch_shapes=blocks + [pltpu.SemaphoreType.DMA((3,))] + PROBS_SCRATCH,
        )

    def kernel(*refs):
        probs_kernel(*refs[:4], *refs[5:])

    return call(
        kernel, "probs_part", outs, [(SMEM, at), (wide, queries), (narrow, keys), (wide, upstream), (ANY, dv)], after,
        out_specs=[VMEM, narrow], grid=(1,), scratch_shapes=PROBS_SCRATCH, input_output_aliases={4: 1},
    )


def grads_kernel(g, at_ref, q_ref, k_ref, up_ref, mine_ref, theirs_ref, p_ref, gq_ref, gk_ref, token_ref, dp_ref, ds_ref, dk_acc):
    token_ref[...] = jnp.zeros_like(token_ref)
    dk_acc[...] = jnp.zeros_like(dk_acc)
    col = pl.ds(HEAD * (g % 2), HEAD)
    all_values = jnp.where(at_ref[3] == g // 2, mine_ref[:, col], theirs_ref[:, col])
    for i in range(BLOCKS):
        width = BLOCK * (i + 1)
        at = pl.ds(BLOCK * i, BLOCK)
        ups = jnp.concatenate([up_ref[at, pl.ds(HEAD * h, HEAD)] for h in range(GROUP)], axis=0)
        dp_ref[:, :width] = dot(ups, all_values[:width], (1, 1))
        for h in range(GROUP):
            rows = pl.ds(BLOCK * h, BLOCK)
            dprobs = dp_ref[rows, :width]
            probs = p_ref[h, at, :width].astype(F32)
            delta = jnp.sum(probs * dprobs, axis=1, keepdims=True)
            ds_ref[rows, :width] = (probs * (dprobs - delta)).astype(BF16)
        dscores = ds_ref[:, :width]
        gq = dot(dscores, k_ref[:width, :], (1, 0)) * FACTOR
        for h in range(GROUP):
            gq_ref[at, pl.ds(HEAD * h, HEAD)] = gq[BLOCK * h : BLOCK * (h + 1)].astype(BF16)
        qs = jnp.concatenate([q_ref[at, pl.ds(HEAD * h, HEAD)] for h in range(GROUP)], axis=0)
        dk_acc[:, :width] += dot(qs, dscores, (0, 0))
    gk_ref[...] = (dk_acc[...] * FACTOR).T.astype(BF16)


def grads_part(g, at, queries, keys, upstream, mine, theirs, probs, held, after):
    wide = pl.BlockSpec((COUNT, WIDE), lambda i: (0, g))
    narrow = pl.BlockSpec((COUNT, HEAD), lambda i: (0, g))
    ins = [(SMEM, at), (wide, queries), (narrow, keys), (wide, upstream), (VMEM, mine), (VMEM, theirs), (VMEM, probs)]

    def kernel(*refs):
        grads_kernel(g, *refs[:7], *refs[len(refs) - 6 :])

    extra = {}
    if held is not None:
        ins += [(ANY, held[0]), (ANY, held[1])]
        extra["input_output_aliases"] = {7: 0, 8: 1}
    return call(
        kernel, "grads_part", [shape(*queries.shape), shape(*keys.shape), TOKEN], ins, after,
        out_specs=[wide, narrow, VMEM], grid=(1,),
        scratch_shapes=[pltpu.VMEM((GROUP * BLOCK, COUNT), F32), pltpu.VMEM((GROUP * BLOCK, COUNT), BF16), pltpu.VMEM((HEAD, COUNT), F32)], **extra,
    )


Z_ORDER = (0, 4, 2, 6, 1, 5, 3, 7)
SHARD = 32
CHIP = 2 * SHARD
HALF = 256
DEPTH = 4096


def own_columns(at_ref):
    return pl.ds(pl.multiple_of(at_ref[3] * HALF, HALF), HALF)


def first_join(at_ref, own_hbm, other_ref, out_ref, sem):
    c, cols = at_ref[3], own_columns(at_ref)
    copy = pltpu.make_async_copy(
        own_hbm.at[:, cols], out_ref.at[pl.ds(pl.multiple_of(c * SHARD, SHARD), SHARD), :], sem
    )
    copy.start()
    out_ref[pl.ds(pl.multiple_of((1 - c) * SHARD, SHARD), SHARD), :] = other_ref[:, cols]
    copy.wait()


def copy_kernel(in_ref, out_ref, sem):
    copy = pltpu.make_async_copy(in_ref, out_ref, sem)
    copy.start()
    copy.wait()


def join_kernel(own_ref, other_ref, out_ref):
    n = own_ref.shape[0]
    out_ref[:n, :] = own_ref[...]
    out_ref[n:, :] = other_ref[...]


def core_join_kernel(at_ref, own_ref, got1, got2, got3, first_ref, second_ref):
    n = own_ref.shape[0]
    first_ref[:n, :] = own_ref[...]
    first_ref[n:, :] = got1[...]

    @pl.when(at_ref[3] == 0)
    def _():
        second_ref[:n, :] = own_ref[...]
        second_ref[n:, :] = got1[...]

    @pl.when(at_ref[3] == 1)
    def _():
        second_ref[:n, :] = got2[...]
        second_ref[n:, :] = got3[...]


def put_in_order(at_ref, pieces, codes_ref):
    z, y, x, c = at_ref[0], at_ref[1], at_ref[2], at_ref[3]
    first, second, got1, got2, got3 = pieces

    def place(piece, half, k, xi):
        for zi in range(8):
            to = ((z ^ Z_ORDER[zi]) * 4 + ((y + 4 - k) & 3)) * 2 + (x ^ xi)
            rows = pl.ds(pl.multiple_of(to * CHIP, CHIP), CHIP)
            codes_ref[rows, :] = piece[pl.ds((half * 8 + zi) * CHIP, CHIP), :]

    @pl.when(c == 0)
    def _():
        for k, piece in enumerate((first, got1, got2, got3)):
            for xi in range(2):
                place(piece, xi, k, xi)

    @pl.when(c == 1)
    def _():
        for j, piece in enumerate((first, second, got1, got2)):
            for half in range(2):
                place(piece, half, 2 * (j % 2) + half, j // 2)


def raw_kernel(at_ref, own_ref, other_ref, dv_own, dv_other, scale_ref, *refs):
    pieces, (mine_ref, theirs_ref, sums_ref, codes_ref) = refs[:5], refs[5:]
    put_in_order(at_ref, pieces, codes_ref)
    cols = own_columns(at_ref)
    scale = scale_ref[:, cols]
    sums = jnp.zeros((1, HALF), F32)
    for hidden_ref, dv_ref, values_ref in ((other_ref, dv_other, theirs_ref), (own_ref, dv_own, mine_ref)):
        raw = dot(hidden_ref[...], codes_ref[...], (1, 0))
        values_ref[...] = (raw * scale).astype(BF16)
        sums += jnp.sum(raw * dv_ref[:, cols], axis=0, keepdims=True)
    sums_ref[...] = sums


def raw_part(at, hidden, hidden_other, dv, dv_other, scale, pieces):
    return call(
        raw_kernel, "raw_part", [shape(COUNT, HALF), shape(COUNT, HALF), shape(1, HALF, dtype=F32)],
        [(SMEM, at)] + [(VMEM, a) for a in [hidden, hidden_other, dv, dv_other, scale] + pieces],
        scratch_shapes=[pltpu.VMEM((DEPTH, HALF), BF16)],
    )


NEAR = 640
BESIDES = DEPTH // 2 - NEAR


def split_kernel(at_ref, dv_ref, scale_ref, *refs):
    pieces, (kept_ref, near_ref, beside_ref, codes_ref) = refs[:5], refs[5:]
    put_in_order(at_ref, pieces, codes_ref)
    s, half = at_ref[4], DEPTH // 2
    kept_ref[...] = codes_ref[pl.ds(pl.multiple_of(s * half, half), half), :]
    base = (1 - s) * half
    for j in range(2):
        cols = pl.ds(j * HALF, HALF)
        near_ref[pl.ds(j * COUNT, COUNT), :] = (dv_ref[:, cols] * scale_ref[:, cols]).astype(BF16)
    near_ref[2 * COUNT :, :] = codes_ref[pl.ds(pl.multiple_of(base, half), NEAR), :]
    beside_ref[...] = codes_ref[pl.ds(pl.multiple_of(base + NEAR, 128), BESIDES), :]


def split_part(at, dv, scale, pieces, after):
    return call(
        split_kernel, "split_part", [shape(DEPTH // 2, HALF), shape(2 * COUNT + NEAR, HALF), shape(BESIDES, HALF)],
        [(SMEM, at), (VMEM, dv), (VMEM, scale)] + [(VMEM, p) for p in pieces], after,
        scratch_shapes=[pltpu.VMEM((DEPTH, HALF), BF16)],
    )


def codes_join_kernel(kept_ref, near_ref, beside_ref, out_ref):
    half = DEPTH // 2
    out_ref[:half, :] = kept_ref[...]
    out_ref[half : half + NEAR, :] = near_ref[2 * COUNT :, :]
    out_ref[half + NEAR :, :] = beside_ref[...]


BATCH = 512


def hidden_kernel(at_ref, dv_ref, scale_ref, near_ref, codes_ref, far_ref, out_ref, token_ref):
    c = at_ref[3]
    terms = []
    for other, ref in enumerate((codes_ref, far_ref)):
        cols = pl.ds(pl.multiple_of((c ^ other) * HALF, HALF), HALF)
        own = (dv_ref[:, cols] * scale_ref[:, cols]).astype(BF16)
        rows = pl.ds(pl.multiple_of((c ^ other) * COUNT, COUNT), COUNT)
        terms += [(own, ref, 0), (near_ref[rows, :], ref, DEPTH // 2)]
    for i in range(0, DEPTH // 2, BATCH):
        total = sum(dot(a, b[pl.ds(base + i, BATCH), :], (1, 1)) for a, b, base in terms)
        out_ref[:, pl.ds(i, BATCH)] = total.astype(BF16)
    token_ref[...] = jnp.zeros_like(token_ref)


def hidden_part(at, *arrays, after):
    return call(
        hidden_kernel, "hidden_part", [shape(COUNT, DEPTH // 2), TOKEN],
        [(SMEM, at)] + [(VMEM, a) for a in arrays], after,
    )


def add_kernel(a_ref, b_ref, out_ref):
    out_ref[...] = a_ref[...] + b_ref[...]


def last_kernel(at_ref, own_ref, other_ref, scale_ref, out_ref):
    c = at_ref[3]
    low = jnp.where(c == 0, own_ref[...], other_ref[...])
    high = jnp.where(c == 0, other_ref[...], own_ref[...])
    out_ref[:, :HALF] = low * scale_ref[:, :HALF]
    out_ref[:, HALF:] = high * scale_ref[:, HALF:]


def pairs(move):
    out = []
    for i in range(128):
        z, y, x, c = move(i // 16, i // 4 % 4, i // 2 % 2, i % 2)
        out.append((i, ((z * 4 + y) * 2 + x) * 2 + c))
    return out


def z_swap(bit):
    return pairs(lambda z, y, x, c: (z ^ bit, y, x, c))


def y_shift(k):
    return pairs(lambda z, y, x, c: (z, (y + k) % 4, x, c))


def y_swap(bit):
    return pairs(lambda z, y, x, c: (z, y ^ bit, x, c))


def core_pairs(move0, move1):
    return [move for c, moves in enumerate((move0, move1)) for move in moves if move[0] % 2 == c]


X_SWAP = pairs(lambda z, y, x, c: (z, y, x ^ 1, c))
C_SWAP = pairs(lambda z, y, x, c: (z, y, x, c ^ 1))
SEQ_SWAP = [(0, 1), (1, 0)]
BESIDE = [(2 * a + s, 2 * b + 1 - s) for a, b in X_SWAP for s in range(2)]


def send(x, perm):
    return lax.ppermute(x, "dp", perm)


def shards(hidden, queries, keys, value_codes, value_scale, upstream, lengths):
    me, s = lax.axis_index("dp"), lax.axis_index("seq")
    place = jnp.stack([me // 16, me // 4 % 4, me // 2 % 2, me % 2, s]).astype(jnp.int32)
    at = jnp.concatenate([place, lengths[0, :3]])
    scale = value_scale.reshape(1, -1)

    rows = call(
        first_join, "join", shape(CHIP, HALF), [(SMEM, at), (HBM, value_codes), (VMEM, send(value_codes, C_SWAP))],
        scratch_shapes=[pltpu.SemaphoreType.DMA],
    )
    probs, dv = [], None
    for g, bit in enumerate((4, 2, 1)):
        got = send(rows, z_swap(bit))
        p, dv = probs_part(g, at, queries, keys, upstream, dv, (rows,))
        probs.append(p)
        n = rows.shape[0]
        ins = [(VMEM, rows), (VMEM, got)]
        if bit > 1:
            rows = call(join_kernel, "join", shape(2 * n, HALF), ins, (p,))
        else:
            hidden = call(
                copy_kernel, "copy", shape(*hidden.shape), [(ANY, hidden)], (rows,),
                out_specs=[ANY], scratch_shapes=[pltpu.SemaphoreType.DMA],
            )
            rows, hidden = call(join_kernel, "join", shape(2 * n, HALF), ins, (p,), (hidden,))
    got = [send(rows, core_pairs(X_SWAP if k == 1 else [], y_shift(k))) for k in (1, 2, 3)]
    hidden_other = send(hidden, C_SWAP)
    p, dv = probs_part(3, at, queries, keys, upstream, dv, (rows,))
    probs.append(p)
    n = rows.shape[0]
    first, second, dv = call(
        core_join_kernel, "join", [shape(2 * n, HALF)] * 2,
        [(SMEM, at)] + [(VMEM, a) for a in [rows] + got], (hidden_other, p), (dv,),
    )
    pieces = [first, second]
    for k, rows in enumerate((first, second, first), 1):
        pieces.append(send(rows, core_pairs(y_shift(k), X_SWAP if k < 3 else [])))
    mine, theirs, sums = raw_part(at, hidden, hidden_other, dv, send(dv, C_SWAP), scale, pieces)

    got = send(sums, X_SWAP)
    values_far = send(theirs, C_SWAP)
    kept, near, beside = split_part(at, dv, scale, pieces, (values_far,))
    sums, near, beside = call(
        add_kernel, "add", shape(1, HALF, dtype=F32), [(VMEM, sums), (VMEM, got)], (kept,), (near, beside)
    )
    near = lax.ppermute(near, "seq", SEQ_SWAP)
    beside = lax.ppermute(beside, ("dp", "seq"), BESIDE)
    held = None
    for g, perm in enumerate((y_swap(1), y_swap(2), z_swap(1), z_swap(2))):
        got = send(sums, perm)
        *held, token = grads_part(g, at, queries, keys, upstream, mine, values_far, probs[g], held, (sums,))
        after = (token,)
        if g == 3:
            codes = call(
                codes_join_kernel, "join", shape(DEPTH, HALF), [(VMEM, kept), (VMEM, near), (VMEM, beside)], (sums,)
            )
            codes_far = send(codes, C_SWAP)
            after += (codes,)
        sums = call(add_kernel, "add", shape(1, HALF, dtype=F32), [(VMEM, sums), (VMEM, got)], after)
    got = send(sums, z_swap(4))
    grad_hidden, token = hidden_part(at, dv, scale, near, codes, codes_far, after=(sums,))
    sums = call(add_kernel, "add", shape(1, HALF, dtype=F32), [(VMEM, sums), (VMEM, got)], (token,))
    last = call(
        last_kernel, "last", shape(1, 2 * HALF, dtype=F32),
        [(SMEM, at), (VMEM, sums), (VMEM, send(sums, C_SWAP)), (VMEM, scale)],
    )
    return held[0], held[1], grad_hidden, last.reshape(-1)


def solution(mesh):
    placed = (
        P("dp", None),
        P("dp", "seq"),
        P("dp", "seq"),
        P("dp", "seq"),
        P("seq"),
        P("dp", "seq"),
        P("dp", None),
    )
    return jax.shard_map(
        shards,
        mesh=mesh,
        in_specs=placed,
        out_specs=(P("dp", "seq"), P("dp", "seq"), P("dp", "seq"), P("seq")),
        check_vma=False,
    )
```

```python
import functools
import math

import jax
import jax.numpy as jnp
from jax import lax
from jax.experimental import pallas as pl
from jax.experimental.pallas import tpu as pltpu
from jax.sharding import PartitionSpec as P

COUNT = 384
HEAD = 128
GROUP = 4
BLOCK = 128
BLOCKS = COUNT // BLOCK
FACTOR = 1.0 / math.sqrt(HEAD)
LOG2E = math.log2(math.e)
BF16 = jnp.bfloat16
F32 = jnp.float32
VMEM_LIMIT = 20 * 1024 * 1024


def dot(a, b, dims):
    return lax.dot_general(a, b, ((dims[:1], dims[1:]), ((), ())), preferred_element_type=F32)

VMEM = pl.BlockSpec(memory_space=pltpu.VMEM)
SMEM = pl.BlockSpec(memory_space=pltpu.SMEM)
ANY = pl.BlockSpec(memory_space=pl.ANY)
HBM = pl.BlockSpec(memory_space=pltpu.HBM)
TOKEN = jax.ShapeDtypeStruct((8, 128), F32)
WIDE = GROUP * HEAD


def call(kernel, name, out_shape, ins, after=(), through=(), **kw):
    specs = [spec for spec, _ in ins]
    args = tuple(pltpu.with_memory_space_constraint(a, pltpu.HBM) if spec is HBM else a for spec, a in ins)
    n_in = len(args) + len(after)
    single = not isinstance(out_shape, (list, tuple))
    outs = [out_shape] if single else list(out_shape)
    kw.setdefault("out_specs", [VMEM] * len(outs))

    n_out = len(outs)
    if through:
        kw["input_output_aliases"] = {n_in + j: n_out + j for j in range(len(through))}
        outs += [jax.ShapeDtypeStruct(a.shape, a.dtype) for a in through]
        kw["out_specs"] = list(kw["out_specs"]) + [ANY] * len(through)
        single = False

    def run(*refs):
        first = n_in + len(through)
        kernel(*refs[: len(args)], *refs[first : first + n_out], *refs[first + n_out + len(through) :])

    got = pl.pallas_call(
        run,
        in_specs=list(specs) + [ANY] * (len(after) + len(through)),
        out_shape=outs,
        compiler_params=pltpu.CompilerParams(vmem_limit_bytes=VMEM_LIMIT),
        cost_estimate=pl.CostEstimate(flops=1000, bytes_accessed=1000, transcendentals=0),
        name=name,
        **kw,
    )(*args, *after, *through)
    return got[0] if single else got


def shape(*dims, dtype=BF16):
    return jax.ShapeDtypeStruct(dims, dtype)


def probs_kernel(at_ref, q_ref, k_ref, up_ref, p_ref, dv_ref, bias_ref, s_ref, dv_acc):
    rows = lax.broadcasted_iota(jnp.int32, (COUNT, COUNT), 0)
    cols = lax.broadcasted_iota(jnp.int32, (COUNT, COUNT), 1)
    start = jnp.zeros((COUNT, COUNT), jnp.int32)
    end = jnp.int32(0)
    for doc in range(3):
        end = end + at_ref[5 + doc]
        start = jnp.where(rows >= end, end, start)
    bias_ref[...] = jnp.where((cols <= rows) & (cols >= start), 0.0, -1e30).astype(F32)
    dv_acc[...] = jnp.zeros_like(dv_acc)
    for i in range(BLOCKS):
        width = BLOCK * (i + 1)
        at = pl.ds(BLOCK * i, BLOCK)
        qs = jnp.concatenate([q_ref[at, pl.ds(HEAD * h, HEAD)] for h in range(GROUP)], axis=0)
        s_ref[:, :width] = dot(qs, k_ref[:width, :], (1, 1))
        for h in range(GROUP):
            scores = s_ref[pl.ds(BLOCK * h, BLOCK), :width] * (FACTOR * LOG2E) + bias_ref[at, :width]
            expo = jnp.exp2(scores - jnp.max(scores, axis=1, keepdims=True))
            probs = expo * (1.0 / jnp.sum(expo, axis=1, keepdims=True))
            p_ref[h, at, :width] = probs.astype(BF16)
        low = jnp.concatenate([p_ref[h, at, :width] for h in range(GROUP)], axis=0)
        ups = jnp.concatenate([up_ref[at, pl.ds(HEAD * h, HEAD)] for h in range(GROUP)], axis=0)
        dv_acc[:, :width] += dot(ups, low, (0, 0))
    dv_ref[...] = dv_acc[...].T


PROBS_SCRATCH = [pltpu.VMEM((COUNT, COUNT), F32), pltpu.VMEM((GROUP * BLOCK, COUNT), F32), pltpu.VMEM((HEAD, COUNT), F32)]


def first_probs_kernel(at_ref, q_hbm, k_hbm, up_hbm, p_ref, dv_ref, q_ref, k_ref, up_ref, sems, *scratch):
    copies = [
        pltpu.make_async_copy(a.at[:, pl.ds(0, b.shape[1])], b, sems.at[j])
        for j, (a, b) in enumerate(((q_hbm, q_ref), (k_hbm, k_ref), (up_hbm, up_ref)))
    ]
    for copy in copies:
        copy.start()
    for copy in copies:
        copy.wait()
    probs_kernel(at_ref, q_ref, k_ref, up_ref, p_ref, dv_ref, *scratch)


def probs_part(g, at, queries, keys, upstream, dv, after):
    wide = pl.BlockSpec((COUNT, WIDE), lambda i: (0, g))
    narrow = pl.BlockSpec((COUNT, HEAD), lambda i: (0, g))
    outs = [shape(GROUP, COUNT, COUNT), shape(COUNT, 4 * HEAD, dtype=F32)]
    if g == 0:
        blocks = [pltpu.VMEM((COUNT, WIDE), BF16), pltpu.VMEM((COUNT, HEAD), BF16), pltpu.VMEM((COUNT, WIDE), BF16)]
        return call(
            first_probs_kernel, "probs_part", outs, [(SMEM, at), (HBM, queries), (HBM, keys), (HBM, upstream)], after,
            out_specs=[VMEM, narrow], grid=(1,), scratch_shapes=blocks + [pltpu.SemaphoreType.DMA((3,))] + PROBS_SCRATCH,
        )

    def kernel(*refs):
        probs_kernel(*refs[:4], *refs[5:])

    return call(
        kernel, "probs_part", outs, [(SMEM, at), (wide, queries), (narrow, keys), (wide, upstream), (ANY, dv)], after,
        out_specs=[VMEM, narrow], grid=(1,), scratch_shapes=PROBS_SCRATCH, input_output_aliases={4: 1},
    )


def grads_kernel(g, at_ref, q_ref, k_ref, up_ref, mine_ref, theirs_ref, p_ref, gq_ref, gk_ref, token_ref, dp_ref, ds_ref, dk_acc):
    token_ref[...] = jnp.zeros_like(token_ref)
    dk_acc[...] = jnp.zeros_like(dk_acc)
    col = pl.ds(HEAD * (g % 2), HEAD)
    all_values = jnp.where(at_ref[3] == g // 2, mine_ref[:, col], theirs_ref[:, col])
    for i in range(BLOCKS):
        width = BLOCK * (i + 1)
        at = pl.ds(BLOCK * i, BLOCK)
        ups = jnp.concatenate([up_ref[at, pl.ds(HEAD * h, HEAD)] for h in range(GROUP)], axis=0)
        dp_ref[:, :width] = dot(ups, all_values[:width], (1, 1))
        for h in range(GROUP):
            rows = pl.ds(BLOCK * h, BLOCK)
            dprobs = dp_ref[rows, :width]
            probs = p_ref[h, at, :width].astype(F32)
            delta = jnp.sum(probs * dprobs, axis=1, keepdims=True)
            ds_ref[rows, :width] = (probs * (dprobs - delta)).astype(BF16)
        dscores = ds_ref[:, :width]
        gq = dot(dscores, k_ref[:width, :], (1, 0)) * FACTOR
        for h in range(GROUP):
            gq_ref[at, pl.ds(HEAD * h, HEAD)] = gq[BLOCK * h : BLOCK * (h + 1)].astype(BF16)
        qs = jnp.concatenate([q_ref[at, pl.ds(HEAD * h, HEAD)] for h in range(GROUP)], axis=0)
        dk_acc[:, :width] += dot(qs, dscores, (0, 0))
    gk_ref[...] = (dk_acc[...] * FACTOR).T.astype(BF16)


def grads_part(g, at, queries, keys, upstream, mine, theirs, probs, held, after):
    wide = pl.BlockSpec((COUNT, WIDE), lambda i: (0, g))
    narrow = pl.BlockSpec((COUNT, HEAD), lambda i: (0, g))
    ins = [(SMEM, at), (wide, queries), (narrow, keys), (wide, upstream), (VMEM, mine), (VMEM, theirs), (VMEM, probs)]

    def kernel(*refs):
        grads_kernel(g, *refs[:7], *refs[len(refs) - 6 :])

    extra = {}
    if held is not None:
        ins += [(ANY, held[0]), (ANY, held[1])]
        extra["input_output_aliases"] = {7: 0, 8: 1}
    return call(
        kernel, "grads_part", [shape(*queries.shape), shape(*keys.shape), TOKEN], ins, after,
        out_specs=[wide, narrow, VMEM], grid=(1,),
        scratch_shapes=[pltpu.VMEM((GROUP * BLOCK, COUNT), F32), pltpu.VMEM((GROUP * BLOCK, COUNT), BF16), pltpu.VMEM((HEAD, COUNT), F32)], **extra,
    )


Z_ORDER = (0, 4, 2, 6, 1, 5, 3, 7)
SHARD = 32
CHIP = 2 * SHARD
HALF = 256
DEPTH = 4096


def own_columns(at_ref):
    return pl.ds(pl.multiple_of(at_ref[3] * HALF, HALF), HALF)


def own_part(at_ref, own_hbm, out_ref, sem):
    copy = pltpu.make_async_copy(own_hbm.at[:, own_columns(at_ref)], out_ref, sem)
    copy.start()
    copy.wait()


def first_join(at_ref, own_ref, other_ref, out_ref):
    c = at_ref[3]
    out_ref[pl.ds(pl.multiple_of(c * SHARD, SHARD), SHARD), :] = own_ref[...]
    out_ref[pl.ds(pl.multiple_of((1 - c) * SHARD, SHARD), SHARD), :] = other_ref[:, own_columns(at_ref)]


def copy_kernel(in_ref, out_ref, sem):
    copy = pltpu.make_async_copy(in_ref, out_ref, sem)
    copy.start()
    copy.wait()


def join_kernel(own_ref, other_ref, out_ref):
    n = own_ref.shape[0]
    out_ref[:n, :] = own_ref[...]
    out_ref[n:, :] = other_ref[...]


def core_join_kernel(at_ref, own_ref, got1, got2, got3, first_ref, second_ref):
    n = own_ref.shape[0]
    first_ref[:n, :] = own_ref[...]
    first_ref[n:, :] = got1[...]

    @pl.when(at_ref[3] == 0)
    def _():
        second_ref[:n, :] = own_ref[...]
        second_ref[n:, :] = got1[...]

    @pl.when(at_ref[3] == 1)
    def _():
        second_ref[:n, :] = got2[...]
        second_ref[n:, :] = got3[...]


def put_in_order(at_ref, pieces, codes_ref):
    z, y, x, c = at_ref[0], at_ref[1], at_ref[2], at_ref[3]
    first, second, got1, got2, got3 = pieces

    def place(piece, half, k, xi):
        for zi in range(8):
            to = ((z ^ Z_ORDER[zi]) * 4 + ((y + 4 - k) & 3)) * 2 + (x ^ xi)
            rows = pl.ds(pl.multiple_of(to * CHIP, CHIP), CHIP)
            codes_ref[rows, :] = piece[pl.ds((half * 8 + zi) * CHIP, CHIP), :]

    @pl.when(c == 0)
    def _():
        for k, piece in enumerate((first, got1, got2, got3)):
            for xi in range(2):
                place(piece, xi, k, xi)

    @pl.when(c == 1)
    def _():
        for j, piece in enumerate((first, second, got1, got2)):
            for half in range(2):
                place(piece, half, 2 * (j % 2) + half, j // 2)


NEAR = 640
BESIDES = DEPTH // 2 - NEAR


def raw_kernel(at_ref, own_ref, other_ref, dv_own, dv_other, scale_ref, *refs):
    pieces, (mine_ref, theirs_ref, sums_ref, kept_ref, near_ref, beside_ref, codes_ref) = refs[:5], refs[5:]
    put_in_order(at_ref, pieces, codes_ref)
    cols = own_columns(at_ref)
    scale = scale_ref[:, cols]
    sums = jnp.zeros((1, HALF), F32)
    for hidden_ref, dv_ref, values_ref in ((other_ref, dv_other, theirs_ref), (own_ref, dv_own, mine_ref)):
        raw = dot(hidden_ref[...], codes_ref[...], (1, 0))
        values_ref[...] = (raw * scale).astype(BF16)
        sums += jnp.sum(raw * dv_ref[:, cols], axis=0, keepdims=True)
    sums_ref[...] = sums
    s, half = at_ref[4], DEPTH // 2
    kept_ref[...] = codes_ref[pl.ds(pl.multiple_of(s * half, half), half), :]
    base = (1 - s) * half
    for j in range(2):
        part = pl.ds(j * HALF, HALF)
        near_ref[pl.ds(j * COUNT, COUNT), :] = (dv_own[:, part] * scale_ref[:, part]).astype(BF16)
    near_ref[2 * COUNT :, :] = codes_ref[pl.ds(pl.multiple_of(base, half), NEAR), :]
    beside_ref[...] = codes_ref[pl.ds(pl.multiple_of(base + NEAR, 128), BESIDES), :]


def raw_part(at, hidden, hidden_other, dv, dv_other, scale, pieces):
    outs = [shape(COUNT, HALF), shape(COUNT, HALF), shape(1, HALF, dtype=F32)]
    outs += [shape(DEPTH // 2, HALF), shape(2 * COUNT + NEAR, HALF), shape(BESIDES, HALF)]
    return call(
        raw_kernel, "raw_part", outs,
        [(SMEM, at)] + [(VMEM, a) for a in [hidden, hidden_other, dv, dv_other, scale] + pieces],
        scratch_shapes=[pltpu.VMEM((DEPTH, HALF), BF16)],
    )


def codes_join_kernel(kept_ref, near_ref, beside_ref, out_ref):
    half = DEPTH // 2
    out_ref[:half, :] = kept_ref[...]
    out_ref[half : half + NEAR, :] = near_ref[2 * COUNT :, :]
    out_ref[half + NEAR :, :] = beside_ref[...]


BATCH = 512


def hidden_kernel(at_ref, dv_ref, scale_ref, near_ref, codes_ref, far_ref, out_ref, token_ref):
    c = at_ref[3]
    terms = []
    for other, ref in enumerate((codes_ref, far_ref)):
        cols = pl.ds(pl.multiple_of((c ^ other) * HALF, HALF), HALF)
        own = (dv_ref[:, cols] * scale_ref[:, cols]).astype(BF16)
        rows = pl.ds(pl.multiple_of((c ^ other) * COUNT, COUNT), COUNT)
        terms += [(own, ref, 0), (near_ref[rows, :], ref, DEPTH // 2)]
    for i in range(0, DEPTH // 2, BATCH):
        total = sum(dot(a, b[pl.ds(base + i, BATCH), :], (1, 1)) for a, b, base in terms)
        out_ref[:, pl.ds(i, BATCH)] = total.astype(BF16)
    token_ref[...] = jnp.zeros_like(token_ref)


def hidden_part(at, *arrays, after):
    return call(
        hidden_kernel, "hidden_part", [shape(COUNT, DEPTH // 2), TOKEN],
        [(SMEM, at)] + [(VMEM, a) for a in arrays], after,
    )


def add_kernel(a_ref, b_ref, out_ref):
    out_ref[...] = a_ref[...] + b_ref[...]


def pairs(move):
    out = []
    for i in range(128):
        z, y, x, c = move(i // 16, i // 4 % 4, i // 2 % 2, i % 2)
        out.append((i, ((z * 4 + y) * 2 + x) * 2 + c))
    return out


def z_swap(bit):
    return pairs(lambda z, y, x, c: (z ^ bit, y, x, c))


def y_shift(k):
    return pairs(lambda z, y, x, c: (z, (y + k) % 4, x, c))


def y_swap(bit):
    return pairs(lambda z, y, x, c: (z, y ^ bit, x, c))


def core_pairs(move0, move1):
    return [move for c, moves in enumerate((move0, move1)) for move in moves if move[0] % 2 == c]


X_SWAP = pairs(lambda z, y, x, c: (z, y, x ^ 1, c))
C_SWAP = pairs(lambda z, y, x, c: (z, y, x, c ^ 1))
SEQ_SWAP = [(0, 1), (1, 0)]
BESIDE = [(2 * a + s, 2 * b + 1 - s) for a, b in X_SWAP for s in range(2)]


def send(x, perm):
    return lax.ppermute(x, "dp", perm)


def shards(hidden, queries, keys, value_codes, value_scale, upstream, lengths):
    me, s = lax.axis_index("dp"), lax.axis_index("seq")
    place = jnp.stack([me // 16, me // 4 % 4, me // 2 % 2, me % 2, s]).astype(jnp.int32)
    at = jnp.concatenate([place, lengths[0, :3]])
    scale = value_scale.reshape(1, -1)

    own = call(
        own_part, "own", shape(SHARD, HALF), [(SMEM, at), (HBM, value_codes)], scratch_shapes=[pltpu.SemaphoreType.DMA]
    )
    other = send(value_codes, C_SWAP)
    rows = call(first_join, "join", shape(CHIP, HALF), [(SMEM, at), (VMEM, own), (VMEM, other)])
    probs, dv = [], None
    for bit, heads in ((4, (0,)), (2, (1, 2)), (1, (3,))):
        got = send(rows, z_swap(bit))
        for g in heads:
            p, dv = probs_part(g, at, queries, keys, upstream, dv, (rows,))
            probs.append(p)
        n = rows.shape[0]
        ins = [(VMEM, rows), (VMEM, got)]
        if bit > 1:
            rows = call(join_kernel, "join", shape(2 * n, HALF), ins, (p,))
        else:
            hidden = call(
                copy_kernel, "copy", shape(*hidden.shape), [(ANY, hidden)], (rows,),
                out_specs=[ANY], scratch_shapes=[pltpu.SemaphoreType.DMA],
            )
            rows, hidden, dv = call(join_kernel, "join", shape(2 * n, HALF), ins, (p,), (hidden, dv))
    got = [send(rows, core_pairs(X_SWAP if k == 1 else [], y_shift(k))) for k in (1, 2, 3)]
    hidden_other, dv_other = send(hidden, C_SWAP), send(dv, C_SWAP)
    n = rows.shape[0]
    first, second = call(
        core_join_kernel, "join", [shape(2 * n, HALF)] * 2, [(SMEM, at)] + [(VMEM, a) for a in [rows] + got],
        (dv_other,),
    )
    pieces = [first, second]
    for k, rows in enumerate((first, second, first), 1):
        pieces.append(send(rows, core_pairs(y_shift(k), X_SWAP if k < 3 else [])))
    mine, theirs, sums, kept, near, beside = raw_part(at, hidden, hidden_other, dv, dv_other, scale, pieces)

    values_far = send(theirs, C_SWAP)
    held = None
    for step, perm in enumerate((X_SWAP, y_swap(1), y_swap(2), z_swap(1), z_swap(2), z_swap(4))):
        if step == 1:
            near = lax.ppermute(near, "seq", SEQ_SWAP)
            beside = lax.ppermute(beside, ("dp", "seq"), BESIDE)
        got = send(sums, perm)
        through = ()
        if step < 4:
            *held, token = grads_part(step, at, queries, keys, upstream, mine, values_far, probs[step], held, (sums,))
            if step == 0:
                through = (near, beside)
        elif step == 4:
            token = codes = call(
                codes_join_kernel, "join", shape(DEPTH, HALF), [(VMEM, kept), (VMEM, near), (VMEM, beside)], (sums,)
            )
            codes_far = send(codes, C_SWAP)
        else:
            grad_hidden, token = hidden_part(at, dv, scale, near, codes, codes_far, after=(sums,))
        ins = [(VMEM, sums), (VMEM, got)]
        if through:
            sums, near, beside = call(add_kernel, "add", shape(1, HALF, dtype=F32), ins, (token,), through)
        else:
            sums = call(add_kernel, "add", shape(1, HALF, dtype=F32), ins, (token,))
    far = send(sums, C_SWAP)
    both = jnp.concatenate([jnp.where(me % 2 == 0, sums, far), jnp.where(me % 2 == 0, far, sums)], axis=1)
    return held[0], held[1], grad_hidden, (both * scale).reshape(-1)


def solution(mesh):
    placed = (
        P("dp", None),
        P("dp", "seq"),
        P("dp", "seq"),
        P("dp", "seq"),
        P("seq"),
        P("dp", "seq"),
        P("dp", None),
    )
    return jax.shard_map(
        shards,
        mesh=mesh,
        in_specs=placed,
        out_specs=(P("dp", "seq"), P("dp", "seq"), P("dp", "seq"), P("seq")),
        check_vma=False,
    )
```

```python
import functools
import math

import jax
import jax.numpy as jnp
from jax import lax
from jax.experimental import pallas as pl
from jax.experimental.pallas import tpu as pltpu
from jax.sharding import PartitionSpec as P

COUNT = 384
HEAD = 128
GROUP = 4
BLOCK = 128
BLOCKS = COUNT // BLOCK
FACTOR = 1.0 / math.sqrt(HEAD)
LOG2E = math.log2(math.e)
BF16 = jnp.bfloat16
F32 = jnp.float32
VMEM_LIMIT = 20 * 1024 * 1024


def dot(a, b, dims):
    return lax.dot_general(a, b, ((dims[:1], dims[1:]), ((), ())), preferred_element_type=F32)

VMEM = pl.BlockSpec(memory_space=pltpu.VMEM)
SMEM = pl.BlockSpec(memory_space=pltpu.SMEM)
ANY = pl.BlockSpec(memory_space=pl.ANY)
HBM = pl.BlockSpec(memory_space=pltpu.HBM)
TOKEN = jax.ShapeDtypeStruct((8, 128), F32)
WIDE = GROUP * HEAD


def call(kernel, name, out_shape, ins, after=(), through=(), **kw):
    specs = [spec for spec, _ in ins]
    args = tuple(pltpu.with_memory_space_constraint(a, pltpu.HBM) if spec is HBM else a for spec, a in ins)
    n_in = len(args) + len(after)
    single = not isinstance(out_shape, (list, tuple))
    outs = [out_shape] if single else list(out_shape)
    kw.setdefault("out_specs", [VMEM] * len(outs))

    n_out = len(outs)
    if through:
        kw["input_output_aliases"] = {n_in + j: n_out + j for j in range(len(through))}
        outs += [jax.ShapeDtypeStruct(a.shape, a.dtype) for a in through]
        kw["out_specs"] = list(kw["out_specs"]) + [ANY] * len(through)
        single = False

    def run(*refs):
        first = n_in + len(through)
        kernel(*refs[: len(args)], *refs[first : first + n_out], *refs[first + n_out + len(through) :])

    got = pl.pallas_call(
        run,
        in_specs=list(specs) + [ANY] * (len(after) + len(through)),
        out_shape=outs,
        compiler_params=pltpu.CompilerParams(vmem_limit_bytes=VMEM_LIMIT),
        cost_estimate=pl.CostEstimate(flops=1000, bytes_accessed=1000, transcendentals=0),
        name=name,
        **kw,
    )(*args, *after, *through)
    return got[0] if single else got


def shape(*dims, dtype=BF16):
    return jax.ShapeDtypeStruct(dims, dtype)


def probs_kernel(at_ref, q_ref, k_ref, up_ref, p_ref, dv_ref, bias_ref, s_ref, dv_acc):
    row = lax.broadcasted_iota(jnp.int32, (COUNT, 1), 0)
    start = jnp.zeros((COUNT, 1), jnp.int32)
    end = jnp.int32(0)
    for doc in range(3):
        end = end + at_ref[5 + doc]
        start = jnp.where(row >= end, end, start)
    rows = lax.broadcasted_iota(jnp.int32, (COUNT, COUNT), 0)
    cols = lax.broadcasted_iota(jnp.int32, (COUNT, COUNT), 1)
    bias_ref[...] = jnp.where((cols <= rows) & (cols >= start), 0.0, -1e30).astype(F32)
    dv_acc[...] = jnp.zeros_like(dv_acc)
    for i in range(BLOCKS):
        width = BLOCK * (i + 1)
        at = pl.ds(BLOCK * i, BLOCK)
        qs = jnp.concatenate([q_ref[at, pl.ds(HEAD * h, HEAD)] for h in range(GROUP)], axis=0)
        s_ref[:, :width] = dot(qs, k_ref[:width, :], (1, 1))
        for h in range(GROUP):
            scores = s_ref[pl.ds(BLOCK * h, BLOCK), :width] * (FACTOR * LOG2E) + bias_ref[at, :width]
            expo = jnp.exp2(scores - jnp.max(scores, axis=1, keepdims=True))
            probs = expo * (1.0 / jnp.sum(expo, axis=1, keepdims=True))
            p_ref[h, at, :width] = probs.astype(BF16)
        low = jnp.concatenate([p_ref[h, at, :width] for h in range(GROUP)], axis=0)
        ups = jnp.concatenate([up_ref[at, pl.ds(HEAD * h, HEAD)] for h in range(GROUP)], axis=0)
        dv_acc[:, :width] += dot(ups, low, (0, 0))
    dv_ref[...] = dv_acc[...].T


PROBS_SCRATCH = [pltpu.VMEM((COUNT, COUNT), F32), pltpu.VMEM((GROUP * BLOCK, COUNT), F32), pltpu.VMEM((HEAD, COUNT), F32)]


def first_probs_kernel(
    at_ref, q_hbm, k_hbm, up_hbm, hidden_hbm, p_ref, dv_ref, hidden_out, q_ref, k_ref, up_ref, sems, *scratch
):
    copies = [
        pltpu.make_async_copy(a.at[:, pl.ds(0, b.shape[1])], b, sems.at[j])
        for j, (a, b) in enumerate(((q_hbm, q_ref), (k_hbm, k_ref), (up_hbm, up_ref)))
    ]
    for copy in copies:
        copy.start()
    whole = pltpu.make_async_copy(hidden_hbm, hidden_out, sems.at[3])
    whole.start()
    for copy in copies:
        copy.wait()
    probs_kernel(at_ref, q_ref, k_ref, up_ref, p_ref, dv_ref, *scratch)
    whole.wait()


def probs_part(g, at, queries, keys, upstream, dv, after, hidden=None):
    wide = pl.BlockSpec((COUNT, WIDE), lambda i: (0, g))
    narrow = pl.BlockSpec((COUNT, HEAD), lambda i: (0, g))
    outs = [shape(GROUP, COUNT, COUNT), shape(COUNT, 4 * HEAD, dtype=F32)]
    if hidden is not None:
        blocks = [pltpu.VMEM((COUNT, WIDE), BF16), pltpu.VMEM((COUNT, HEAD), BF16), pltpu.VMEM((COUNT, WIDE), BF16)]
        return call(
            first_probs_kernel, "probs_part", outs + [shape(*hidden.shape)],
            [(SMEM, at), (HBM, queries), (HBM, keys), (HBM, upstream), (HBM, hidden)], after, out_specs=[VMEM, narrow, ANY],
            grid=(1,), scratch_shapes=blocks + [pltpu.SemaphoreType.DMA((4,))] + PROBS_SCRATCH,
        )

    def kernel(*refs):
        probs_kernel(*refs[:4], *refs[5:])

    return call(
        kernel, "probs_part", outs, [(SMEM, at), (wide, queries), (narrow, keys), (wide, upstream), (ANY, dv)], after,
        out_specs=[VMEM, narrow], grid=(1,), scratch_shapes=PROBS_SCRATCH, input_output_aliases={4: 1},
    )


def grads_kernel(g, at_ref, q_ref, k_ref, up_ref, mine_ref, theirs_ref, p_ref, gq_ref, gk_ref, token_ref, dp_ref, ds_ref, dk_acc):
    token_ref[...] = jnp.zeros_like(token_ref)
    dk_acc[...] = jnp.zeros_like(dk_acc)
    col = pl.ds(HEAD * (g % 2), HEAD)
    all_values = jnp.where(at_ref[3] == g // 2, mine_ref[:, col], theirs_ref[:, col])
    for i in range(BLOCKS):
        width = BLOCK * (i + 1)
        at = pl.ds(BLOCK * i, BLOCK)
        ups = jnp.concatenate([up_ref[at, pl.ds(HEAD * h, HEAD)] for h in range(GROUP)], axis=0)
        dp_ref[:, :width] = dot(ups, all_values[:width], (1, 1))
        for h in range(GROUP):
            rows = pl.ds(BLOCK * h, BLOCK)
            dprobs = dp_ref[rows, :width]
            probs = p_ref[h, at, :width].astype(F32)
            delta = jnp.sum(probs * dprobs, axis=1, keepdims=True)
            ds_ref[rows, :width] = (probs * (dprobs - delta)).astype(BF16)
        dscores = ds_ref[:, :width]
        gq = dot(dscores, k_ref[:width, :], (1, 0)) * FACTOR
        for h in range(GROUP):
            gq_ref[at, pl.ds(HEAD * h, HEAD)] = gq[BLOCK * h : BLOCK * (h + 1)].astype(BF16)
        qs = jnp.concatenate([q_ref[at, pl.ds(HEAD * h, HEAD)] for h in range(GROUP)], axis=0)
        dk_acc[:, :width] += dot(qs, dscores, (0, 0))
    gk_ref[...] = (dk_acc[...] * FACTOR).T.astype(BF16)


def grads_part(g, at, queries, keys, upstream, mine, theirs, probs, held, after):
    wide = pl.BlockSpec((COUNT, WIDE), lambda i: (0, g))
    narrow = pl.BlockSpec((COUNT, HEAD), lambda i: (0, g))
    ins = [(SMEM, at), (wide, queries), (narrow, keys), (wide, upstream), (VMEM, mine), (VMEM, theirs), (VMEM, probs)]

    def kernel(*refs):
        grads_kernel(g, *refs[:7], *refs[len(refs) - 6 :])

    extra = {}
    if held is not None:
        ins += [(ANY, held[0]), (ANY, held[1])]
        extra["input_output_aliases"] = {7: 0, 8: 1}
    return call(
        kernel, "grads_part", [shape(*queries.shape), shape(*keys.shape), TOKEN], ins, after,
        out_specs=[wide, narrow, VMEM], grid=(1,),
        scratch_shapes=[pltpu.VMEM((GROUP * BLOCK, COUNT), F32), pltpu.VMEM((GROUP * BLOCK, COUNT), BF16), pltpu.VMEM((HEAD, COUNT), F32)], **extra,
    )


Z_ORDER = (0, 4, 2, 6, 1, 5, 3, 7)
SHARD = 32
CHIP = 2 * SHARD
HALF = 256
DEPTH = 4096


def own_columns(at_ref):
    return pl.ds(pl.multiple_of(at_ref[3] * HALF, HALF), HALF)


def own_part(at_ref, own_hbm, out_ref, sem):
    copy = pltpu.make_async_copy(own_hbm.at[:, own_columns(at_ref)], out_ref, sem)
    copy.start()
    copy.wait()


def first_join(at_ref, own_ref, other_ref, out_ref):
    c = at_ref[3]
    out_ref[pl.ds(pl.multiple_of(c * SHARD, SHARD), SHARD), :] = own_ref[...]
    out_ref[pl.ds(pl.multiple_of((1 - c) * SHARD, SHARD), SHARD), :] = other_ref[:, own_columns(at_ref)]


def join_kernel(own_ref, other_ref, out_ref):
    n = own_ref.shape[0]
    out_ref[:n, :] = own_ref[...]
    out_ref[n:, :] = other_ref[...]


def join_take_kernel(at_ref, own_ref, other_ref, dv_ref, out_ref, dv_out):
    join_kernel(own_ref, other_ref, out_ref)
    dv_out[...] = dv_ref[:, pl.ds(pl.multiple_of((1 - at_ref[3]) * HALF, HALF), HALF)]


def core_join_kernel(at_ref, own_ref, got1, got2, got3, first_ref, second_ref):
    n = own_ref.shape[0]
    first_ref[:n, :] = own_ref[...]
    first_ref[n:, :] = got1[...]

    @pl.when(at_ref[3] == 0)
    def _():
        second_ref[:n, :] = own_ref[...]
        second_ref[n:, :] = got1[...]

    @pl.when(at_ref[3] == 1)
    def _():
        second_ref[:n, :] = got2[...]
        second_ref[n:, :] = got3[...]


def put_in_order(at_ref, pieces, codes_ref):
    z, y, x, c = at_ref[0], at_ref[1], at_ref[2], at_ref[3]
    first, second, got1, got2, got3 = pieces

    def place(piece, half, k, xi):
        for zi in range(8):
            to = ((z ^ Z_ORDER[zi]) * 4 + ((y + 4 - k) & 3)) * 2 + (x ^ xi)
            rows = pl.ds(pl.multiple_of(to * CHIP, CHIP), CHIP)
            codes_ref[rows, :] = piece[pl.ds((half * 8 + zi) * CHIP, CHIP), :]

    @pl.when(c == 0)
    def _():
        for k, piece in enumerate((first, got1, got2, got3)):
            for xi in range(2):
                place(piece, xi, k, xi)

    @pl.when(c == 1)
    def _():
        for j, piece in enumerate((first, second, got1, got2)):
            for half in range(2):
                place(piece, half, 2 * (j % 2) + half, j // 2)


NEAR = 640
BESIDES = DEPTH // 2 - NEAR


def raw_kernel(at_ref, own_ref, other_ref, dv_own, dv_other, scale_ref, *refs):
    pieces, (mine_ref, theirs_ref, sums_ref, kept_ref, near_ref, beside_ref, codes_ref) = refs[:5], refs[5:]
    put_in_order(at_ref, pieces, codes_ref)
    cols = own_columns(at_ref)
    scale = scale_ref[:, cols]
    sums = jnp.zeros((1, HALF), F32)
    terms = ((other_ref, dv_other[...], theirs_ref), (own_ref, dv_own[:, cols], mine_ref))
    for hidden_ref, dv, values_ref in terms:
        raw = dot(hidden_ref[...], codes_ref[...], (1, 0))
        values_ref[...] = (raw * scale).astype(BF16)
        sums += jnp.sum(raw * dv, axis=0, keepdims=True)
    sums_ref[...] = sums
    s, half = at_ref[4], DEPTH // 2
    kept_ref[...] = codes_ref[pl.ds(pl.multiple_of(s * half, half), half), :]
    base = (1 - s) * half
    for j in range(2):
        part = pl.ds(j * HALF, HALF)
        near_ref[pl.ds(j * COUNT, COUNT), :] = (dv_own[:, part] * scale_ref[:, part]).astype(BF16)
    near_ref[2 * COUNT :, :] = codes_ref[pl.ds(pl.multiple_of(base, half), NEAR), :]
    beside_ref[...] = codes_ref[pl.ds(pl.multiple_of(base + NEAR, 128), BESIDES), :]


def raw_part(at, hidden, hidden_other, dv, dv_other, scale, pieces):
    outs = [shape(COUNT, HALF), shape(COUNT, HALF), shape(1, HALF, dtype=F32)]
    outs += [shape(DEPTH // 2, HALF), shape(2 * COUNT + NEAR, HALF), shape(BESIDES, HALF)]
    return call(
        raw_kernel, "raw_part", outs,
        [(SMEM, at)] + [(VMEM, a) for a in [hidden, hidden_other, dv, dv_other, scale] + pieces],
        scratch_shapes=[pltpu.VMEM((DEPTH, HALF), BF16)],
    )


def codes_join_kernel(near_ref, beside_ref, out_ref):
    out_ref[:NEAR, :] = near_ref[2 * COUNT :, :]
    out_ref[NEAR:, :] = beside_ref[...]


BATCH = 512


def hidden_terms(c, dv_ref, scale_ref, near_ref, own_codes, seq_codes):
    cols = pl.ds(pl.multiple_of(c * HALF, HALF), HALF)
    own = (dv_ref[:, cols] * scale_ref[:, cols]).astype(BF16)
    far = near_ref[pl.ds(pl.multiple_of(c * COUNT, COUNT), COUNT), :]
    for i in range(0, DEPTH // 2, BATCH):
        rows = pl.ds(i, BATCH)
        yield rows, dot(own, own_codes[rows, :], (1, 1)) + dot(far, seq_codes[rows, :], (1, 1))


def own_terms_kernel(at_ref, dv_ref, scale_ref, near_ref, own_codes, seq_codes, out_ref):
    for rows, total in hidden_terms(at_ref[3], dv_ref, scale_ref, near_ref, own_codes, seq_codes):
        out_ref[:, rows] = total


def last_kernel(
    at_ref, dv_ref, scale_ref, near_ref, own_codes, seq_codes, part_ref, own0, own1, far0, far1, out_ref, sums_ref
):
    c = at_ref[3]
    own, far = own0[...] + own1[...], far0[...] + far1[...]
    sums_ref[:, :HALF] = jnp.where(c == 0, own, far) * scale_ref[:, :HALF]
    sums_ref[:, HALF:] = jnp.where(c == 0, far, own) * scale_ref[:, HALF:]
    for rows, total in hidden_terms(1 - c, dv_ref, scale_ref, near_ref, own_codes, seq_codes):
        out_ref[:, rows] = (total + part_ref[:, rows]).astype(BF16)


def add_kernel(a_ref, b_ref, out_ref):
    out_ref[...] = a_ref[...] + b_ref[...]


def pairs(move):
    out = []
    for i in range(128):
        z, y, x, c = move(i // 16, i // 4 % 4, i // 2 % 2, i % 2)
        out.append((i, ((z * 4 + y) * 2 + x) * 2 + c))
    return out


def z_swap(bit):
    return pairs(lambda z, y, x, c: (z ^ bit, y, x, c))


def y_shift(k):
    return pairs(lambda z, y, x, c: (z, (y + k) % 4, x, c))


def y_swap(bit):
    return pairs(lambda z, y, x, c: (z, y ^ bit, x, c))


def core_pairs(move0, move1):
    return [move for c, moves in enumerate((move0, move1)) for move in moves if move[0] % 2 == c]


X_SWAP = pairs(lambda z, y, x, c: (z, y, x ^ 1, c))
C_SWAP = pairs(lambda z, y, x, c: (z, y, x, c ^ 1))
SEQ_SWAP = [(0, 1), (1, 0)]
BESIDE = [(2 * a + s, 2 * b + 1 - s) for a, b in X_SWAP for s in range(2)]


def send(x, perm):
    return lax.ppermute(x, "dp", perm)


def shards(hidden, queries, keys, value_codes, value_scale, upstream, lengths):
    me, s = lax.axis_index("dp"), lax.axis_index("seq")
    place = jnp.stack([me // 16, me // 4 % 4, me // 2 % 2, me % 2, s]).astype(jnp.int32)
    at = jnp.concatenate([place, lengths[0, :3]])
    scale = value_scale.reshape(1, -1)

    own = call(
        own_part, "own", shape(SHARD, HALF), [(SMEM, at), (HBM, value_codes)], scratch_shapes=[pltpu.SemaphoreType.DMA]
    )
    other = send(value_codes, C_SWAP)
    rows = call(first_join, "join", shape(CHIP, HALF), [(SMEM, at), (VMEM, own), (VMEM, other)])
    probs, dv = [], None
    for bit, heads in ((4, (0,)), (2, (1, 2)), (1, (3,))):
        got = send(rows, z_swap(bit))
        for g in heads:
            if g == 0:
                p, dv, hidden = probs_part(g, at, queries, keys, upstream, dv, (rows,), hidden)
            else:
                p, dv = probs_part(g, at, queries, keys, upstream, dv, (rows,))
            probs.append(p)
        n = rows.shape[0]
        ins = [(VMEM, rows), (VMEM, got)]
        if bit == 4:
            rows, hidden = call(join_kernel, "join", shape(2 * n, HALF), ins, (p,), (hidden,))
            hidden_other = send(hidden, C_SWAP)
        elif bit == 2:
            rows = call(join_kernel, "join", shape(2 * n, HALF), ins, (p,))
        else:
            rows, dv_half = call(
                join_take_kernel, "join", [shape(2 * n, HALF), shape(COUNT, HALF, dtype=F32)],
                [(SMEM, at)] + ins + [(VMEM, dv)], (hidden_other,),
            )
    got = [send(rows, core_pairs(X_SWAP if k == 1 else [], y_shift(k))) for k in (1, 2, 3)]
    dv_other = send(dv_half, C_SWAP)
    n = rows.shape[0]
    first, second = call(
        core_join_kernel, "join", [shape(2 * n, HALF)] * 2, [(SMEM, at)] + [(VMEM, a) for a in [rows] + got],
        (dv_other,),
    )
    pieces = [first, second]
    for k, rows in enumerate((first, second, first), 1):
        pieces.append(send(rows, core_pairs(y_shift(k), X_SWAP if k < 3 else [])))
    mine, theirs, sums, kept, near, beside = raw_part(at, hidden, hidden_other, dv, dv_other, scale, pieces)

    values_far = send(theirs, C_SWAP)
    held = None
    for step, perm in enumerate((X_SWAP, y_swap(1), y_swap(2), z_swap(1), z_swap(2), z_swap(4))):
        if step == 1:
            near = lax.ppermute(near, "seq", SEQ_SWAP)
            beside = lax.ppermute(beside, ("dp", "seq"), BESIDE)
        got = send(sums, perm)
        through = ()
        if step < 4:
            *held, token = grads_part(step, at, queries, keys, upstream, mine, values_far, probs[step], held, (sums,))
            if step == 0:
                through = (near, beside, kept)
        elif step == 5:
            codes = call(codes_join_kernel, "join", shape(DEPTH // 2, HALF), [(VMEM, near), (VMEM, beside)], (sums,))
            codes_far = send(codes, C_SWAP)
            break
        ins = [(VMEM, sums), (VMEM, got)]
        after = () if step == 4 else (token,)
        if through:
            sums, near, beside, kept = call(add_kernel, "add", shape(1, HALF, dtype=F32), ins, after, through)
            kept_far = send(kept, C_SWAP)
        else:
            sums = call(add_kernel, "add", shape(1, HALF, dtype=F32), ins, after)
    far = [send(sums, C_SWAP), send(sums, pairs(lambda z, y, x, c: (z ^ 4, y, x, c ^ 1)))]
    base = [(SMEM, at), (VMEM, dv), (VMEM, scale), (VMEM, near)]
    part = call(
        own_terms_kernel, "own_terms", shape(COUNT, DEPTH // 2, dtype=F32), base + [(VMEM, kept), (VMEM, codes)], (sums,)
    )
    grad_hidden, last = call(
        last_kernel, "last", [shape(COUNT, DEPTH // 2), shape(1, 2 * HALF, dtype=F32)],
        base + [(VMEM, a) for a in [kept_far, codes_far, part, sums, got] + far],
    )
    return held[0], held[1], grad_hidden, last.reshape(-1)


def solution(mesh):
    placed = (
        P("dp", None),
        P("dp", "seq"),
        P("dp", "seq"),
        P("dp", "seq"),
        P("seq"),
        P("dp", "seq"),
        P("dp", None),
    )
    return jax.shard_map(
        shards,
        mesh=mesh,
        in_specs=placed,
        out_specs=(P("dp", "seq"), P("dp", "seq"), P("dp", "seq"), P("seq")),
        check_vma=False,
    )
```

```python
import functools
import math

import jax
import jax.numpy as jnp
from jax import lax
from jax.experimental import pallas as pl
from jax.experimental.pallas import tpu as pltpu
from jax.sharding import PartitionSpec as P

COUNT = 384
HEAD = 128
GROUP = 4
BLOCK = 128
BLOCKS = COUNT // BLOCK
FACTOR = 1.0 / math.sqrt(HEAD)
LOG2E = math.log2(math.e)
BF16 = jnp.bfloat16
F32 = jnp.float32
VMEM_LIMIT = 20 * 1024 * 1024


def dot(a, b, dims):
    return lax.dot_general(a, b, ((dims[:1], dims[1:]), ((), ())), preferred_element_type=F32)

VMEM = pl.BlockSpec(memory_space=pltpu.VMEM)
SMEM = pl.BlockSpec(memory_space=pltpu.SMEM)
ANY = pl.BlockSpec(memory_space=pl.ANY)
HBM = pl.BlockSpec(memory_space=pltpu.HBM)
TOKEN = jax.ShapeDtypeStruct((8, 128), F32)
WIDE = GROUP * HEAD


def call(kernel, name, out_shape, ins, after=(), through=(), **kw):
    specs = [spec for spec, _ in ins]
    args = tuple(pltpu.with_memory_space_constraint(a, pltpu.HBM) if spec is HBM else a for spec, a in ins)
    n_in = len(args) + len(after)
    single = not isinstance(out_shape, (list, tuple))
    outs = [out_shape] if single else list(out_shape)
    kw.setdefault("out_specs", [VMEM] * len(outs))

    n_out = len(outs)
    if through:
        kw["input_output_aliases"] = {n_in + j: n_out + j for j in range(len(through))}
        outs += [jax.ShapeDtypeStruct(a.shape, a.dtype) for a in through]
        kw["out_specs"] = list(kw["out_specs"]) + [ANY] * len(through)
        single = False

    def run(*refs):
        first = n_in + len(through)
        kernel(*refs[: len(args)], *refs[first : first + n_out], *refs[first + n_out + len(through) :])

    got = pl.pallas_call(
        run,
        in_specs=list(specs) + [ANY] * (len(after) + len(through)),
        out_shape=outs,
        compiler_params=pltpu.CompilerParams(vmem_limit_bytes=VMEM_LIMIT),
        cost_estimate=pl.CostEstimate(flops=1000, bytes_accessed=1000, transcendentals=0),
        name=name,
        **kw,
    )(*args, *after, *through)
    return got[0] if single else got


def shape(*dims, dtype=BF16):
    return jax.ShapeDtypeStruct(dims, dtype)


def probs_kernel(at_ref, q_ref, k_ref, up_ref, p_ref, dv_ref, bias_ref, s_ref, dv_acc):
    row = lax.broadcasted_iota(jnp.int32, (COUNT, 1), 0)
    start = jnp.zeros((COUNT, 1), jnp.int32)
    end = jnp.int32(0)
    for doc in range(3):
        end = end + at_ref[5 + doc]
        start = jnp.where(row >= end, end, start)
    rows = lax.broadcasted_iota(jnp.int32, (COUNT, COUNT), 0)
    cols = lax.broadcasted_iota(jnp.int32, (COUNT, COUNT), 1)
    bias_ref[...] = jnp.where((cols <= rows) & (cols >= start), 0.0, -1e30).astype(F32)
    dv_acc[...] = jnp.zeros_like(dv_acc)
    for i in range(BLOCKS):
        width = BLOCK * (i + 1)
        at = pl.ds(BLOCK * i, BLOCK)
        qs = jnp.concatenate([q_ref[at, pl.ds(HEAD * h, HEAD)] for h in range(GROUP)], axis=0)
        s_ref[:, :width] = dot(qs, k_ref[:width, :], (1, 1))
        for h in range(GROUP):
            scores = s_ref[pl.ds(BLOCK * h, BLOCK), :width] * (FACTOR * LOG2E) + bias_ref[at, :width]
            expo = jnp.exp2(scores - jnp.max(scores, axis=1, keepdims=True))
            probs = expo * (1.0 / jnp.sum(expo, axis=1, keepdims=True))
            p_ref[h, at, :width] = probs.astype(BF16)
        low = jnp.concatenate([p_ref[h, at, :width] for h in range(GROUP)], axis=0)
        ups = jnp.concatenate([up_ref[at, pl.ds(HEAD * h, HEAD)] for h in range(GROUP)], axis=0)
        dv_acc[:, :width] += dot(ups, low, (0, 0))
    dv_ref[...] = dv_acc[...].T


PROBS_SCRATCH = [pltpu.VMEM((COUNT, COUNT), F32), pltpu.VMEM((GROUP * BLOCK, COUNT), F32), pltpu.VMEM((HEAD, COUNT), F32)]


def first_probs_kernel(
    at_ref, q_hbm, k_hbm, up_hbm, hidden_hbm, p_ref, dv_ref, hidden_out, q_ref, k_ref, up_ref, sems, *scratch
):
    copies = [
        pltpu.make_async_copy(a.at[:, pl.ds(0, b.shape[1])], b, sems.at[j])
        for j, (a, b) in enumerate(((q_hbm, q_ref), (k_hbm, k_ref), (up_hbm, up_ref)))
    ]
    for copy in copies:
        copy.start()
    whole = pltpu.make_async_copy(hidden_hbm, hidden_out, sems.at[3])
    whole.start()
    for copy in copies:
        copy.wait()
    probs_kernel(at_ref, q_ref, k_ref, up_ref, p_ref, dv_ref, *scratch)
    whole.wait()


def probs_part(g, at, queries, keys, upstream, dv, after, hidden=None):
    wide = pl.BlockSpec((COUNT, WIDE), lambda i: (0, g))
    narrow = pl.BlockSpec((COUNT, HEAD), lambda i: (0, g))
    outs = [shape(GROUP, COUNT, COUNT), shape(COUNT, 4 * HEAD, dtype=F32)]
    if hidden is not None:
        blocks = [pltpu.VMEM((COUNT, WIDE), BF16), pltpu.VMEM((COUNT, HEAD), BF16), pltpu.VMEM((COUNT, WIDE), BF16)]
        return call(
            first_probs_kernel, "probs_part", outs + [shape(*hidden.shape)],
            [(SMEM, at), (HBM, queries), (HBM, keys), (HBM, upstream), (HBM, hidden)], after, out_specs=[VMEM, narrow, ANY],
            grid=(1,), scratch_shapes=blocks + [pltpu.SemaphoreType.DMA((4,))] + PROBS_SCRATCH,
        )

    def kernel(*refs):
        probs_kernel(*refs[:4], *refs[5:])

    return call(
        kernel, "probs_part", outs, [(SMEM, at), (wide, queries), (narrow, keys), (wide, upstream), (ANY, dv)], after,
        out_specs=[VMEM, narrow], grid=(1,), scratch_shapes=PROBS_SCRATCH, input_output_aliases={4: 1},
    )


def grads_kernel(g, at_ref, q_ref, k_ref, up_ref, mine_ref, theirs_ref, p_ref, gq_ref, gk_ref, token_ref, dp_ref, ds_ref, dk_acc):
    token_ref[...] = jnp.zeros_like(token_ref)
    dk_acc[...] = jnp.zeros_like(dk_acc)
    col = pl.ds(HEAD * (g % 2), HEAD)
    all_values = jnp.where(at_ref[3] == g // 2, mine_ref[:, col], theirs_ref[:, col])
    for i in range(BLOCKS):
        width = BLOCK * (i + 1)
        at = pl.ds(BLOCK * i, BLOCK)
        ups = jnp.concatenate([up_ref[at, pl.ds(HEAD * h, HEAD)] for h in range(GROUP)], axis=0)
        dp_ref[:, :width] = dot(ups, all_values[:width], (1, 1))
        for h in range(GROUP):
            rows = pl.ds(BLOCK * h, BLOCK)
            dprobs = dp_ref[rows, :width]
            probs = p_ref[h, at, :width].astype(F32)
            delta = jnp.sum(probs * dprobs, axis=1, keepdims=True)
            ds_ref[rows, :width] = (probs * (dprobs - delta)).astype(BF16)
        dscores = ds_ref[:, :width]
        gq = dot(dscores, k_ref[:width, :], (1, 0)) * FACTOR
        for h in range(GROUP):
            gq_ref[at, pl.ds(HEAD * h, HEAD)] = gq[BLOCK * h : BLOCK * (h + 1)].astype(BF16)
        qs = jnp.concatenate([q_ref[at, pl.ds(HEAD * h, HEAD)] for h in range(GROUP)], axis=0)
        dk_acc[:, :width] += dot(qs, dscores, (0, 0))
    gk_ref[...] = (dk_acc[...] * FACTOR).T.astype(BF16)


def grads_part(g, at, queries, keys, upstream, mine, theirs, probs, held, after):
    wide = pl.BlockSpec((COUNT, WIDE), lambda i: (0, g))
    narrow = pl.BlockSpec((COUNT, HEAD), lambda i: (0, g))
    ins = [(SMEM, at), (wide, queries), (narrow, keys), (wide, upstream), (VMEM, mine), (VMEM, theirs), (VMEM, probs)]

    def kernel(*refs):
        grads_kernel(g, *refs[:7], *refs[len(refs) - 6 :])

    extra = {}
    if held is not None:
        ins += [(ANY, held[0]), (ANY, held[1])]
        extra["input_output_aliases"] = {7: 0, 8: 1}
    return call(
        kernel, "grads_part", [shape(*queries.shape), shape(*keys.shape), TOKEN], ins, after,
        out_specs=[wide, narrow, VMEM], grid=(1,),
        scratch_shapes=[pltpu.VMEM((GROUP * BLOCK, COUNT), F32), pltpu.VMEM((GROUP * BLOCK, COUNT), BF16), pltpu.VMEM((HEAD, COUNT), F32)], **extra,
    )


SHARD = 32
CHIP = 2 * SHARD
HALF = 256
DEPTH = 4096


def own_columns(at_ref):
    return pl.ds(pl.multiple_of(at_ref[3] * HALF, HALF), HALF)


def first_join(own_hbm, other_ref, out_ref, sem):
    c = lax.rem(lax.axis_index("dp"), 2)
    cols = pl.ds(pl.multiple_of(c * HALF, HALF), HALF)
    copy = pltpu.make_async_copy(
        own_hbm.at[:, cols], out_ref.at[pl.ds(pl.multiple_of(c * SHARD, SHARD), SHARD), :], sem
    )
    copy.start()
    out_ref[pl.ds(pl.multiple_of((1 - c) * SHARD, SHARD), SHARD), :] = other_ref[:, cols]
    copy.wait()


def join_kernel(own_ref, other_ref, out_ref):
    n = own_ref.shape[0]
    out_ref[:n, :] = own_ref[...]
    out_ref[n:, :] = other_ref[...]


def join_take_kernel(at_ref, own_ref, other_ref, dv_ref, out_ref, dv_out):
    join_kernel(own_ref, other_ref, out_ref)
    dv_out[...] = dv_ref[:, pl.ds(pl.multiple_of((1 - at_ref[3]) * HALF, HALF), HALF)]


def put_in_order(at_ref, pieces, codes_ref):
    z, y, x = at_ref[0], at_ref[1], at_ref[2]
    for k, piece in enumerate(pieces):
        for i in range(16):
            zi, xi = (i & 1) * 4 + (i >> 2 & 1) * 2 + (i >> 3), i >> 1 & 1
            to = ((z ^ zi) * 4 + ((y + 4 - k) & 3)) * 2 + (x ^ xi)
            rows = pl.ds(pl.multiple_of(to * CHIP, CHIP), CHIP)
            codes_ref[rows, :] = piece[pl.ds(i * CHIP, CHIP), :]


NEAR = 640
BESIDES = DEPTH // 2 - NEAR


def raw_kernel(at_ref, own_ref, other_ref, dv_own, dv_other, scale_ref, *refs):
    pieces, (mine_ref, theirs_ref, sums_ref, kept_ref, near_ref, beside_ref, codes_ref) = refs[:4], refs[4:]
    put_in_order(at_ref, pieces, codes_ref)
    cols = own_columns(at_ref)
    scale = scale_ref[:, cols]
    sums = jnp.zeros((1, HALF), F32)
    terms = ((other_ref, dv_other[...], theirs_ref), (own_ref, dv_own[:, cols], mine_ref))
    for hidden_ref, dv, values_ref in terms:
        raw = dot(hidden_ref[...], codes_ref[...], (1, 0))
        values_ref[...] = (raw * scale).astype(BF16)
        sums += jnp.sum(raw * dv, axis=0, keepdims=True)
    sums_ref[...] = sums
    s, half = at_ref[4], DEPTH // 2
    kept_ref[...] = codes_ref[pl.ds(pl.multiple_of(s * half, half), half), :]
    base = (1 - s) * half
    for j in range(2):
        part = pl.ds(j * HALF, HALF)
        near_ref[pl.ds(j * COUNT, COUNT), :] = (dv_own[:, part] * scale_ref[:, part]).astype(BF16)
    near_ref[2 * COUNT :, :] = codes_ref[pl.ds(pl.multiple_of(base, half), NEAR), :]
    beside_ref[...] = codes_ref[pl.ds(pl.multiple_of(base + NEAR, 128), BESIDES), :]


def raw_part(at, hidden, hidden_other, dv, dv_other, scale, pieces):
    outs = [shape(COUNT, HALF), shape(COUNT, HALF), shape(1, HALF, dtype=F32)]
    outs += [shape(DEPTH // 2, HALF), shape(2 * COUNT + NEAR, HALF), shape(BESIDES, HALF)]
    return call(
        raw_kernel, "raw_part", outs,
        [(SMEM, at)] + [(VMEM, a) for a in [hidden, hidden_other, dv, dv_other, scale] + pieces],
        scratch_shapes=[pltpu.VMEM((DEPTH, HALF), BF16)],
    )


def codes_join_kernel(near_ref, beside_ref, out_ref):
    out_ref[:NEAR, :] = near_ref[2 * COUNT :, :]
    out_ref[NEAR:, :] = beside_ref[...]


BATCH = 512


def hidden_terms(c, dv_ref, scale_ref, near_ref, own_codes, seq_codes):
    cols = pl.ds(pl.multiple_of(c * HALF, HALF), HALF)
    own = (dv_ref[:, cols] * scale_ref[:, cols]).astype(BF16)
    far = near_ref[pl.ds(pl.multiple_of(c * COUNT, COUNT), COUNT), :]
    for i in range(0, DEPTH // 2, BATCH):
        rows = pl.ds(i, BATCH)
        yield rows, dot(own, own_codes[rows, :], (1, 1)) + dot(far, seq_codes[rows, :], (1, 1))


def own_terms_kernel(at_ref, dv_ref, scale_ref, near_ref, own_codes, seq_codes, out_ref):
    for rows, total in hidden_terms(at_ref[3], dv_ref, scale_ref, near_ref, own_codes, seq_codes):
        out_ref[:, rows] = total


def far_terms_kernel(at_ref, dv_ref, scale_ref, near_ref, own_codes, seq_codes, part_ref, sums_ref, out_ref, sums_out):
    sums_out[...] = sums_ref[...]
    for rows, total in hidden_terms(1 - at_ref[3], dv_ref, scale_ref, near_ref, own_codes, seq_codes):
        out_ref[:, rows] = (total + part_ref[:, rows]).astype(BF16)


def add_kernel(a_ref, b_ref, out_ref):
    out_ref[...] = a_ref[...] + b_ref[...]


def pairs(move):
    out = []
    for i in range(128):
        z, y, x, c = move(i // 16, i // 4 % 4, i // 2 % 2, i % 2)
        out.append((i, ((z * 4 + y) * 2 + x) * 2 + c))
    return out


def z_swap(bit):
    return pairs(lambda z, y, x, c: (z ^ bit, y, x, c))


def y_shift(k):
    return pairs(lambda z, y, x, c: (z, (y + k) % 4, x, c))


def y_swap(bit):
    return pairs(lambda z, y, x, c: (z, y ^ bit, x, c))


X_SWAP = pairs(lambda z, y, x, c: (z, y, x ^ 1, c))
C_SWAP = pairs(lambda z, y, x, c: (z, y, x, c ^ 1))
SEQ_SWAP = [(0, 1), (1, 0)]
BESIDE = [(2 * a + s, 2 * b + 1 - s) for a, b in X_SWAP for s in range(2)]


def send(x, perm):
    return lax.ppermute(x, "dp", perm)


def shards(hidden, queries, keys, value_codes, value_scale, upstream, lengths):
    me, s = lax.axis_index("dp"), lax.axis_index("seq")
    place = jnp.stack([me // 16, me // 4 % 4, me // 2 % 2, me % 2, s]).astype(jnp.int32)
    at = jnp.concatenate([place, lengths[0, :3]])
    scale = value_scale.reshape(1, -1)

    rows = call(
        first_join, "join", shape(CHIP, HALF), [(HBM, value_codes), (VMEM, send(value_codes, C_SWAP))],
        scratch_shapes=[pltpu.SemaphoreType.DMA],
    )
    probs, dv = [], None
    for step, (perm, heads) in enumerate(((z_swap(4), (0, 1)), (X_SWAP, (2,)), (z_swap(2), (3,)), (z_swap(1), ()))):
        got = send(rows, perm)
        after = ()
        for g in heads:
            if g == 0:
                p, dv, hidden = probs_part(g, at, queries, keys, upstream, dv, (rows,), hidden)
            else:
                p, dv = probs_part(g, at, queries, keys, upstream, dv, (rows,))
            probs.append(p)
            after = (p,)
        n = rows.shape[0]
        ins = [(VMEM, rows), (VMEM, got)]
        if step == 0:
            rows, hidden = call(join_kernel, "join", shape(2 * n, HALF), ins, after, (hidden,))
            hidden_other = send(hidden, C_SWAP)
        elif step == 2:
            rows, dv_half = call(
                join_take_kernel, "join", [shape(2 * n, HALF), shape(COUNT, HALF, dtype=F32)],
                [(SMEM, at)] + ins + [(VMEM, dv)], after,
            )
            dv_other = send(dv_half, C_SWAP)
        elif step == 3:
            rows = call(join_kernel, "join", shape(2 * n, HALF), ins, (hidden_other, dv_other))
        else:
            rows = call(join_kernel, "join", shape(2 * n, HALF), ins, after)
    pieces = [rows] + [send(rows, y_shift(k)) for k in (1, 2, 3)]
    mine, theirs, sums, kept, near, beside = raw_part(at, hidden, hidden_other, dv, dv_other, scale, pieces)

    values_far, kept_far = send(theirs, C_SWAP), send(kept, C_SWAP)
    near = lax.ppermute(near, "seq", SEQ_SWAP)
    beside = lax.ppermute(beside, ("dp", "seq"), BESIDE)
    base = [(SMEM, at), (VMEM, dv), (VMEM, scale)]
    held = None
    for step, perm in enumerate((X_SWAP, y_swap(1), y_swap(2), z_swap(1), z_swap(2), z_swap(4))):
        got = send(sums, perm)
        after = ()
        if 1 <= step <= 4:
            *held, token = grads_part(
                step - 1, at, queries, keys, upstream, mine, values_far, probs[step - 1], held, (sums,)
            )
            after = (token,)
        if step == 4:
            codes = call(codes_join_kernel, "join", shape(DEPTH // 2, HALF), [(VMEM, near), (VMEM, beside)], (sums,))
            codes_far = send(codes, C_SWAP)
        elif step == 5:
            part = call(
                own_terms_kernel, "own_terms", shape(COUNT, DEPTH // 2, dtype=F32),
                base + [(VMEM, near), (VMEM, kept), (VMEM, codes)], (sums,),
            )
            after = (part,)
        sums = call(add_kernel, "add", shape(1, HALF, dtype=F32), [(VMEM, sums), (VMEM, got)], after)
    far = send(sums, C_SWAP)
    grad_hidden, sums = call(
        far_terms_kernel, "far_terms", [shape(COUNT, DEPTH // 2), shape(1, HALF, dtype=F32)],
        base + [(VMEM, a) for a in (near, kept_far, codes_far, part, sums)],
    )
    both = jnp.concatenate([jnp.where(me % 2 == 0, sums, far), jnp.where(me % 2 == 0, far, sums)], axis=1)
    return held[0], held[1], grad_hidden, (both * scale).reshape(-1)


def solution(mesh):
    placed = (
        P("dp", None),
        P("dp", "seq"),
        P("dp", "seq"),
        P("dp", "seq"),
        P("seq"),
        P("dp", "seq"),
        P("dp", None),
    )
    return jax.shard_map(
        shards,
        mesh=mesh,
        in_specs=placed,
        out_specs=(P("dp", "seq"), P("dp", "seq"), P("dp", "seq"), P("seq")),
        check_vma=False,
    )
```

```python
import functools
import math

import jax
import jax.numpy as jnp
from jax import lax
from jax.experimental import pallas as pl
from jax.experimental.pallas import tpu as pltpu
from jax.sharding import PartitionSpec as P

COUNT = 384
HEAD = 128
GROUP = 4
BLOCK = 128
BLOCKS = COUNT // BLOCK
FACTOR = 1.0 / math.sqrt(HEAD)
LOG2E = math.log2(math.e)
BF16 = jnp.bfloat16
F32 = jnp.float32
VMEM_LIMIT = 14 * 1024 * 1024


def dot(a, b, dims):
    return lax.dot_general(a, b, ((dims[:1], dims[1:]), ((), ())), preferred_element_type=F32)

VMEM = pl.BlockSpec(memory_space=pltpu.VMEM)
SMEM = pl.BlockSpec(memory_space=pltpu.SMEM)
ANY = pl.BlockSpec(memory_space=pl.ANY)
HBM = pl.BlockSpec(memory_space=pltpu.HBM)
TOKEN = jax.ShapeDtypeStruct((8, 128), F32)
WIDE = GROUP * HEAD


def call(kernel, name, out_shape, ins, after=(), through=(), **kw):
    specs = [spec for spec, _ in ins]
    args = tuple(pltpu.with_memory_space_constraint(a, pltpu.HBM) if spec is HBM else a for spec, a in ins)
    n_in = len(args) + len(after)
    single = not isinstance(out_shape, (list, tuple))
    outs = [out_shape] if single else list(out_shape)
    kw.setdefault("out_specs", [VMEM] * len(outs))

    n_out = len(outs)
    if through:
        kw["input_output_aliases"] = {n_in + j: n_out + j for j in range(len(through))}
        outs += [jax.ShapeDtypeStruct(a.shape, a.dtype) for a in through]
        kw["out_specs"] = list(kw["out_specs"]) + [ANY] * len(through)
        single = False

    def run(*refs):
        first = n_in + len(through)
        kernel(*refs[: len(args)], *refs[first : first + n_out], *refs[first + n_out + len(through) :])

    got = pl.pallas_call(
        run,
        in_specs=list(specs) + [ANY] * (len(after) + len(through)),
        out_shape=outs,
        compiler_params=pltpu.CompilerParams(vmem_limit_bytes=VMEM_LIMIT),
        cost_estimate=pl.CostEstimate(flops=1000, bytes_accessed=1000, transcendentals=0),
        name=name,
        **kw,
    )(*args, *after, *through)
    return got[0] if single else got


def shape(*dims, dtype=BF16):
    return jax.ShapeDtypeStruct(dims, dtype)


def probs_kernel(at_ref, q_ref, k_ref, up_ref, p_ref, dv_ref, bias_ref, s_ref, dv_acc):
    row = lax.broadcasted_iota(jnp.int32, (COUNT, 1), 0)
    start = jnp.zeros((COUNT, 1), jnp.int32)
    end = jnp.int32(0)
    for doc in range(3):
        end = end + at_ref[5 + doc]
        start = jnp.where(row >= end, end, start)
    rows = lax.broadcasted_iota(jnp.int32, (COUNT, COUNT), 0)
    cols = lax.broadcasted_iota(jnp.int32, (COUNT, COUNT), 1)
    bias_ref[...] = jnp.where((cols <= rows) & (cols >= start), 0.0, -1e30).astype(F32)
    dv_acc[...] = jnp.zeros_like(dv_acc)
    for i in range(BLOCKS):
        width = BLOCK * (i + 1)
        at = pl.ds(BLOCK * i, BLOCK)
        qs = jnp.concatenate([q_ref[at, pl.ds(HEAD * h, HEAD)] for h in range(GROUP)], axis=0)
        s_ref[:, :width] = dot(qs, k_ref[:width, :], (1, 1))
        for h in range(GROUP):
            scores = s_ref[pl.ds(BLOCK * h, BLOCK), :width] * (FACTOR * LOG2E) + bias_ref[at, :width]
            expo = jnp.exp2(scores - jnp.max(scores, axis=1, keepdims=True))
            probs = expo * (1.0 / jnp.sum(expo, axis=1, keepdims=True))
            p_ref[h, at, :width] = probs.astype(BF16)
        low = jnp.concatenate([p_ref[h, at, :width] for h in range(GROUP)], axis=0)
        ups = jnp.concatenate([up_ref[at, pl.ds(HEAD * h, HEAD)] for h in range(GROUP)], axis=0)
        dv_acc[:, :width] += dot(ups, low, (0, 0))
    dv_ref[...] = dv_acc[...].T


PROBS_SCRATCH = [pltpu.VMEM((COUNT, COUNT), F32), pltpu.VMEM((GROUP * BLOCK, COUNT), F32), pltpu.VMEM((HEAD, COUNT), F32)]


def first_probs_kernel(
    at_ref, q_hbm, k_hbm, up_hbm, hidden_hbm, p_ref, dv_ref, hidden_out, q_ref, k_ref, up_ref, sems, *scratch
):
    copies = [
        pltpu.make_async_copy(a.at[:, pl.ds(0, b.shape[1])], b, sems.at[j])
        for j, (a, b) in enumerate(((q_hbm, q_ref), (k_hbm, k_ref), (up_hbm, up_ref)))
    ]
    for copy in copies:
        copy.start()
    whole = pltpu.make_async_copy(hidden_hbm, hidden_out, sems.at[3])
    whole.start()
    for copy in copies:
        copy.wait()
    probs_kernel(at_ref, q_ref, k_ref, up_ref, p_ref, dv_ref, *scratch)
    whole.wait()


def probs_part(g, at, queries, keys, upstream, dv, after, hidden=None):
    wide = pl.BlockSpec((COUNT, WIDE), lambda i: (0, g))
    narrow = pl.BlockSpec((COUNT, HEAD), lambda i: (0, g))
    outs = [shape(GROUP, COUNT, COUNT), shape(COUNT, 4 * HEAD, dtype=F32)]
    if hidden is not None:
        blocks = [pltpu.VMEM((COUNT, WIDE), BF16), pltpu.VMEM((COUNT, HEAD), BF16), pltpu.VMEM((COUNT, WIDE), BF16)]
        return call(
            first_probs_kernel, "probs_part", outs + [shape(*hidden.shape)],
            [(SMEM, at), (HBM, queries), (HBM, keys), (HBM, upstream), (HBM, hidden)], after, out_specs=[VMEM, narrow, ANY],
            grid=(1,), scratch_shapes=blocks + [pltpu.SemaphoreType.DMA((4,))] + PROBS_SCRATCH,
        )

    def kernel(*refs):
        probs_kernel(*refs[:4], *refs[5:])

    return call(
        kernel, "probs_part", outs, [(SMEM, at), (wide, queries), (narrow, keys), (wide, upstream), (ANY, dv)], after,
        out_specs=[VMEM, narrow], grid=(1,), scratch_shapes=PROBS_SCRATCH, input_output_aliases={4: 1},
    )


def grads_kernel(g, at_ref, q_ref, k_ref, up_ref, mine_ref, theirs_ref, p_ref, gq_ref, gk_ref, token_ref, dp_ref, ds_ref, dk_acc):
    token_ref[...] = jnp.zeros_like(token_ref)
    dk_acc[...] = jnp.zeros_like(dk_acc)
    col = pl.ds(HEAD * (g % 2), HEAD)
    all_values = jnp.where(at_ref[3] == g // 2, mine_ref[:, col], theirs_ref[:COUNT, col])
    for i in range(BLOCKS):
        width = BLOCK * (i + 1)
        at = pl.ds(BLOCK * i, BLOCK)
        ups = jnp.concatenate([up_ref[at, pl.ds(HEAD * h, HEAD)] for h in range(GROUP)], axis=0)
        dp_ref[:, :width] = dot(ups, all_values[:width], (1, 1))
        for h in range(GROUP):
            rows = pl.ds(BLOCK * h, BLOCK)
            dprobs = dp_ref[rows, :width]
            probs = p_ref[h, at, :width].astype(F32)
            delta = jnp.sum(probs * dprobs, axis=1, keepdims=True)
            ds_ref[rows, :width] = (probs * (dprobs - delta)).astype(BF16)
        dscores = ds_ref[:, :width]
        gq = dot(dscores, k_ref[:width, :], (1, 0)) * FACTOR
        for h in range(GROUP):
            gq_ref[at, pl.ds(HEAD * h, HEAD)] = gq[BLOCK * h : BLOCK * (h + 1)].astype(BF16)
        qs = jnp.concatenate([q_ref[at, pl.ds(HEAD * h, HEAD)] for h in range(GROUP)], axis=0)
        dk_acc[:, :width] += dot(qs, dscores, (0, 0))
    gk_ref[...] = (dk_acc[...] * FACTOR).T.astype(BF16)


def grads_part(g, at, queries, keys, upstream, mine, theirs, probs, held, after):
    wide = pl.BlockSpec((COUNT, WIDE), lambda i: (0, g))
    narrow = pl.BlockSpec((COUNT, HEAD), lambda i: (0, g))
    ins = [(SMEM, at), (wide, queries), (narrow, keys), (wide, upstream), (VMEM, mine), (VMEM, theirs), (VMEM, probs)]

    def kernel(*refs):
        grads_kernel(g, *refs[:7], *refs[len(refs) - 6 :])

    extra = {}
    if held is not None:
        ins += [(ANY, held[0]), (ANY, held[1])]
        extra["input_output_aliases"] = {7: 0, 8: 1}
    return call(
        kernel, "grads_part", [shape(*queries.shape), shape(*keys.shape), TOKEN], ins, after,
        out_specs=[wide, narrow, VMEM], grid=(1,),
        scratch_shapes=[pltpu.VMEM((GROUP * BLOCK, COUNT), F32), pltpu.VMEM((GROUP * BLOCK, COUNT), BF16), pltpu.VMEM((HEAD, COUNT), F32)], **extra,
    )


SHARD = 32
CHIP = 2 * SHARD
HALF = 256
DEPTH = 4096


def own_columns(at_ref):
    return pl.ds(pl.multiple_of(at_ref[3] * HALF, HALF), HALF)


def first_join(own_hbm, other_ref, out_ref, sem):
    c = lax.rem(lax.axis_index("dp"), 2)
    cols = pl.ds(pl.multiple_of(c * HALF, HALF), HALF)
    copy = pltpu.make_async_copy(
        own_hbm.at[:, cols], out_ref.at[pl.ds(pl.multiple_of(c * SHARD, SHARD), SHARD), :], sem
    )
    copy.start()
    out_ref[pl.ds(pl.multiple_of((1 - c) * SHARD, SHARD), SHARD), :] = other_ref[:, cols]
    copy.wait()


def join_kernel(own_ref, other_ref, out_ref):
    n = own_ref.shape[0]
    out_ref[:n, :] = own_ref[...]
    out_ref[n:, :] = other_ref[...]


def join_split_kernel(at_ref, own_ref, other_ref, dv_ref, first_ref, second_ref, dv_out):
    n = own_ref.shape[0]
    for j, out_ref in enumerate((first_ref, second_ref)):
        out_ref[:n, :] = own_ref[:, HEAD * j : HEAD * (j + 1)]
        out_ref[n:, :] = other_ref[:, HEAD * j : HEAD * (j + 1)]
    dv_out[...] = dv_ref[:, pl.ds(pl.multiple_of((1 - at_ref[3]) * HALF, HALF), HALF)]


def two_joins_kernel(a0, a1, b0, b1, b2, b3, first_ref, second_ref):
    n = a0.shape[0]
    for j, part in enumerate((a0, a1)):
        first_ref[n * j : n * (j + 1), :] = part[...]
    for j, part in enumerate((b0, b1, b2, b3)):
        second_ref[n * j : n * (j + 1), :] = part[...]


def put_in_order(at_ref, pieces, codes_ref):
    z, y, x = at_ref[0], at_ref[1], at_ref[2]

    def place(piece, row, i, k, xi, col):
        zi = (i & 1) * 4 + (i & 2) + (i >> 2)
        to = ((z ^ zi) * 4 + ((y + 4 - k) & 3)) * 2 + (x ^ xi)
        rows = pl.ds(pl.multiple_of(to * CHIP, CHIP), CHIP)
        codes_ref[rows, pl.ds(col, HEAD)] = piece[pl.ds(row, CHIP), :]

    for k in range(4):
        for xi in range(2):
            for i in range(8):
                place(pieces[k], (xi * 8 + i) * CHIP, i, k, xi, 0)
                place(pieces[4 + xi], (k * 8 + i) * CHIP, i, k, xi, HEAD)


NEAR = 640
BESIDES = DEPTH // 2 - NEAR


def raw_kernel(at_ref, own_ref, other_ref, dv_own, dv_other, scale_ref, *refs):
    pieces, (mine_ref, core_ref, sums_ref, near_ref, beside_ref, codes_ref) = refs[:6], refs[6:]
    put_in_order(at_ref, pieces, codes_ref)
    cols = own_columns(at_ref)
    scale = scale_ref[:, cols]
    sums = jnp.zeros((1, HALF), F32)
    terms = ((other_ref, dv_other[...], core_ref), (own_ref, dv_own[:, cols], mine_ref))
    for hidden_ref, dv, values_ref in terms:
        raw = dot(hidden_ref[...], codes_ref[...], (1, 0))
        values_ref[:COUNT, :] = (raw * scale).astype(BF16)
        sums += jnp.sum(raw * dv, axis=0, keepdims=True)
    sums_ref[...] = sums
    s, half = at_ref[4], DEPTH // 2
    core_ref[COUNT:, :] = codes_ref[pl.ds(pl.multiple_of(s * half, half), half), :]
    base = (1 - s) * half
    for j in range(2):
        part = pl.ds(j * HALF, HALF)
        near_ref[pl.ds(j * COUNT, COUNT), :] = (dv_own[:, part] * scale_ref[:, part]).astype(BF16)
    near_ref[2 * COUNT :, :] = codes_ref[pl.ds(pl.multiple_of(base, half), NEAR), :]
    beside_ref[...] = codes_ref[pl.ds(pl.multiple_of(base + NEAR, 128), BESIDES), :]


def raw_part(at, hidden, hidden_other, dv, dv_other, scale, pieces):
    outs = [shape(COUNT, HALF), shape(COUNT + DEPTH // 2, HALF), shape(1, HALF, dtype=F32)]
    outs += [shape(2 * COUNT + NEAR, HALF), shape(BESIDES, HALF)]
    return call(
        raw_kernel, "raw_part", outs,
        [(SMEM, at)] + [(VMEM, a) for a in [hidden, hidden_other, dv, dv_other, scale] + pieces],
        scratch_shapes=[pltpu.VMEM((DEPTH, HALF), BF16)],
    )


def codes_join_kernel(near_ref, beside_ref, out_ref):
    out_ref[:NEAR, :] = near_ref[2 * COUNT :, :]
    out_ref[NEAR:, :] = beside_ref[...]


BATCH = 512


def hidden_terms(c, dv_ref, scale_ref, near_ref, core_codes, seq_codes):
    cols = pl.ds(pl.multiple_of(c * HALF, HALF), HALF)
    own = (dv_ref[:, cols] * scale_ref[:, cols]).astype(BF16)
    far = near_ref[pl.ds(pl.multiple_of(c * COUNT, COUNT), COUNT), :]
    for i in range(0, DEPTH // 2, BATCH):
        total = dot(own, core_codes[COUNT + i : COUNT + i + BATCH, :], (1, 1))
        yield pl.ds(i, BATCH), total + dot(far, seq_codes[i : i + BATCH, :], (1, 1))


def own_terms_kernel(at_ref, dv_ref, scale_ref, near_ref, core_codes, seq_codes, out_ref):
    for rows, total in hidden_terms(at_ref[3], dv_ref, scale_ref, near_ref, core_codes, seq_codes):
        out_ref[:, rows] = total


def far_terms_kernel(at_ref, dv_ref, scale_ref, near_ref, core_codes, seq_codes, part_ref, sums_ref, out_ref, sums_out):
    sums_out[...] = sums_ref[...]
    for rows, total in hidden_terms(1 - at_ref[3], dv_ref, scale_ref, near_ref, core_codes, seq_codes):
        out_ref[:, rows] = (total + part_ref[:, rows]).astype(BF16)


def add_kernel(a_ref, b_ref, out_ref):
    out_ref[...] = a_ref[...] + b_ref[...]


def pairs(move):
    out = []
    for i in range(128):
        z, y, x, c = move(i // 16, i // 4 % 4, i // 2 % 2, i % 2)
        out.append((i, ((z * 4 + y) * 2 + x) * 2 + c))
    return out


def z_swap(bit):
    return pairs(lambda z, y, x, c: (z ^ bit, y, x, c))


def y_shift(k):
    return pairs(lambda z, y, x, c: (z, (y + k) % 4, x, c))


def y_swap(bit):
    return pairs(lambda z, y, x, c: (z, y ^ bit, x, c))


X_SWAP = pairs(lambda z, y, x, c: (z, y, x ^ 1, c))
C_SWAP = pairs(lambda z, y, x, c: (z, y, x, c ^ 1))
SEQ_SWAP = [(0, 1), (1, 0)]
BESIDE = [(2 * a + s, 2 * b + 1 - s) for a, b in X_SWAP for s in range(2)]


def send(x, perm):
    return lax.ppermute(x, "dp", perm)


def shards(hidden, queries, keys, value_codes, value_scale, upstream, lengths):
    me, s = lax.axis_index("dp"), lax.axis_index("seq")
    place = jnp.stack([me // 16, me // 4 % 4, me // 2 % 2, me % 2, s]).astype(jnp.int32)
    at = jnp.concatenate([place, lengths[0, :3]])
    scale = value_scale.reshape(1, -1)

    rows = call(
        first_join, "join", shape(CHIP, HALF), [(HBM, value_codes), (VMEM, send(value_codes, C_SWAP))], (at,),
        scratch_shapes=[pltpu.SemaphoreType.DMA],
    )
    probs, dv = [], None
    for bit, heads in ((4, (0,)), (2, (1, 2)), (1, (3,))):
        got = send(rows, z_swap(bit))
        for g in heads:
            if g == 0:
                p, dv, hidden = probs_part(g, at, queries, keys, upstream, dv, (rows,), hidden)
            else:
                p, dv = probs_part(g, at, queries, keys, upstream, dv, (rows,))
            probs.append(p)
        n = rows.shape[0]
        ins = [(VMEM, rows), (VMEM, got)]
        if bit == 4:
            rows, hidden = call(join_kernel, "join", shape(2 * n, HALF), ins, (p,), (hidden,))
            hidden_other = send(hidden, C_SWAP)
        elif bit == 2:
            rows = call(join_kernel, "join", shape(2 * n, HALF), ins, (p,))
        else:
            first, second, dv_half = call(
                join_split_kernel, "join", [shape(2 * n, HEAD)] * 2 + [shape(COUNT, HALF, dtype=F32)],
                [(SMEM, at)] + ins + [(VMEM, dv)], (hidden_other,),
            )
    first_x = send(first, X_SWAP)
    second_y = [send(second, y_shift(k)) for k in (1, 2, 3)]
    dv_other = send(dv_half, C_SWAP)
    n = first.shape[0]
    first, second = call(
        two_joins_kernel, "join", [shape(2 * n, HEAD), shape(4 * n, HEAD)],
        [(VMEM, a) for a in [first, first_x, second] + second_y], (dv_other,),
    )
    pieces = [first] + [send(first, y_shift(k)) for k in (1, 2, 3)] + [second, send(second, X_SWAP)]
    mine, core, sums, near, beside = raw_part(at, hidden, hidden_other, dv, dv_other, scale, pieces)

    core_far = send(core, C_SWAP)
    base = [(SMEM, at), (VMEM, dv), (VMEM, scale)]
    held = None
    for step, perm in enumerate((X_SWAP, y_swap(1), y_swap(2), z_swap(1), z_swap(2), z_swap(4))):
        got = send(sums, perm)
        ins, after = [(VMEM, sums), (VMEM, got)], ()
        if step == 0:
            sums, near, beside = call(add_kernel, "add", shape(1, HALF, dtype=F32), ins, after, (near, beside))
            near = lax.ppermute(near, "seq", SEQ_SWAP)
            beside = lax.ppermute(beside, ("dp", "seq"), BESIDE)
            continue
        if step <= 4:
            g = step - 1
            *held, token = grads_part(g, at, queries, keys, upstream, mine, core_far, probs[g], held, (sums,))
            after = (token,)
        else:
            codes = call(codes_join_kernel, "join", shape(DEPTH // 2, HALF), [(VMEM, near), (VMEM, beside)], (sums,))
            codes_far = send(codes, C_SWAP)
            part = call(
                own_terms_kernel, "own_terms", shape(COUNT, DEPTH // 2, dtype=F32),
                base + [(VMEM, near), (VMEM, core), (VMEM, codes)], (sums,),
            )
            after = (part,)
        sums = call(add_kernel, "add", shape(1, HALF, dtype=F32), ins, after)
    far = send(sums, C_SWAP)
    grad_hidden, sums = call(
        far_terms_kernel, "far_terms", [shape(COUNT, DEPTH // 2), shape(1, HALF, dtype=F32)],
        base + [(VMEM, a) for a in (near, core_far, codes_far, part, sums)],
    )
    both = jnp.concatenate([jnp.where(me % 2 == 0, sums, far), jnp.where(me % 2 == 0, far, sums)], axis=1)
    return held[0], held[1], grad_hidden, (both * scale).reshape(-1)


def solution(mesh):
    placed = (
        P("dp", None),
        P("dp", "seq"),
        P("dp", "seq"),
        P("dp", "seq"),
        P("seq"),
        P("dp", "seq"),
        P("dp", None),
    )
    return jax.shard_map(
        shards,
        mesh=mesh,
        in_specs=placed,
        out_specs=(P("dp", "seq"), P("dp", "seq"), P("dp", "seq"), P("seq")),
        check_vma=False,
    )
```

```python
import functools
import math

import jax
import jax.numpy as jnp
from jax import lax
from jax.experimental import pallas as pl
from jax.experimental.pallas import tpu as pltpu
from jax.sharding import PartitionSpec as P

COUNT = 384
HEAD = 128
GROUP = 4
BLOCK = 128
BLOCKS = COUNT // BLOCK
FACTOR = 1.0 / math.sqrt(HEAD)
LOG2E = math.log2(math.e)
BF16 = jnp.bfloat16
F32 = jnp.float32
VMEM_LIMIT = 16 * 1024 * 1024


def dot(a, b, dims):
    return lax.dot_general(a, b, ((dims[:1], dims[1:]), ((), ())), preferred_element_type=F32)

VMEM = pl.BlockSpec(memory_space=pltpu.VMEM)
SMEM = pl.BlockSpec(memory_space=pltpu.SMEM)
ANY = pl.BlockSpec(memory_space=pl.ANY)
HBM = pl.BlockSpec(memory_space=pltpu.HBM)
TOKEN = jax.ShapeDtypeStruct((8, 128), F32)
WIDE = GROUP * HEAD


def call(kernel, name, out_shape, ins, after=(), through=(), **kw):
    specs = [spec for spec, _ in ins]
    args = tuple(pltpu.with_memory_space_constraint(a, pltpu.HBM) if spec is HBM else a for spec, a in ins)
    n_in = len(args) + len(after)
    single = not isinstance(out_shape, (list, tuple))
    outs = [out_shape] if single else list(out_shape)
    kw.setdefault("out_specs", [VMEM] * len(outs))

    n_out = len(outs)
    if through:
        kw["input_output_aliases"] = {n_in + j: n_out + j for j in range(len(through))}
        outs += [jax.ShapeDtypeStruct(a.shape, a.dtype) for a in through]
        kw["out_specs"] = list(kw["out_specs"]) + [ANY] * len(through)
        single = False

    def run(*refs):
        first = n_in + len(through)
        kernel(*refs[: len(args)], *refs[first : first + n_out], *refs[first + n_out + len(through) :])

    got = pl.pallas_call(
        run,
        in_specs=list(specs) + [ANY] * (len(after) + len(through)),
        out_shape=outs,
        compiler_params=pltpu.CompilerParams(vmem_limit_bytes=VMEM_LIMIT),
        cost_estimate=pl.CostEstimate(flops=1000, bytes_accessed=1000, transcendentals=0),
        name=name,
        **kw,
    )(*args, *after, *through)
    return got[0] if single else got


def shape(*dims, dtype=BF16):
    return jax.ShapeDtypeStruct(dims, dtype)


def probs_kernel(at_ref, q_ref, k_ref, up_ref, p_ref, dv_ref, bias_ref, s_ref, dv_acc):
    row = lax.broadcasted_iota(jnp.int32, (COUNT, 1), 0)
    start = jnp.zeros((COUNT, 1), jnp.int32)
    end = jnp.int32(0)
    for doc in range(3):
        end = end + at_ref[5 + doc]
        start = jnp.where(row >= end, end, start)
    rows = lax.broadcasted_iota(jnp.int32, (COUNT, COUNT), 0)
    cols = lax.broadcasted_iota(jnp.int32, (COUNT, COUNT), 1)
    bias_ref[...] = jnp.where((cols <= rows) & (cols >= start), 0.0, -1e30).astype(F32)
    dv_acc[...] = jnp.zeros_like(dv_acc)
    for i in range(BLOCKS):
        width = BLOCK * (i + 1)
        at = pl.ds(BLOCK * i, BLOCK)
        qs = jnp.concatenate([q_ref[at, pl.ds(HEAD * h, HEAD)] for h in range(GROUP)], axis=0)
        s_ref[:, :width] = dot(qs, k_ref[:width, :], (1, 1))
        for h in range(GROUP):
            scores = s_ref[pl.ds(BLOCK * h, BLOCK), :width] * (FACTOR * LOG2E) + bias_ref[at, :width]
            expo = jnp.exp2(scores - jnp.max(scores, axis=1, keepdims=True))
            probs = expo * (1.0 / jnp.sum(expo, axis=1, keepdims=True))
            p_ref[h, at, :width] = probs.astype(BF16)
        low = jnp.concatenate([p_ref[h, at, :width] for h in range(GROUP)], axis=0)
        ups = jnp.concatenate([up_ref[at, pl.ds(HEAD * h, HEAD)] for h in range(GROUP)], axis=0)
        dv_acc[:, :width] += dot(ups, low, (0, 0))
    dv_ref[...] = dv_acc[...].T


PROBS_SCRATCH = [pltpu.VMEM((COUNT, COUNT), F32), pltpu.VMEM((GROUP * BLOCK, COUNT), F32), pltpu.VMEM((HEAD, COUNT), F32)]


def first_probs_kernel(
    at_ref, q_hbm, k_hbm, up_hbm, hidden_hbm, p_ref, dv_ref, hidden_out, q_ref, k_ref, up_ref, sems, *scratch
):
    copies = [
        pltpu.make_async_copy(a.at[:, pl.ds(0, b.shape[1])], b, sems.at[j])
        for j, (a, b) in enumerate(((q_hbm, q_ref), (k_hbm, k_ref), (up_hbm, up_ref)))
    ]
    for copy in copies:
        copy.start()
    whole = pltpu.make_async_copy(hidden_hbm, hidden_out, sems.at[3])
    whole.start()
    for copy in copies:
        copy.wait()
    probs_kernel(at_ref, q_ref, k_ref, up_ref, p_ref, dv_ref, *scratch)
    whole.wait()


def probs_part(g, at, queries, keys, upstream, dv, after, hidden=None):
    wide = pl.BlockSpec((COUNT, WIDE), lambda i: (0, g))
    narrow = pl.BlockSpec((COUNT, HEAD), lambda i: (0, g))
    outs = [shape(GROUP, COUNT, COUNT), shape(COUNT, 4 * HEAD, dtype=F32)]
    if hidden is not None:
        blocks = [pltpu.VMEM((COUNT, WIDE), BF16), pltpu.VMEM((COUNT, HEAD), BF16), pltpu.VMEM((COUNT, WIDE), BF16)]
        return call(
            first_probs_kernel, "probs_part", outs + [shape(*hidden.shape)],
            [(SMEM, at), (HBM, queries), (HBM, keys), (HBM, upstream), (HBM, hidden)], after, out_specs=[VMEM, narrow, ANY],
            grid=(1,), scratch_shapes=blocks + [pltpu.SemaphoreType.DMA((4,))] + PROBS_SCRATCH,
        )

    def kernel(*refs):
        probs_kernel(*refs[:4], *refs[5:])

    return call(
        kernel, "probs_part", outs, [(SMEM, at), (wide, queries), (narrow, keys), (wide, upstream), (ANY, dv)], after,
        out_specs=[VMEM, narrow], grid=(1,), scratch_shapes=PROBS_SCRATCH, input_output_aliases={4: 1},
    )


def grads_kernel(g, at_ref, q_ref, k_ref, up_ref, mine_ref, theirs_ref, p_ref, gq_ref, gk_ref, token_ref, dp_ref, ds_ref, dk_acc):
    token_ref[...] = jnp.zeros_like(token_ref)
    dk_acc[...] = jnp.zeros_like(dk_acc)
    col = pl.ds(HEAD * (g % 2), HEAD)
    all_values = jnp.where(at_ref[3] == g // 2, mine_ref[:, col], theirs_ref[:, col])
    for i in range(BLOCKS):
        width = BLOCK * (i + 1)
        at = pl.ds(BLOCK * i, BLOCK)
        ups = jnp.concatenate([up_ref[at, pl.ds(HEAD * h, HEAD)] for h in range(GROUP)], axis=0)
        dp_ref[:, :width] = dot(ups, all_values[:width], (1, 1))
        for h in range(GROUP):
            rows = pl.ds(BLOCK * h, BLOCK)
            dprobs = dp_ref[rows, :width]
            probs = p_ref[h, at, :width].astype(F32)
            delta = jnp.sum(probs * dprobs, axis=1, keepdims=True)
            ds_ref[rows, :width] = (probs * (dprobs - delta)).astype(BF16)
        dscores = ds_ref[:, :width]
        gq = dot(dscores, k_ref[:width, :], (1, 0)) * FACTOR
        for h in range(GROUP):
            gq_ref[at, pl.ds(HEAD * h, HEAD)] = gq[BLOCK * h : BLOCK * (h + 1)].astype(BF16)
        qs = jnp.concatenate([q_ref[at, pl.ds(HEAD * h, HEAD)] for h in range(GROUP)], axis=0)
        dk_acc[:, :width] += dot(qs, dscores, (0, 0))
    gk_ref[...] = (dk_acc[...] * FACTOR).T.astype(BF16)


def grads_part(g, at, queries, keys, upstream, mine, theirs, probs, held, after):
    wide = pl.BlockSpec((COUNT, WIDE), lambda i: (0, g))
    narrow = pl.BlockSpec((COUNT, HEAD), lambda i: (0, g))
    ins = [(SMEM, at), (wide, queries), (narrow, keys), (wide, upstream), (VMEM, mine), (VMEM, theirs), (VMEM, probs)]

    def kernel(*refs):
        grads_kernel(g, *refs[:7], *refs[len(refs) - 6 :])

    extra = {}
    if held is not None:
        ins += [(ANY, held[0]), (ANY, held[1])]
        extra["input_output_aliases"] = {7: 0, 8: 1}
    return call(
        kernel, "grads_part", [shape(*queries.shape), shape(*keys.shape), TOKEN], ins, after,
        out_specs=[wide, narrow, VMEM], grid=(1,),
        scratch_shapes=[pltpu.VMEM((GROUP * BLOCK, COUNT), F32), pltpu.VMEM((GROUP * BLOCK, COUNT), BF16), pltpu.VMEM((HEAD, COUNT), F32)], **extra,
    )


SHARD = 32
CHIP = 2 * SHARD
HALF = 256
DEPTH = 4096


def own_columns(at_ref):
    return pl.ds(pl.multiple_of(at_ref[3] * HALF, HALF), HALF)


def first_join(own_hbm, other_ref, out_ref, sem):
    c = lax.rem(lax.axis_index("dp"), 2)
    cols = pl.ds(pl.multiple_of(c * HALF, HALF), HALF)
    copy = pltpu.make_async_copy(
        own_hbm.at[:, cols], out_ref.at[pl.ds(pl.multiple_of(c * SHARD, SHARD), SHARD), :], sem
    )
    copy.start()
    out_ref[pl.ds(pl.multiple_of((1 - c) * SHARD, SHARD), SHARD), :] = other_ref[:, cols]
    copy.wait()


def join_kernel(own_ref, other_ref, out_ref):
    n = own_ref.shape[0]
    out_ref[:n, :] = own_ref[...]
    out_ref[n:, :] = other_ref[...]


def join_split_kernel(at_ref, own_ref, other_ref, dv_ref, first_ref, second_ref, dv_out):
    n = own_ref.shape[0]
    for j, out_ref in enumerate((first_ref, second_ref)):
        out_ref[:n, :] = own_ref[:, HEAD * j : HEAD * (j + 1)]
        out_ref[n:, :] = other_ref[:, HEAD * j : HEAD * (j + 1)]
    dv_out[...] = dv_ref[:, pl.ds(pl.multiple_of((1 - at_ref[3]) * HALF, HALF), HALF)]


def two_joins_kernel(a0, a1, b0, b1, b2, b3, first_ref, second_ref):
    n = a0.shape[0]
    for j, part in enumerate((a0, a1)):
        first_ref[n * j : n * (j + 1), :] = part[...]
    for j, part in enumerate((b0, b1, b2, b3)):
        second_ref[n * j : n * (j + 1), :] = part[...]


def put_in_order(at_ref, pieces, codes_ref):
    z, y, x = at_ref[0], at_ref[1], at_ref[2]

    def place(piece, row, i, k, xi, col):
        zi = (i & 1) * 4 + (i & 2) + (i >> 2)
        to = ((z ^ zi) * 4 + ((y + 4 - k) & 3)) * 2 + (x ^ xi)
        rows = pl.ds(pl.multiple_of(to * CHIP, CHIP), CHIP)
        codes_ref[rows, pl.ds(col, HEAD)] = piece[pl.ds(row, CHIP), :]

    for k in range(4):
        for xi in range(2):
            for i in range(8):
                place(pieces[k], (xi * 8 + i) * CHIP, i, k, xi, 0)
                place(pieces[4 + xi], (k * 8 + i) * CHIP, i, k, xi, HEAD)


NEAR = 640
BESIDES = DEPTH // 2 - NEAR


def raw_kernel(at_ref, own_ref, other_ref, dv_own, dv_other, scale_ref, *refs):
    pieces, (mine_ref, theirs_ref, sums_ref, kept_ref, near_ref, beside_ref, codes_ref) = refs[:6], refs[6:]
    put_in_order(at_ref, pieces, codes_ref)
    cols = own_columns(at_ref)
    scale = scale_ref[:, cols]
    sums = jnp.zeros((1, HALF), F32)
    terms = ((other_ref, dv_other[...], theirs_ref), (own_ref, dv_own[:, cols], mine_ref))
    for hidden_ref, dv, values_ref in terms:
        raw = dot(hidden_ref[...], codes_ref[...], (1, 0))
        values_ref[...] = (raw * scale).astype(BF16)
        sums += jnp.sum(raw * dv, axis=0, keepdims=True)
    sums_ref[...] = sums
    s, half = at_ref[4], DEPTH // 2
    kept_ref[...] = codes_ref[pl.ds(pl.multiple_of(s * half, half), half), :]
    base = (1 - s) * half
    for j in range(2):
        part = pl.ds(j * HALF, HALF)
        near_ref[pl.ds(j * COUNT, COUNT), :] = (dv_own[:, part] * scale_ref[:, part]).astype(BF16)
    near_ref[2 * COUNT :, :] = codes_ref[pl.ds(pl.multiple_of(base, half), NEAR), :]
    beside_ref[...] = codes_ref[pl.ds(pl.multiple_of(base + NEAR, 128), BESIDES), :]


def raw_part(at, hidden, hidden_other, dv, dv_other, scale, pieces):
    outs = [shape(COUNT, HALF), shape(COUNT, HALF), shape(1, HALF, dtype=F32)]
    outs += [shape(DEPTH // 2, HALF), shape(2 * COUNT + NEAR, HALF), shape(BESIDES, HALF)]
    return call(
        raw_kernel, "raw_part", outs,
        [(SMEM, at)] + [(VMEM, a) for a in [hidden, hidden_other, dv, dv_other, scale] + pieces],
        scratch_shapes=[pltpu.VMEM((DEPTH, HALF), BF16)],
    )


BATCH = 512


def hidden_kernel(
    at_ref, dv_ref, scale_ref, near_ref, beside_ref, kept_ref, near_far, beside_far, kept_far, out_ref, token_ref
):
    token_ref[...] = jnp.zeros_like(token_ref)
    sides = []
    for other, near, beside, kept in ((0, near_ref, beside_ref, kept_ref), (1, near_far, beside_far, kept_far)):
        c = at_ref[3] ^ other
        cols = pl.ds(pl.multiple_of(c * HALF, HALF), HALF)
        own = (dv_ref[:, cols] * scale_ref[:, cols]).astype(BF16)
        seq = near_ref[pl.ds(pl.multiple_of(c * COUNT, COUNT), COUNT), :]
        sides.append((own, seq, near, beside, kept))
    at = 0
    while at < DEPTH // 2:
        end = min(at + BATCH, NEAR if at < NEAR else DEPTH // 2)
        total = 0.0
        for own, seq, near, beside, kept in sides:
            total += dot(own, kept[at:end, :], (1, 1))
            codes = near[2 * COUNT + at : 2 * COUNT + end, :] if at < NEAR else beside[at - NEAR : end - NEAR, :]
            total += dot(seq, codes, (1, 1))
        out_ref[:, at:end] = total.astype(BF16)
        at = end


def add_kernel(a_ref, b_ref, out_ref):
    out_ref[...] = a_ref[...] + b_ref[...]


def pairs(move):
    out = []
    for i in range(128):
        z, y, x, c = move(i // 16, i // 4 % 4, i // 2 % 2, i % 2)
        out.append((i, ((z * 4 + y) * 2 + x) * 2 + c))
    return out


def z_swap(bit):
    return pairs(lambda z, y, x, c: (z ^ bit, y, x, c))


def y_shift(k):
    return pairs(lambda z, y, x, c: (z, (y + k) % 4, x, c))


def y_swap(bit):
    return pairs(lambda z, y, x, c: (z, y ^ bit, x, c))


X_SWAP = pairs(lambda z, y, x, c: (z, y, x ^ 1, c))
C_SWAP = pairs(lambda z, y, x, c: (z, y, x, c ^ 1))
SEQ_SWAP = [(0, 1), (1, 0)]
BESIDE = [(2 * a + s, 2 * b + 1 - s) for a, b in X_SWAP for s in range(2)]


def send(x, perm):
    return lax.ppermute(x, "dp", perm)


def shards(hidden, queries, keys, value_codes, value_scale, upstream, lengths):
    me, s = lax.axis_index("dp"), lax.axis_index("seq")
    place = jnp.stack([me // 16, me // 4 % 4, me // 2 % 2, me % 2, s]).astype(jnp.int32)
    at = jnp.concatenate([place, lengths[0, :3]])
    scale = value_scale.reshape(1, -1)

    rows = call(
        first_join, "join", shape(CHIP, HALF), [(HBM, value_codes), (VMEM, send(value_codes, C_SWAP))], (at,),
        scratch_shapes=[pltpu.SemaphoreType.DMA],
    )
    probs, dv = [], None
    for bit, heads in ((4, (0,)), (2, (1, 2)), (1, (3,))):
        got = send(rows, z_swap(bit))
        for g in heads:
            if g == 0:
                p, dv, hidden = probs_part(g, at, queries, keys, upstream, dv, (rows,), hidden)
            else:
                p, dv = probs_part(g, at, queries, keys, upstream, dv, (rows,))
            probs.append(p)
        n = rows.shape[0]
        ins = [(VMEM, rows), (VMEM, got)]
        if bit == 4:
            rows, hidden = call(join_kernel, "join", shape(2 * n, HALF), ins, (p,), (hidden,))
            hidden_other = send(hidden, C_SWAP)
        elif bit == 2:
            rows = call(join_kernel, "join", shape(2 * n, HALF), ins, (p,))
        else:
            first, second, dv_half = call(
                join_split_kernel, "join", [shape(2 * n, HEAD)] * 2 + [shape(COUNT, HALF, dtype=F32)],
                [(SMEM, at)] + ins + [(VMEM, dv)], (hidden_other,),
            )
    first_x = send(first, X_SWAP)
    second_y = [send(second, y_shift(k)) for k in (1, 2, 3)]
    dv_other = send(dv_half, C_SWAP)
    n = first.shape[0]
    first, second = call(
        two_joins_kernel, "join", [shape(2 * n, HEAD), shape(4 * n, HEAD)],
        [(VMEM, a) for a in [first, first_x, second] + second_y], (dv_other,),
    )
    pieces = [first] + [send(first, y_shift(k)) for k in (1, 2, 3)] + [second, send(second, X_SWAP)]
    mine, theirs, sums, kept, near, beside = raw_part(at, hidden, hidden_other, dv, dv_other, scale, pieces)

    values_far = send(theirs, C_SWAP)
    near = lax.ppermute(near, "seq", SEQ_SWAP)
    beside = lax.ppermute(beside, ("dp", "seq"), BESIDE)
    held = None
    for step, perm in enumerate((y_swap(1), y_swap(2), z_swap(1), z_swap(2), z_swap(4), X_SWAP)):
        got = send(sums, perm)
        after, through = (), ()
        if step < 4:
            *held, token = grads_part(
                step, at, queries, keys, upstream, mine, values_far, probs[step], held, (sums,)
            )
            after = (token,)
            if step == 3:
                through = (near, beside, kept)
        elif step == 5:
            grad_hidden, token = call(
                hidden_kernel, "hidden_part", [shape(COUNT, DEPTH // 2), TOKEN],
                [(SMEM, at)] + [(VMEM, a) for a in [dv, scale, near, beside, kept] + far], (sums,),
            )
            after = (token,)
        ins = [(VMEM, sums), (VMEM, got)]
        if through:
            sums, near, beside, kept = call(add_kernel, "add", shape(1, HALF, dtype=F32), ins, after, through)
            far = [send(a, C_SWAP) for a in (near, beside, kept)]
        else:
            sums = call(add_kernel, "add", shape(1, HALF, dtype=F32), ins, after)
    far = send(sums, C_SWAP)
    both = jnp.concatenate([jnp.where(me % 2 == 0, sums, far), jnp.where(me % 2 == 0, far, sums)], axis=1)
    return held[0], held[1], grad_hidden, (both * scale).reshape(-1)


def solution(mesh):
    placed = (
        P("dp", None),
        P("dp", "seq"),
        P("dp", "seq"),
        P("dp", "seq"),
        P("seq"),
        P("dp", "seq"),
        P("dp", None),
    )
    return jax.shard_map(
        shards,
        mesh=mesh,
        in_specs=placed,
        out_specs=(P("dp", "seq"), P("dp", "seq"), P("dp", "seq"), P("seq")),
        check_vma=False,
    )
```

```python
import functools
import math

import jax
import jax.numpy as jnp
from jax import lax
from jax.experimental import pallas as pl
from jax.experimental.pallas import tpu as pltpu
from jax.sharding import PartitionSpec as P

COUNT = 384
HEAD = 128
GROUP = 4
BLOCK = 128
BLOCKS = COUNT // BLOCK
FACTOR = 1.0 / math.sqrt(HEAD)
LOG2E = math.log2(math.e)
BF16 = jnp.bfloat16
F32 = jnp.float32
VMEM_LIMIT = 16 * 1024 * 1024


def dot(a, b, dims):
    return lax.dot_general(a, b, ((dims[:1], dims[1:]), ((), ())), preferred_element_type=F32)

VMEM = pl.BlockSpec(memory_space=pltpu.VMEM)
SMEM = pl.BlockSpec(memory_space=pltpu.SMEM)
ANY = pl.BlockSpec(memory_space=pl.ANY)
HBM = pl.BlockSpec(memory_space=pltpu.HBM)
TOKEN = jax.ShapeDtypeStruct((8, 128), F32)
WIDE = GROUP * HEAD


def call(kernel, name, out_shape, ins, after=(), through=(), **kw):
    specs = [spec for spec, _ in ins]
    args = tuple(pltpu.with_memory_space_constraint(a, pltpu.HBM) if spec is HBM else a for spec, a in ins)
    n_in = len(args) + len(after)
    single = not isinstance(out_shape, (list, tuple))
    outs = [out_shape] if single else list(out_shape)
    kw.setdefault("out_specs", [VMEM] * len(outs))

    n_out = len(outs)
    if through:
        kw["input_output_aliases"] = {n_in + j: n_out + j for j in range(len(through))}
        outs += [jax.ShapeDtypeStruct(a.shape, a.dtype) for a in through]
        kw["out_specs"] = list(kw["out_specs"]) + [ANY] * len(through)
        single = False

    def run(*refs):
        first = n_in + len(through)
        kernel(*refs[: len(args)], *refs[first : first + n_out], *refs[first + n_out + len(through) :])

    got = pl.pallas_call(
        run,
        in_specs=list(specs) + [ANY] * (len(after) + len(through)),
        out_shape=outs,
        compiler_params=pltpu.CompilerParams(vmem_limit_bytes=VMEM_LIMIT),
        cost_estimate=pl.CostEstimate(flops=1000, bytes_accessed=1000, transcendentals=0),
        name=name,
        **kw,
    )(*args, *after, *through)
    return got[0] if single else got


def shape(*dims, dtype=BF16):
    return jax.ShapeDtypeStruct(dims, dtype)


def probs_kernel(at_ref, q_ref, k_ref, up_ref, p_ref, dv_ref, bias_ref, s_ref, dv_acc):
    row = lax.broadcasted_iota(jnp.int32, (COUNT, 1), 0)
    start = jnp.zeros((COUNT, 1), jnp.int32)
    end = jnp.int32(0)
    for doc in range(3):
        end = end + at_ref[5 + doc]
        start = jnp.where(row >= end, end, start)
    rows = lax.broadcasted_iota(jnp.int32, (COUNT, COUNT), 0)
    cols = lax.broadcasted_iota(jnp.int32, (COUNT, COUNT), 1)
    bias_ref[...] = jnp.where((cols <= rows) & (cols >= start), 0.0, -1e30).astype(F32)
    dv_acc[...] = jnp.zeros_like(dv_acc)
    for i in range(BLOCKS):
        width = BLOCK * (i + 1)
        at = pl.ds(BLOCK * i, BLOCK)
        qs = jnp.concatenate([q_ref[at, pl.ds(HEAD * h, HEAD)] for h in range(GROUP)], axis=0)
        s_ref[:, :width] = dot(qs, k_ref[:width, :], (1, 1))
        for h in range(GROUP):
            scores = s_ref[pl.ds(BLOCK * h, BLOCK), :width] * (FACTOR * LOG2E) + bias_ref[at, :width]
            expo = jnp.exp2(scores - jnp.max(scores, axis=1, keepdims=True))
            probs = expo * (1.0 / jnp.sum(expo, axis=1, keepdims=True))
            p_ref[h, at, :width] = probs.astype(BF16)
        low = jnp.concatenate([p_ref[h, at, :width] for h in range(GROUP)], axis=0)
        ups = jnp.concatenate([up_ref[at, pl.ds(HEAD * h, HEAD)] for h in range(GROUP)], axis=0)
        dv_acc[:, :width] += dot(ups, low, (0, 0))
    dv_ref[...] = dv_acc[...].T


PROBS_SCRATCH = [pltpu.VMEM((COUNT, COUNT), F32), pltpu.VMEM((GROUP * BLOCK, COUNT), F32), pltpu.VMEM((HEAD, COUNT), F32)]


def first_probs_kernel(
    at_ref, q_hbm, k_hbm, up_hbm, hidden_hbm, p_ref, dv_ref, hidden_out, q_ref, k_ref, up_ref, sems, *scratch
):
    copies = [
        pltpu.make_async_copy(a.at[:, pl.ds(0, b.shape[1])], b, sems.at[j])
        for j, (a, b) in enumerate(((q_hbm, q_ref), (k_hbm, k_ref), (up_hbm, up_ref)))
    ]
    for copy in copies:
        copy.start()
    whole = pltpu.make_async_copy(hidden_hbm, hidden_out, sems.at[3])
    whole.start()
    for copy in copies:
        copy.wait()
    probs_kernel(at_ref, q_ref, k_ref, up_ref, p_ref, dv_ref, *scratch)
    whole.wait()


def probs_part(g, at, queries, keys, upstream, dv, after, hidden=None):
    wide = pl.BlockSpec((COUNT, WIDE), lambda i: (0, g))
    narrow = pl.BlockSpec((COUNT, HEAD), lambda i: (0, g))
    outs = [shape(GROUP, COUNT, COUNT), shape(COUNT, 4 * HEAD, dtype=F32)]
    if hidden is not None:
        blocks = [pltpu.VMEM((COUNT, WIDE), BF16), pltpu.VMEM((COUNT, HEAD), BF16), pltpu.VMEM((COUNT, WIDE), BF16)]
        return call(
            first_probs_kernel, "probs_part", outs + [shape(*hidden.shape)],
            [(SMEM, at), (HBM, queries), (HBM, keys), (HBM, upstream), (HBM, hidden)], after, out_specs=[VMEM, narrow, ANY],
            grid=(1,), scratch_shapes=blocks + [pltpu.SemaphoreType.DMA((4,))] + PROBS_SCRATCH,
        )

    def kernel(*refs):
        probs_kernel(*refs[:4], *refs[5:])

    return call(
        kernel, "probs_part", outs, [(SMEM, at), (wide, queries), (narrow, keys), (wide, upstream), (ANY, dv)], after,
        out_specs=[VMEM, narrow], grid=(1,), scratch_shapes=PROBS_SCRATCH, input_output_aliases={4: 1},
    )


def grads_kernel(g, at_ref, q_ref, k_ref, up_ref, mine_ref, theirs_ref, p_ref, gq_ref, gk_ref, token_ref, dp_ref, ds_ref, dk_acc):
    token_ref[...] = jnp.zeros_like(token_ref)
    dk_acc[...] = jnp.zeros_like(dk_acc)
    col = pl.ds(HEAD * (g % 2), HEAD)
    all_values = jnp.where(at_ref[3] == g // 2, mine_ref[:, col], theirs_ref[:, col])
    for i in range(BLOCKS):
        width = BLOCK * (i + 1)
        at = pl.ds(BLOCK * i, BLOCK)
        ups = jnp.concatenate([up_ref[at, pl.ds(HEAD * h, HEAD)] for h in range(GROUP)], axis=0)
        dp_ref[:, :width] = dot(ups, all_values[:width], (1, 1))
        for h in range(GROUP):
            rows = pl.ds(BLOCK * h, BLOCK)
            dprobs = dp_ref[rows, :width]
            probs = p_ref[h, at, :width].astype(F32)
            delta = jnp.sum(probs * dprobs, axis=1, keepdims=True)
            ds_ref[rows, :width] = (probs * (dprobs - delta)).astype(BF16)
        dscores = ds_ref[:, :width]
        gq = dot(dscores, k_ref[:width, :], (1, 0)) * FACTOR
        for h in range(GROUP):
            gq_ref[at, pl.ds(HEAD * h, HEAD)] = gq[BLOCK * h : BLOCK * (h + 1)].astype(BF16)
        qs = jnp.concatenate([q_ref[at, pl.ds(HEAD * h, HEAD)] for h in range(GROUP)], axis=0)
        dk_acc[:, :width] += dot(qs, dscores, (0, 0))
    gk_ref[...] = (dk_acc[...] * FACTOR).T.astype(BF16)


def grads_part(g, at, queries, keys, upstream, mine, theirs, probs, held, after):
    wide = pl.BlockSpec((COUNT, WIDE), lambda i: (0, g))
    narrow = pl.BlockSpec((COUNT, HEAD), lambda i: (0, g))
    ins = [(SMEM, at), (wide, queries), (narrow, keys), (wide, upstream), (VMEM, mine), (VMEM, theirs), (VMEM, probs)]

    def kernel(*refs):
        grads_kernel(g, *refs[:7], *refs[len(refs) - 6 :])

    extra = {}
    if held is not None:
        ins += [(ANY, held[0]), (ANY, held[1])]
        extra["input_output_aliases"] = {7: 0, 8: 1}
    return call(
        kernel, "grads_part", [shape(*queries.shape), shape(*keys.shape), TOKEN], ins, after,
        out_specs=[wide, narrow, VMEM], grid=(1,),
        scratch_shapes=[pltpu.VMEM((GROUP * BLOCK, COUNT), F32), pltpu.VMEM((GROUP * BLOCK, COUNT), BF16), pltpu.VMEM((HEAD, COUNT), F32)], **extra,
    )


SHARD = 32
CHIP = 2 * SHARD
HALF = 256
DEPTH = 4096


def own_columns(at_ref):
    return pl.ds(pl.multiple_of(at_ref[3] * HALF, HALF), HALF)


def first_join(own_hbm, other_ref, out_ref, sem):
    c = lax.rem(lax.axis_index("dp"), 2)
    cols = pl.ds(pl.multiple_of(c * HALF, HALF), HALF)
    copy = pltpu.make_async_copy(
        own_hbm.at[:, cols], out_ref.at[pl.ds(pl.multiple_of(c * SHARD, SHARD), SHARD), :], sem
    )
    copy.start()
    out_ref[pl.ds(pl.multiple_of((1 - c) * SHARD, SHARD), SHARD), :] = other_ref[:, cols]
    copy.wait()


def join_kernel(own_ref, other_ref, out_ref):
    n = own_ref.shape[0]
    out_ref[:n, :] = own_ref[...]
    out_ref[n:, :] = other_ref[...]


def join_split_kernel(own_ref, other_ref, first_ref, second_ref):
    n = own_ref.shape[0]
    for j, out_ref in enumerate((first_ref, second_ref)):
        out_ref[:n, :] = own_ref[:, HEAD * j : HEAD * (j + 1)]
        out_ref[n:, :] = other_ref[:, HEAD * j : HEAD * (j + 1)]


def two_joins_kernel(at_ref, dv_ref, a0, a1, b0, b1, b2, b3, first_ref, second_ref, dv_out):
    dv_out[...] = dv_ref[:, pl.ds(pl.multiple_of((1 - at_ref[3]) * HALF, HALF), HALF)]
    n = a0.shape[0]
    for j, part in enumerate((a0, a1)):
        first_ref[n * j : n * (j + 1), :] = part[...]
    for j, part in enumerate((b0, b1, b2, b3)):
        second_ref[n * j : n * (j + 1), :] = part[...]


def put_in_order(at_ref, pieces, codes_ref):
    z, y, x = at_ref[0], at_ref[1], at_ref[2]

    def place(piece, row, i, k, xi, col):
        zi = (i & 1) * 4 + (i & 2) + (i >> 2)
        to = ((z ^ zi) * 4 + ((y + 4 - k) & 3)) * 2 + (x ^ xi)
        rows = pl.ds(pl.multiple_of(to * CHIP, CHIP), CHIP)
        codes_ref[rows, pl.ds(col, HEAD)] = piece[pl.ds(row, CHIP), :]

    for k in range(4):
        for xi in range(2):
            for i in range(8):
                place(pieces[k], (xi * 8 + i) * CHIP, i, k, xi, 0)
                place(pieces[4 + xi], (k * 8 + i) * CHIP, i, k, xi, HEAD)


NEAR = 640
BESIDES = DEPTH // 2 - NEAR


def raw_kernel(at_ref, own_ref, other_ref, dv_own, dv_other, scale_ref, *refs):
    pieces, (mine_ref, theirs_ref, sums_ref, kept_ref, near_ref, beside_ref, codes_ref) = refs[:6], refs[6:]
    put_in_order(at_ref, pieces, codes_ref)
    cols = own_columns(at_ref)
    scale = scale_ref[:, cols]
    sums = jnp.zeros((1, HALF), F32)
    terms = ((other_ref, dv_other[...], theirs_ref), (own_ref, dv_own[:, cols], mine_ref))
    for hidden_ref, dv, values_ref in terms:
        raw = dot(hidden_ref[...], codes_ref[...], (1, 0))
        values_ref[...] = (raw * scale).astype(BF16)
        sums += jnp.sum(raw * dv, axis=0, keepdims=True)
    sums_ref[...] = sums
    s, half = at_ref[4], DEPTH // 2
    kept_ref[...] = codes_ref[pl.ds(pl.multiple_of(s * half, half), half), :]
    base = (1 - s) * half
    for j in range(2):
        part = pl.ds(j * HALF, HALF)
        near_ref[pl.ds(j * COUNT, COUNT), :] = (dv_own[:, part] * scale_ref[:, part]).astype(BF16)
    near_ref[2 * COUNT :, :] = codes_ref[pl.ds(pl.multiple_of(base, half), NEAR), :]
    beside_ref[...] = codes_ref[pl.ds(pl.multiple_of(base + NEAR, 128), BESIDES), :]


def raw_part(at, hidden, hidden_other, dv, dv_other, scale, pieces):
    outs = [shape(COUNT, HALF), shape(COUNT, HALF), shape(1, HALF, dtype=F32)]
    outs += [shape(DEPTH // 2, HALF), shape(2 * COUNT + NEAR, HALF), shape(BESIDES, HALF)]
    return call(
        raw_kernel, "raw_part", outs,
        [(SMEM, at)] + [(VMEM, a) for a in [hidden, hidden_other, dv, dv_other, scale] + pieces],
        scratch_shapes=[pltpu.VMEM((DEPTH, HALF), BF16)],
    )


BATCH = 512


def hidden_kernel(
    at_ref, dv_ref, scale_ref, near_ref, beside_ref, kept_ref, near_far, beside_far, kept_far, out_ref, token_ref
):
    token_ref[...] = jnp.zeros_like(token_ref)
    sides = []
    for other, near, beside, kept in ((0, near_ref, beside_ref, kept_ref), (1, near_far, beside_far, kept_far)):
        c = at_ref[3] ^ other
        cols = pl.ds(pl.multiple_of(c * HALF, HALF), HALF)
        own = (dv_ref[:, cols] * scale_ref[:, cols]).astype(BF16)
        seq = near_ref[pl.ds(pl.multiple_of(c * COUNT, COUNT), COUNT), :]
        sides.append((own, seq, near, beside, kept))
    at = 0
    while at < DEPTH // 2:
        end = min(at + BATCH, NEAR if at < NEAR else DEPTH // 2)
        total = 0.0
        for own, seq, near, beside, kept in sides:
            total += dot(own, kept[at:end, :], (1, 1))
            codes = near[2 * COUNT + at : 2 * COUNT + end, :] if at < NEAR else beside[at - NEAR : end - NEAR, :]
            total += dot(seq, codes, (1, 1))
        out_ref[:, at:end] = total.astype(BF16)
        at = end


def add_kernel(a_ref, b_ref, out_ref):
    out_ref[...] = a_ref[...] + b_ref[...]


def pairs(move):
    out = []
    for i in range(128):
        z, y, x, c = move(i // 16, i // 4 % 4, i // 2 % 2, i % 2)
        out.append((i, ((z * 4 + y) * 2 + x) * 2 + c))
    return out


def z_swap(bit):
    return pairs(lambda z, y, x, c: (z ^ bit, y, x, c))


def y_shift(k):
    return pairs(lambda z, y, x, c: (z, (y + k) % 4, x, c))


def y_swap(bit):
    return pairs(lambda z, y, x, c: (z, y ^ bit, x, c))


X_SWAP = pairs(lambda z, y, x, c: (z, y, x ^ 1, c))
C_SWAP = pairs(lambda z, y, x, c: (z, y, x, c ^ 1))
SEQ_SWAP = [(0, 1), (1, 0)]
BESIDE = [(2 * a + s, 2 * b + 1 - s) for a, b in X_SWAP for s in range(2)]


def send(x, perm):
    return lax.ppermute(x, "dp", perm)


def shards(hidden, queries, keys, value_codes, value_scale, upstream, lengths):
    me, s = lax.axis_index("dp"), lax.axis_index("seq")
    place = jnp.stack([me // 16, me // 4 % 4, me // 2 % 2, me % 2, s]).astype(jnp.int32)
    at = jnp.concatenate([place, lengths[0, :3]])
    scale = value_scale.reshape(1, -1)

    rows = call(
        first_join, "join", shape(CHIP, HALF), [(HBM, value_codes), (VMEM, send(value_codes, C_SWAP))], (at,),
        scratch_shapes=[pltpu.SemaphoreType.DMA],
    )
    probs, dv = [], None
    for bit, heads in ((4, (0,)), (2, (1,)), (1, (2,))):
        got = send(rows, z_swap(bit))
        for g in heads:
            if g == 0:
                p, dv, hidden = probs_part(g, at, queries, keys, upstream, dv, (rows,), hidden)
            else:
                p, dv = probs_part(g, at, queries, keys, upstream, dv, (rows,))
            probs.append(p)
        n = rows.shape[0]
        ins = [(VMEM, rows), (VMEM, got)]
        if bit == 4:
            rows, hidden = call(join_kernel, "join", shape(2 * n, HALF), ins, (p,), (hidden,))
            hidden_other = send(hidden, C_SWAP)
        elif bit == 2:
            rows = call(join_kernel, "join", shape(2 * n, HALF), ins, (p,))
        else:
            first, second = call(join_split_kernel, "join", [shape(2 * n, HEAD)] * 2, ins, (hidden_other, p))
    first_x = send(first, X_SWAP)
    second_y = [send(second, y_shift(k)) for k in (1, 2, 3)]
    p, dv = probs_part(3, at, queries, keys, upstream, dv, (first,))
    probs.append(p)
    n = first.shape[0]
    first, second, dv_half = call(
        two_joins_kernel, "join", [shape(2 * n, HEAD), shape(4 * n, HEAD), shape(COUNT, HALF, dtype=F32)],
        [(SMEM, at)] + [(VMEM, a) for a in [dv, first, first_x, second] + second_y],
    )
    pieces = [first] + [send(first, y_shift(k)) for k in (1, 2, 3)] + [second, send(second, X_SWAP)]
    dv_other = send(dv_half, C_SWAP)
    mine, theirs, sums, kept, near, beside = raw_part(at, hidden, hidden_other, dv, dv_other, scale, pieces)

    held, far = None, None
    for step, perm in enumerate((y_swap(1), y_swap(2), z_swap(1), z_swap(2), z_swap(4), X_SWAP)):
        got = send(sums, perm)
        after, through = (), ()
        if step == 0:
            values_far = send(theirs, C_SWAP)
            near = lax.ppermute(near, "seq", SEQ_SWAP)
            beside = lax.ppermute(beside, ("dp", "seq"), BESIDE)
            after = (values_far,)
        elif step < 5:
            g = step - 1
            if step == 4:
                far = [send(a, C_SWAP) for a in (near, beside, kept)]
            *held, token = grads_part(g, at, queries, keys, upstream, mine, values_far, probs[g], held, (sums,))
            after = (token,)
        else:
            grad_hidden, token = call(
                hidden_kernel, "hidden_part", [shape(COUNT, DEPTH // 2), TOKEN],
                [(SMEM, at)] + [(VMEM, a) for a in [dv, scale, near, beside, kept] + far], (sums,),
            )
            after = (token,)
        ins = [(VMEM, sums), (VMEM, got)]
        if step == 3:
            sums, near, beside, kept = call(
                add_kernel, "add", shape(1, HALF, dtype=F32), ins, after, (near, beside, kept)
            )
        else:
            sums = call(add_kernel, "add", shape(1, HALF, dtype=F32), ins, after)
    far = send(sums, C_SWAP)
    both = jnp.concatenate([jnp.where(me % 2 == 0, sums, far), jnp.where(me % 2 == 0, far, sums)], axis=1)
    return held[0], held[1], grad_hidden, (both * scale).reshape(-1)


def solution(mesh):
    placed = (
        P("dp", None),
        P("dp", "seq"),
        P("dp", "seq"),
        P("dp", "seq"),
        P("seq"),
        P("dp", "seq"),
        P("dp", None),
    )
    return jax.shard_map(
        shards,
        mesh=mesh,
        in_specs=placed,
        out_specs=(P("dp", "seq"), P("dp", "seq"), P("dp", "seq"), P("seq")),
        check_vma=False,
    )
```

```python
import functools
import math

import jax
import jax.numpy as jnp
from jax import lax
from jax.experimental import pallas as pl
from jax.experimental.pallas import tpu as pltpu
from jax.sharding import PartitionSpec as P

COUNT = 384
HEAD = 128
GROUP = 4
BLOCK = 128
BLOCKS = COUNT // BLOCK
FACTOR = 1.0 / math.sqrt(HEAD)
LOG2E = math.log2(math.e)
BF16 = jnp.bfloat16
F32 = jnp.float32
VMEM_LIMIT = 16 * 1024 * 1024


def dot(a, b, dims):
    return lax.dot_general(a, b, ((dims[:1], dims[1:]), ((), ())), preferred_element_type=F32)

VMEM = pl.BlockSpec(memory_space=pltpu.VMEM)
SMEM = pl.BlockSpec(memory_space=pltpu.SMEM)
ANY = pl.BlockSpec(memory_space=pl.ANY)
HBM = pl.BlockSpec(memory_space=pltpu.HBM)
TOKEN = jax.ShapeDtypeStruct((8, 128), F32)
WIDE = GROUP * HEAD


def call(kernel, name, out_shape, ins, after=(), through=(), **kw):
    specs = [spec for spec, _ in ins]
    args = tuple(pltpu.with_memory_space_constraint(a, pltpu.HBM) if spec is HBM else a for spec, a in ins)
    n_in = len(args) + len(after)
    single = not isinstance(out_shape, (list, tuple))
    outs = [out_shape] if single else list(out_shape)
    kw.setdefault("out_specs", [VMEM] * len(outs))

    n_out = len(outs)
    if through:
        kw["input_output_aliases"] = {n_in + j: n_out + j for j in range(len(through))}
        outs += [jax.ShapeDtypeStruct(a.shape, a.dtype) for a in through]
        kw["out_specs"] = list(kw["out_specs"]) + [ANY] * len(through)
        single = False

    def run(*refs):
        first = n_in + len(through)
        kernel(*refs[: len(args)], *refs[first : first + n_out], *refs[first + n_out + len(through) :])

    got = pl.pallas_call(
        run,
        in_specs=list(specs) + [ANY] * (len(after) + len(through)),
        out_shape=outs,
        compiler_params=pltpu.CompilerParams(vmem_limit_bytes=VMEM_LIMIT),
        cost_estimate=pl.CostEstimate(flops=1000, bytes_accessed=1000, transcendentals=0),
        name=name,
        **kw,
    )(*args, *after, *through)
    return got[0] if single else got


def shape(*dims, dtype=BF16):
    return jax.ShapeDtypeStruct(dims, dtype)


def probs_kernel(at_ref, q_ref, k_ref, up_ref, p_ref, dv_ref, bias_ref, s_ref, dv_acc):
    row = lax.broadcasted_iota(jnp.int32, (COUNT, 1), 0)
    start = jnp.zeros((COUNT, 1), jnp.int32)
    end = jnp.int32(0)
    for doc in range(3):
        end = end + at_ref[5 + doc]
        start = jnp.where(row >= end, end, start)
    rows = lax.broadcasted_iota(jnp.int32, (COUNT, COUNT), 0)
    cols = lax.broadcasted_iota(jnp.int32, (COUNT, COUNT), 1)
    bias_ref[...] = jnp.where((cols <= rows) & (cols >= start), 0.0, -1e30).astype(F32)
    dv_acc[...] = jnp.zeros_like(dv_acc)
    for i in range(BLOCKS):
        width = BLOCK * (i + 1)
        at = pl.ds(BLOCK * i, BLOCK)
        qs = jnp.concatenate([q_ref[at, pl.ds(HEAD * h, HEAD)] for h in range(GROUP)], axis=0)
        s_ref[:, :width] = dot(qs, k_ref[:width, :], (1, 1))
        for h in range(GROUP):
            scores = s_ref[pl.ds(BLOCK * h, BLOCK), :width] * (FACTOR * LOG2E) + bias_ref[at, :width]
            expo = jnp.exp2(scores - jnp.max(scores, axis=1, keepdims=True))
            probs = expo * (1.0 / jnp.sum(expo, axis=1, keepdims=True))
            p_ref[h, at, :width] = probs.astype(BF16)
        low = jnp.concatenate([p_ref[h, at, :width] for h in range(GROUP)], axis=0)
        ups = jnp.concatenate([up_ref[at, pl.ds(HEAD * h, HEAD)] for h in range(GROUP)], axis=0)
        dv_acc[:, :width] += dot(ups, low, (0, 0))
    dv_ref[...] = dv_acc[...].T


PROBS_SCRATCH = [pltpu.VMEM((COUNT, COUNT), F32), pltpu.VMEM((GROUP * BLOCK, COUNT), F32), pltpu.VMEM((HEAD, COUNT), F32)]


def first_probs_kernel(
    at_ref, q_hbm, k_hbm, up_hbm, hidden_hbm, p_ref, dv_ref, hidden_out, q_ref, k_ref, up_ref, sems, *scratch
):
    copies = [
        pltpu.make_async_copy(a.at[:, pl.ds(0, b.shape[1])], b, sems.at[j])
        for j, (a, b) in enumerate(((q_hbm, q_ref), (k_hbm, k_ref), (up_hbm, up_ref)))
    ]
    for copy in copies:
        copy.start()
    whole = pltpu.make_async_copy(hidden_hbm, hidden_out, sems.at[3])
    whole.start()
    for copy in copies:
        copy.wait()
    probs_kernel(at_ref, q_ref, k_ref, up_ref, p_ref, dv_ref, *scratch)
    whole.wait()


def probs_part(g, at, queries, keys, upstream, dv, after, hidden=None):
    wide = pl.BlockSpec((COUNT, WIDE), lambda i: (0, g))
    narrow = pl.BlockSpec((COUNT, HEAD), lambda i: (0, g))
    outs = [shape(GROUP, COUNT, COUNT), shape(COUNT, 4 * HEAD, dtype=F32)]
    if hidden is not None:
        blocks = [pltpu.VMEM((COUNT, WIDE), BF16), pltpu.VMEM((COUNT, HEAD), BF16), pltpu.VMEM((COUNT, WIDE), BF16)]
        return call(
            first_probs_kernel, "probs_part", outs + [shape(*hidden.shape)],
            [(SMEM, at), (HBM, queries), (HBM, keys), (HBM, upstream), (HBM, hidden)], after, out_specs=[VMEM, narrow, ANY],
            grid=(1,), scratch_shapes=blocks + [pltpu.SemaphoreType.DMA((4,))] + PROBS_SCRATCH,
        )

    def kernel(*refs):
        probs_kernel(*refs[:4], *refs[5:])

    return call(
        kernel, "probs_part", outs, [(SMEM, at), (wide, queries), (narrow, keys), (wide, upstream), (ANY, dv)], after,
        out_specs=[VMEM, narrow], grid=(1,), scratch_shapes=PROBS_SCRATCH, input_output_aliases={4: 1},
    )


def grads_kernel(g, at_ref, q_ref, k_ref, up_ref, mine_ref, theirs_ref, p_ref, gq_ref, gk_ref, token_ref, dp_ref, ds_ref, dk_acc):
    token_ref[...] = jnp.zeros_like(token_ref)
    dk_acc[...] = jnp.zeros_like(dk_acc)
    col = pl.ds(HEAD * (g % 2), HEAD)
    all_values = jnp.where(at_ref[3] == g // 2, mine_ref[:, col], theirs_ref[:, col])
    for i in range(BLOCKS):
        width = BLOCK * (i + 1)
        at = pl.ds(BLOCK * i, BLOCK)
        ups = jnp.concatenate([up_ref[at, pl.ds(HEAD * h, HEAD)] for h in range(GROUP)], axis=0)
        dp_ref[:, :width] = dot(ups, all_values[:width], (1, 1))
        for h in range(GROUP):
            rows = pl.ds(BLOCK * h, BLOCK)
            dprobs = dp_ref[rows, :width]
            probs = p_ref[h, at, :width].astype(F32)
            delta = jnp.sum(probs * dprobs, axis=1, keepdims=True)
            ds_ref[rows, :width] = (probs * (dprobs - delta)).astype(BF16)
        dscores = ds_ref[:, :width]
        gq = dot(dscores, k_ref[:width, :], (1, 0)) * FACTOR
        for h in range(GROUP):
            gq_ref[at, pl.ds(HEAD * h, HEAD)] = gq[BLOCK * h : BLOCK * (h + 1)].astype(BF16)
        qs = jnp.concatenate([q_ref[at, pl.ds(HEAD * h, HEAD)] for h in range(GROUP)], axis=0)
        dk_acc[:, :width] += dot(qs, dscores, (0, 0))
    gk_ref[...] = (dk_acc[...] * FACTOR).T.astype(BF16)


def grads_part(g, at, queries, keys, upstream, mine, theirs, probs, held, after):
    wide = pl.BlockSpec((COUNT, WIDE), lambda i: (0, g))
    narrow = pl.BlockSpec((COUNT, HEAD), lambda i: (0, g))
    ins = [(SMEM, at), (wide, queries), (narrow, keys), (wide, upstream), (VMEM, mine), (VMEM, theirs), (VMEM, probs)]

    def kernel(*refs):
        grads_kernel(g, *refs[:7], *refs[len(refs) - 6 :])

    extra = {}
    if held is not None:
        ins += [(ANY, held[0]), (ANY, held[1])]
        extra["input_output_aliases"] = {7: 0, 8: 1}
    return call(
        kernel, "grads_part", [shape(*queries.shape), shape(*keys.shape), TOKEN], ins, after,
        out_specs=[wide, narrow, VMEM], grid=(1,),
        scratch_shapes=[pltpu.VMEM((GROUP * BLOCK, COUNT), F32), pltpu.VMEM((GROUP * BLOCK, COUNT), BF16), pltpu.VMEM((HEAD, COUNT), F32)], **extra,
    )


SHARD = 32
CHIP = 2 * SHARD
HALF = 256
DEPTH = 4096


def own_columns(at_ref):
    return pl.ds(pl.multiple_of(at_ref[3] * HALF, HALF), HALF)


def first_join(own_hbm, other_ref, out_ref, sem):
    c = lax.rem(lax.axis_index("dp"), 2)
    cols = pl.ds(pl.multiple_of(c * HALF, HALF), HALF)
    copy = pltpu.make_async_copy(
        own_hbm.at[:, cols], out_ref.at[pl.ds(pl.multiple_of(c * SHARD, SHARD), SHARD), :], sem
    )
    copy.start()
    out_ref[pl.ds(pl.multiple_of((1 - c) * SHARD, SHARD), SHARD), :] = other_ref[:, cols]
    copy.wait()


def join_kernel(own_ref, other_ref, out_ref):
    n = own_ref.shape[0]
    out_ref[:n, :] = own_ref[...]
    out_ref[n:, :] = other_ref[...]


def join_split_kernel(own_ref, other_ref, first_ref, second_ref):
    n = own_ref.shape[0]
    for j, out_ref in enumerate((first_ref, second_ref)):
        out_ref[:n, :] = own_ref[:, HEAD * j : HEAD * (j + 1)]
        out_ref[n:, :] = other_ref[:, HEAD * j : HEAD * (j + 1)]


def two_joins_kernel(at_ref, dv_ref, a0, a1, b0, b1, b2, b3, first_ref, second_ref, dv_out):
    dv_out[...] = dv_ref[:, pl.ds(pl.multiple_of((1 - at_ref[3]) * HALF, HALF), HALF)].astype(BF16)
    n = a0.shape[0]
    for j, part in enumerate((a0, a1)):
        first_ref[n * j : n * (j + 1), :] = part[...]
    for j, part in enumerate((b0, b1, b2, b3)):
        second_ref[n * j : n * (j + 1), :] = part[...]


def put_in_order(at_ref, pieces, codes_ref):
    z, y, x = at_ref[0], at_ref[1], at_ref[2]

    def place(piece, row, i, k, xi, col):
        zi = (i & 1) * 4 + (i & 2) + (i >> 2)
        to = ((z ^ zi) * 4 + ((y + 4 - k) & 3)) * 2 + (x ^ xi)
        rows = pl.ds(pl.multiple_of(to * CHIP, CHIP), CHIP)
        codes_ref[rows, pl.ds(col, HEAD)] = piece[pl.ds(row, CHIP), :]

    for k in range(4):
        for xi in range(2):
            for i in range(8):
                place(pieces[k], (xi * 8 + i) * CHIP, i, k, xi, 0)
                place(pieces[4 + xi], (k * 8 + i) * CHIP, i, k, xi, HEAD)


NEAR = 640
BESIDES = DEPTH // 2 - NEAR


def raw_kernel(at_ref, own_ref, other_ref, dv_own, dv_other, scale_ref, *refs):
    pieces, (mine_ref, theirs_ref, sums_ref, kept_ref, near_ref, beside_ref, codes_ref) = refs[:6], refs[6:]
    put_in_order(at_ref, pieces, codes_ref)
    cols = own_columns(at_ref)
    scale = scale_ref[:, cols]
    sums = jnp.zeros((1, HALF), F32)
    terms = ((other_ref, dv_other[...].astype(F32), theirs_ref), (own_ref, dv_own[:, cols], mine_ref))
    for hidden_ref, dv, values_ref in terms:
        raw = dot(hidden_ref[...], codes_ref[...], (1, 0))
        values_ref[...] = (raw * scale).astype(BF16)
        sums += jnp.sum(raw * dv, axis=0, keepdims=True)
    sums_ref[...] = sums
    s, half = at_ref[4], DEPTH // 2
    kept_ref[...] = codes_ref[pl.ds(pl.multiple_of(s * half, half), half), :]
    base = (1 - s) * half
    for j in range(2):
        part = pl.ds(j * HALF, HALF)
        near_ref[pl.ds(j * COUNT, COUNT), :] = (dv_own[:, part] * scale_ref[:, part]).astype(BF16)
    near_ref[2 * COUNT :, :] = codes_ref[pl.ds(pl.multiple_of(base, half), NEAR), :]
    beside_ref[...] = codes_ref[pl.ds(pl.multiple_of(base + NEAR, 128), BESIDES), :]


def raw_part(at, hidden, hidden_other, dv, dv_other, scale, pieces):
    outs = [shape(COUNT, HALF), shape(COUNT, HALF), shape(1, HALF, dtype=F32)]
    outs += [shape(DEPTH // 2, HALF), shape(2 * COUNT + NEAR, HALF), shape(BESIDES, HALF)]
    return call(
        raw_kernel, "raw_part", outs,
        [(SMEM, at)] + [(VMEM, a) for a in [hidden, hidden_other, dv, dv_other, scale] + pieces],
        scratch_shapes=[pltpu.VMEM((DEPTH, HALF), BF16)],
    )


BATCH = 512


def hidden_kernel(
    at_ref, dv_ref, scale_ref, near_ref, beside_ref, kept_ref, near_far, beside_far, kept_far, out_ref, token_ref
):
    token_ref[...] = jnp.zeros_like(token_ref)
    sides = []
    for other, near, beside, kept in ((0, near_ref, beside_ref, kept_ref), (1, near_far, beside_far, kept_far)):
        c = at_ref[3] ^ other
        cols = pl.ds(pl.multiple_of(c * HALF, HALF), HALF)
        own = (dv_ref[:, cols] * scale_ref[:, cols]).astype(BF16)
        seq = near_ref[pl.ds(pl.multiple_of(c * COUNT, COUNT), COUNT), :]
        sides.append((own, seq, near, beside, kept))
    at = 0
    while at < DEPTH // 2:
        end = min(at + BATCH, NEAR if at < NEAR else DEPTH // 2)
        total = 0.0
        for own, seq, near, beside, kept in sides:
            total += dot(own, kept[at:end, :], (1, 1))
            codes = near[2 * COUNT + at : 2 * COUNT + end, :] if at < NEAR else beside[at - NEAR : end - NEAR, :]
            total += dot(seq, codes, (1, 1))
        out_ref[:, at:end] = total.astype(BF16)
        at = end


def add_kernel(a_ref, b_ref, out_ref):
    out_ref[...] = a_ref[...] + b_ref[...]


def pairs(move):
    out = []
    for i in range(128):
        z, y, x, c = move(i // 16, i // 4 % 4, i // 2 % 2, i % 2)
        out.append((i, ((z * 4 + y) * 2 + x) * 2 + c))
    return out


def z_swap(bit):
    return pairs(lambda z, y, x, c: (z ^ bit, y, x, c))


def y_shift(k):
    return pairs(lambda z, y, x, c: (z, (y + k) % 4, x, c))


def y_swap(bit):
    return pairs(lambda z, y, x, c: (z, y ^ bit, x, c))


X_SWAP = pairs(lambda z, y, x, c: (z, y, x ^ 1, c))
C_SWAP = pairs(lambda z, y, x, c: (z, y, x, c ^ 1))
SEQ_SWAP = [(0, 1), (1, 0)]
BESIDE = [(2 * a + s, 2 * b + 1 - s) for a, b in X_SWAP for s in range(2)]


def send(x, perm):
    return lax.ppermute(x, "dp", perm)


def shards(hidden, queries, keys, value_codes, value_scale, upstream, lengths):
    me, s = lax.axis_index("dp"), lax.axis_index("seq")
    place = jnp.stack([me // 16, me // 4 % 4, me // 2 % 2, me % 2, s]).astype(jnp.int32)
    at = jnp.concatenate([place, lengths[0, :3]])
    scale = value_scale.reshape(1, -1)

    rows = call(
        first_join, "join", shape(CHIP, HALF), [(HBM, value_codes), (VMEM, send(value_codes, C_SWAP))], (at,),
        scratch_shapes=[pltpu.SemaphoreType.DMA],
    )
    probs, dv = [], None
    for bit, heads in ((4, (0,)), (2, (1,)), (1, (2,))):
        got = send(rows, z_swap(bit))
        for g in heads:
            if g == 0:
                p, dv, hidden = probs_part(g, at, queries, keys, upstream, dv, (rows,), hidden)
            else:
                p, dv = probs_part(g, at, queries, keys, upstream, dv, (rows,))
            probs.append(p)
        n = rows.shape[0]
        ins = [(VMEM, rows), (VMEM, got)]
        if bit == 4:
            rows, hidden = call(join_kernel, "join", shape(2 * n, HALF), ins, (p,), (hidden,))
            hidden_other = send(hidden, C_SWAP)
        elif bit == 2:
            rows = call(join_kernel, "join", shape(2 * n, HALF), ins, (p,))
        else:
            first, second = call(join_split_kernel, "join", [shape(2 * n, HEAD)] * 2, ins, (hidden_other, p))
    first_x = send(first, X_SWAP)
    second_y = [send(second, y_shift(k)) for k in (1, 2, 3)]
    p, dv = probs_part(3, at, queries, keys, upstream, dv, (first,))
    probs.append(p)
    n = first.shape[0]
    first, second, dv_half = call(
        two_joins_kernel, "join", [shape(2 * n, HEAD), shape(4 * n, HEAD), shape(COUNT, HALF)],
        [(SMEM, at)] + [(VMEM, a) for a in [dv, first, first_x, second] + second_y],
    )
    pieces = [first] + [send(first, y_shift(k)) for k in (1, 2, 3)] + [second, send(second, X_SWAP)]
    dv_other = send(dv_half, C_SWAP)
    mine, theirs, sums, kept, near, beside = raw_part(at, hidden, hidden_other, dv, dv_other, scale, pieces)

    held, far = None, None
    for step, perm in enumerate((y_swap(1), y_swap(2), z_swap(1), z_swap(2), z_swap(4), X_SWAP)):
        got = send(sums, perm)
        after, through = (), ()
        if step == 0:
            values_far = send(theirs, C_SWAP)
            near = lax.ppermute(near, "seq", SEQ_SWAP)
            beside = lax.ppermute(beside, ("dp", "seq"), BESIDE)
            kept_far = send(kept, C_SWAP)
            after = (values_far, kept_far)
        elif step < 5:
            g = step - 1
            if step == 4:
                far = [send(a, C_SWAP) for a in (near, beside)] + [kept_far]
            *held, token = grads_part(g, at, queries, keys, upstream, mine, values_far, probs[g], held, (sums,))
            after = (token,)
        else:
            grad_hidden, token = call(
                hidden_kernel, "hidden_part", [shape(COUNT, DEPTH // 2), TOKEN],
                [(SMEM, at)] + [(VMEM, a) for a in [dv, scale, near, beside, kept] + far], (sums,),
            )
            after = (token,)
        ins = [(VMEM, sums), (VMEM, got)]
        if step == 3:
            sums, near, beside = call(add_kernel, "add", shape(1, HALF, dtype=F32), ins, after, (near, beside))
        else:
            sums = call(add_kernel, "add", shape(1, HALF, dtype=F32), ins, after)
    far = send(sums, C_SWAP)
    both = jnp.concatenate([jnp.where(me % 2 == 0, sums, far), jnp.where(me % 2 == 0, far, sums)], axis=1)
    return held[0], held[1], grad_hidden, (both * scale).reshape(-1)


def solution(mesh):
    placed = (
        P("dp", None),
        P("dp", "seq"),
        P("dp", "seq"),
        P("dp", "seq"),
        P("seq"),
        P("dp", "seq"),
        P("dp", None),
    )
    return jax.shard_map(
        shards,
        mesh=mesh,
        in_specs=placed,
        out_specs=(P("dp", "seq"), P("dp", "seq"), P("dp", "seq"), P("seq")),
        check_vma=False,
    )
```

```python
import functools
import math

import jax
import jax.numpy as jnp
from jax import lax
from jax.experimental import pallas as pl
from jax.experimental.pallas import tpu as pltpu
from jax.sharding import PartitionSpec as P

COUNT = 384
HEAD = 128
GROUP = 4
BLOCK = 128
BLOCKS = COUNT // BLOCK
FACTOR = 1.0 / math.sqrt(HEAD)
LOG2E = math.log2(math.e)
BF16 = jnp.bfloat16
F32 = jnp.float32
VMEM_LIMIT = 16 * 1024 * 1024


def dot(a, b, dims):
    return lax.dot_general(a, b, ((dims[:1], dims[1:]), ((), ())), preferred_element_type=F32)

VMEM = pl.BlockSpec(memory_space=pltpu.VMEM)
SMEM = pl.BlockSpec(memory_space=pltpu.SMEM)
ANY = pl.BlockSpec(memory_space=pl.ANY)
HBM = pl.BlockSpec(memory_space=pltpu.HBM)
TOKEN = jax.ShapeDtypeStruct((8, 128), F32)
WIDE = GROUP * HEAD


def call(kernel, name, out_shape, ins, after=(), through=(), **kw):
    specs = [spec for spec, _ in ins]
    args = tuple(pltpu.with_memory_space_constraint(a, pltpu.HBM) if spec is HBM else a for spec, a in ins)
    n_in = len(args) + len(after)
    single = not isinstance(out_shape, (list, tuple))
    outs = [out_shape] if single else list(out_shape)
    kw.setdefault("out_specs", [VMEM] * len(outs))

    n_out = len(outs)
    if through:
        kw["input_output_aliases"] = {n_in + j: n_out + j for j in range(len(through))}
        outs += [jax.ShapeDtypeStruct(a.shape, a.dtype) for a in through]
        kw["out_specs"] = list(kw["out_specs"]) + [ANY] * len(through)
        single = False

    def run(*refs):
        first = n_in + len(through)
        kernel(*refs[: len(args)], *refs[first : first + n_out], *refs[first + n_out + len(through) :])

    got = pl.pallas_call(
        run,
        in_specs=list(specs) + [ANY] * (len(after) + len(through)),
        out_shape=outs,
        compiler_params=pltpu.CompilerParams(vmem_limit_bytes=VMEM_LIMIT),
        cost_estimate=pl.CostEstimate(flops=1000, bytes_accessed=1000, transcendentals=0),
        name=name,
        **kw,
    )(*args, *after, *through)
    return got[0] if single else got


def shape(*dims, dtype=BF16):
    return jax.ShapeDtypeStruct(dims, dtype)


def probs_kernel(at_ref, q_ref, k_ref, up_ref, p_ref, dv_ref, bias_ref, s_ref, dv_acc):
    row = lax.broadcasted_iota(jnp.int32, (COUNT, 1), 0)
    start = jnp.zeros((COUNT, 1), jnp.int32)
    end = jnp.int32(0)
    for doc in range(3):
        end = end + at_ref[5 + doc]
        start = jnp.where(row >= end, end, start)
    rows = lax.broadcasted_iota(jnp.int32, (COUNT, COUNT), 0)
    cols = lax.broadcasted_iota(jnp.int32, (COUNT, COUNT), 1)
    bias_ref[...] = jnp.where((cols <= rows) & (cols >= start), 0.0, -1e30).astype(F32)
    dv_acc[...] = jnp.zeros_like(dv_acc)
    for i in range(BLOCKS):
        width = BLOCK * (i + 1)
        at = pl.ds(BLOCK * i, BLOCK)
        qs = jnp.concatenate([q_ref[at, pl.ds(HEAD * h, HEAD)] for h in range(GROUP)], axis=0)
        s_ref[:, :width] = dot(qs, k_ref[:width, :], (1, 1))
        for h in range(GROUP):
            scores = s_ref[pl.ds(BLOCK * h, BLOCK), :width] * (FACTOR * LOG2E) + bias_ref[at, :width]
            expo = jnp.exp2(scores - jnp.max(scores, axis=1, keepdims=True))
            probs = expo * (1.0 / jnp.sum(expo, axis=1, keepdims=True))
            p_ref[h, at, :width] = probs.astype(BF16)
        low = jnp.concatenate([p_ref[h, at, :width] for h in range(GROUP)], axis=0)
        ups = jnp.concatenate([up_ref[at, pl.ds(HEAD * h, HEAD)] for h in range(GROUP)], axis=0)
        dv_acc[:, :width] += dot(ups, low, (0, 0))
    dv_ref[...] = dv_acc[...].T


PROBS_SCRATCH = [pltpu.VMEM((COUNT, COUNT), F32), pltpu.VMEM((GROUP * BLOCK, COUNT), F32), pltpu.VMEM((HEAD, COUNT), F32)]


def first_probs_kernel(
    at_ref, q_hbm, k_hbm, up_hbm, hidden_hbm, p_ref, dv_ref, hidden_out, q_ref, k_ref, up_ref, sems, *scratch
):
    copies = [
        pltpu.make_async_copy(a.at[:, pl.ds(0, b.shape[1])], b, sems.at[j])
        for j, (a, b) in enumerate(((q_hbm, q_ref), (k_hbm, k_ref), (up_hbm, up_ref)))
    ]
    for copy in copies:
        copy.start()
    whole = pltpu.make_async_copy(hidden_hbm, hidden_out, sems.at[3])
    whole.start()
    for copy in copies:
        copy.wait()
    probs_kernel(at_ref, q_ref, k_ref, up_ref, p_ref, dv_ref, *scratch)
    whole.wait()


def probs_part(g, at, queries, keys, upstream, dv, after, hidden=None):
    wide = pl.BlockSpec((COUNT, WIDE), lambda i: (0, g))
    narrow = pl.BlockSpec((COUNT, HEAD), lambda i: (0, g))
    outs = [shape(GROUP, COUNT, COUNT), shape(COUNT, 4 * HEAD, dtype=F32)]
    if hidden is not None:
        blocks = [pltpu.VMEM((COUNT, WIDE), BF16), pltpu.VMEM((COUNT, HEAD), BF16), pltpu.VMEM((COUNT, WIDE), BF16)]
        return call(
            first_probs_kernel, "probs_part", outs + [shape(*hidden.shape)],
            [(SMEM, at), (HBM, queries), (HBM, keys), (HBM, upstream), (HBM, hidden)], after, out_specs=[VMEM, narrow, ANY],
            grid=(1,), scratch_shapes=blocks + [pltpu.SemaphoreType.DMA((4,))] + PROBS_SCRATCH,
        )

    def kernel(*refs):
        probs_kernel(*refs[:4], *refs[5:])

    return call(
        kernel, "probs_part", outs, [(SMEM, at), (wide, queries), (narrow, keys), (wide, upstream), (ANY, dv)], after,
        out_specs=[VMEM, narrow], grid=(1,), scratch_shapes=PROBS_SCRATCH, input_output_aliases={4: 1},
    )


def grads_kernel(g, at_ref, q_ref, k_ref, up_ref, mine_ref, theirs_ref, p_ref, gq_ref, gk_ref, token_ref, dp_ref, ds_ref, dk_acc):
    token_ref[...] = jnp.zeros_like(token_ref)
    dk_acc[...] = jnp.zeros_like(dk_acc)
    col = pl.ds(HEAD * (g % 2), HEAD)
    all_values = jnp.where(at_ref[3] == g // 2, mine_ref[:, col], theirs_ref[:, col])
    for i in range(BLOCKS):
        width = BLOCK * (i + 1)
        at = pl.ds(BLOCK * i, BLOCK)
        ups = jnp.concatenate([up_ref[at, pl.ds(HEAD * h, HEAD)] for h in range(GROUP)], axis=0)
        dp_ref[:, :width] = dot(ups, all_values[:width], (1, 1))
        for h in range(GROUP):
            rows = pl.ds(BLOCK * h, BLOCK)
            dprobs = dp_ref[rows, :width]
            probs = p_ref[h, at, :width].astype(F32)
            delta = jnp.sum(probs * dprobs, axis=1, keepdims=True)
            ds_ref[rows, :width] = (probs * (dprobs - delta)).astype(BF16)
        dscores = ds_ref[:, :width]
        gq = dot(dscores, k_ref[:width, :], (1, 0)) * FACTOR
        for h in range(GROUP):
            gq_ref[at, pl.ds(HEAD * h, HEAD)] = gq[BLOCK * h : BLOCK * (h + 1)].astype(BF16)
        qs = jnp.concatenate([q_ref[at, pl.ds(HEAD * h, HEAD)] for h in range(GROUP)], axis=0)
        dk_acc[:, :width] += dot(qs, dscores, (0, 0))
    gk_ref[...] = (dk_acc[...] * FACTOR).T.astype(BF16)


def grads_part(g, at, queries, keys, upstream, mine, theirs, probs, held, after):
    wide = pl.BlockSpec((COUNT, WIDE), lambda i: (0, g))
    narrow = pl.BlockSpec((COUNT, HEAD), lambda i: (0, g))
    ins = [(SMEM, at), (wide, queries), (narrow, keys), (wide, upstream), (VMEM, mine), (VMEM, theirs), (VMEM, probs)]

    def kernel(*refs):
        grads_kernel(g, *refs[:7], *refs[len(refs) - 6 :])

    extra = {}
    if held is not None:
        ins += [(ANY, held[0]), (ANY, held[1])]
        extra["input_output_aliases"] = {7: 0, 8: 1}
    return call(
        kernel, "grads_part", [shape(*queries.shape), shape(*keys.shape), TOKEN], ins, after,
        out_specs=[wide, narrow, VMEM], grid=(1,),
        scratch_shapes=[pltpu.VMEM((GROUP * BLOCK, COUNT), F32), pltpu.VMEM((GROUP * BLOCK, COUNT), BF16), pltpu.VMEM((HEAD, COUNT), F32)], **extra,
    )


SHARD = 32
CHIP = 2 * SHARD
HALF = 256
DEPTH = 4096


def own_columns(at_ref):
    return pl.ds(pl.multiple_of(at_ref[3] * HALF, HALF), HALF)


def first_join(own_hbm, other_ref, out_ref, sem):
    c = lax.rem(lax.axis_index("dp"), 2)
    cols = pl.ds(pl.multiple_of(c * HALF, HALF), HALF)
    copy = pltpu.make_async_copy(
        own_hbm.at[:, cols], out_ref.at[pl.ds(pl.multiple_of(c * SHARD, SHARD), SHARD), :], sem
    )
    copy.start()
    out_ref[pl.ds(pl.multiple_of((1 - c) * SHARD, SHARD), SHARD), :] = other_ref[:, cols]
    copy.wait()


def join_kernel(own_ref, other_ref, out_ref):
    n = own_ref.shape[0]
    out_ref[:n, :] = own_ref[...]
    out_ref[n:, :] = other_ref[...]


def join_split_kernel(own_ref, other_ref, first_ref, second_ref):
    n = own_ref.shape[0]
    for j, out_ref in enumerate((first_ref, second_ref)):
        out_ref[:n, :] = own_ref[:, HEAD * j : HEAD * (j + 1)]
        out_ref[n:, :] = other_ref[:, HEAD * j : HEAD * (j + 1)]


def two_joins_kernel(at_ref, dv_ref, a0, a1, b0, b1, b2, b3, first_ref, second_ref, dv_out):
    dv_out[...] = dv_ref[:, pl.ds(pl.multiple_of((1 - at_ref[3]) * HALF, HALF), HALF)].astype(BF16)
    n = a0.shape[0]
    for j, part in enumerate((a0, a1)):
        first_ref[n * j : n * (j + 1), :] = part[...]
    for j, part in enumerate((b0, b1, b2, b3)):
        second_ref[n * j : n * (j + 1), :] = part[...]


def put_in_order(at_ref, pieces, codes_ref):
    z, y, x = at_ref[0], at_ref[1], at_ref[2]

    def place(piece, row, i, k, xi, col):
        zi = (i & 1) * 4 + (i & 2) + (i >> 2)
        to = ((z ^ zi) * 4 + ((y + 4 - k) & 3)) * 2 + (x ^ xi)
        rows = pl.ds(pl.multiple_of(to * CHIP, CHIP), CHIP)
        codes_ref[rows, pl.ds(col, HEAD)] = piece[pl.ds(row, CHIP), :]

    for k in range(4):
        for xi in range(2):
            for i in range(8):
                place(pieces[k], (xi * 8 + i) * CHIP, i, k, xi, 0)
                place(pieces[4 + xi], (k * 8 + i) * CHIP, i, k, xi, HEAD)


NEAR = 640
BESIDES = DEPTH // 2 - NEAR


def raw_kernel(at_ref, own_ref, other_ref, dv_own, dv_other, scale_ref, *refs):
    pieces, (mine_ref, theirs_ref, sums_ref, kept_ref, near_ref, beside_ref, codes_ref) = refs[:6], refs[6:]
    put_in_order(at_ref, pieces, codes_ref)
    cols = own_columns(at_ref)
    scale = scale_ref[:, cols]
    sums = jnp.zeros((1, HALF), F32)
    terms = ((other_ref, dv_other[...].astype(F32), theirs_ref), (own_ref, dv_own[:, cols], mine_ref))
    for hidden_ref, dv, values_ref in terms:
        raw = dot(hidden_ref[...], codes_ref[...], (1, 0))
        values_ref[...] = (raw * scale).astype(BF16)
        sums += jnp.sum(raw * dv, axis=0, keepdims=True)
    sums_ref[...] = sums
    s, half = at_ref[4], DEPTH // 2
    kept_ref[...] = codes_ref[pl.ds(pl.multiple_of(s * half, half), half), :]
    base = (1 - s) * half
    for j in range(2):
        part = pl.ds(j * HALF, HALF)
        near_ref[pl.ds(j * COUNT, COUNT), :] = (dv_own[:, part] * scale_ref[:, part]).astype(BF16)
    near_ref[2 * COUNT :, :] = codes_ref[pl.ds(pl.multiple_of(base, half), NEAR), :]
    beside_ref[...] = codes_ref[pl.ds(pl.multiple_of(base + NEAR, 128), BESIDES), :]


def raw_part(at, hidden, hidden_other, dv, dv_other, scale, pieces):
    outs = [shape(COUNT, HALF), shape(COUNT, HALF), shape(1, HALF, dtype=F32)]
    outs += [shape(DEPTH // 2, HALF), shape(2 * COUNT + NEAR, HALF), shape(BESIDES, HALF)]
    return call(
        raw_kernel, "raw_part", outs,
        [(SMEM, at)] + [(VMEM, a) for a in [hidden, hidden_other, dv, dv_other, scale] + pieces],
        scratch_shapes=[pltpu.VMEM((DEPTH, HALF), BF16)],
    )


BATCH = 512


def hidden_kernel(first, at_ref, dv_ref, scale_ref, near_ref, codes_ref, codes_far, kept_ref, kept_far, *refs):
    out_ref, token_ref, part_ref, sem = refs[-4:]
    token_ref[...] = jnp.zeros_like(token_ref)
    base, size, skip = (0, NEAR, 2 * COUNT) if first else (NEAR, BESIDES, 0)
    sides = []
    for other, codes, kept in ((0, codes_ref, kept_ref), (1, codes_far, kept_far)):
        c = at_ref[3] ^ other
        cols = pl.ds(pl.multiple_of(c * HALF, HALF), HALF)
        own = (dv_ref[:, cols] * scale_ref[:, cols]).astype(BF16)
        seq = near_ref[pl.ds(pl.multiple_of(c * COUNT, COUNT), COUNT), :]
        sides.append((own, seq, codes, kept))
    for at in range(0, size, BATCH):
        end = min(at + BATCH, size)
        total = 0.0
        for own, seq, codes, kept in sides:
            total += dot(own, kept[base + at : base + end, :], (1, 1))
            total += dot(seq, codes[skip + at : skip + end, :], (1, 1))
        part_ref[:, at:end] = total.astype(BF16)
    copy = pltpu.make_async_copy(part_ref, out_ref.at[:, pl.ds(base, size)], sem)
    copy.start()
    copy.wait()


def hidden_part(first, arrays, held, after):
    extra = {}
    ins = [(SMEM, arrays[0])] + [(VMEM, a) for a in arrays[1:]]
    if held is not None:
        extra["input_output_aliases"] = {len(ins): 0}
        ins.append((ANY, held))
    return call(
        functools.partial(hidden_kernel, first), "hidden_part", [shape(COUNT, DEPTH // 2), TOKEN], ins, after,
        out_specs=[ANY, VMEM],
        scratch_shapes=[pltpu.VMEM((COUNT, NEAR if first else BESIDES), BF16), pltpu.SemaphoreType.DMA], **extra,
    )


def add_kernel(a_ref, b_ref, out_ref):
    out_ref[...] = a_ref[...] + b_ref[...]


def pairs(move):
    out = []
    for i in range(128):
        z, y, x, c = move(i // 16, i // 4 % 4, i // 2 % 2, i % 2)
        out.append((i, ((z * 4 + y) * 2 + x) * 2 + c))
    return out


def z_swap(bit):
    return pairs(lambda z, y, x, c: (z ^ bit, y, x, c))


def y_shift(k):
    return pairs(lambda z, y, x, c: (z, (y + k) % 4, x, c))


def y_swap(bit):
    return pairs(lambda z, y, x, c: (z, y ^ bit, x, c))


X_SWAP = pairs(lambda z, y, x, c: (z, y, x ^ 1, c))
C_SWAP = pairs(lambda z, y, x, c: (z, y, x, c ^ 1))
SEQ_SWAP = [(0, 1), (1, 0)]
BESIDE = [(2 * a + s, 2 * b + 1 - s) for a, b in X_SWAP for s in range(2)]


def send(x, perm):
    return lax.ppermute(x, "dp", perm)


def shards(hidden, queries, keys, value_codes, value_scale, upstream, lengths):
    me, s = lax.axis_index("dp"), lax.axis_index("seq")
    place = jnp.stack([me // 16, me // 4 % 4, me // 2 % 2, me % 2, s]).astype(jnp.int32)
    at = jnp.concatenate([place, lengths[0, :3]])
    scale = value_scale.reshape(1, -1)

    rows = call(
        first_join, "join", shape(CHIP, HALF), [(HBM, value_codes), (VMEM, send(value_codes, C_SWAP))], (at,),
        scratch_shapes=[pltpu.SemaphoreType.DMA],
    )
    probs, dv = [], None
    for bit, heads in ((4, (0,)), (2, (1,)), (1, (2,))):
        got = send(rows, z_swap(bit))
        for g in heads:
            if g == 0:
                p, dv, hidden = probs_part(g, at, queries, keys, upstream, dv, (rows,), hidden)
            else:
                p, dv = probs_part(g, at, queries, keys, upstream, dv, (rows,))
            probs.append(p)
        n = rows.shape[0]
        ins = [(VMEM, rows), (VMEM, got)]
        if bit == 4:
            rows, hidden = call(join_kernel, "join", shape(2 * n, HALF), ins, (p,), (hidden,))
            hidden_other = send(hidden, C_SWAP)
        elif bit == 2:
            rows = call(join_kernel, "join", shape(2 * n, HALF), ins, (p,))
        else:
            first, second = call(join_split_kernel, "join", [shape(2 * n, HEAD)] * 2, ins, (hidden_other, p))
    first_x = send(first, X_SWAP)
    second_y = [send(second, y_shift(k)) for k in (1, 2, 3)]
    p, dv = probs_part(3, at, queries, keys, upstream, dv, (first,))
    probs.append(p)
    n = first.shape[0]
    first, second, dv_half = call(
        two_joins_kernel, "join", [shape(2 * n, HEAD), shape(4 * n, HEAD), shape(COUNT, HALF)],
        [(SMEM, at)] + [(VMEM, a) for a in [dv, first, first_x, second] + second_y],
    )
    pieces = [first] + [send(first, y_shift(k)) for k in (1, 2, 3)] + [second, send(second, X_SWAP)]
    dv_other = send(dv_half, C_SWAP)
    mine, theirs, sums, kept, near, beside = raw_part(at, hidden, hidden_other, dv, dv_other, scale, pieces)

    held = None
    for step, perm in enumerate((y_swap(1), y_swap(2), z_swap(1), z_swap(2), z_swap(4), X_SWAP)):
        got = send(sums, perm)
        after, through = (), ()
        if step == 0:
            values_far = send(theirs, C_SWAP)
            near = lax.ppermute(near, "seq", SEQ_SWAP)
            beside = lax.ppermute(beside, ("dp", "seq"), BESIDE)
            kept_far = send(kept, C_SWAP)
            after = (values_far, kept_far)
        elif step < 5:
            g = step - 1
            if step == 4:
                near_far, beside_far = send(near, C_SWAP), send(beside, C_SWAP)
            *held, token = grads_part(g, at, queries, keys, upstream, mine, values_far, probs[g], held, (sums,))
            if step == 4:
                grad_hidden, token = hidden_part(
                    True, (at, dv, scale, near, near, near_far, kept, kept_far), None, (token,)
                )
            after = (token,)
        else:
            grad_hidden, token = hidden_part(
                False, (at, dv, scale, near, beside, beside_far, kept, kept_far), grad_hidden, (sums,)
            )
            after = (token,)
        ins = [(VMEM, sums), (VMEM, got)]
        if step == 3:
            sums, near, beside = call(add_kernel, "add", shape(1, HALF, dtype=F32), ins, after, (near, beside))
        else:
            sums = call(add_kernel, "add", shape(1, HALF, dtype=F32), ins, after)
    far = send(sums, C_SWAP)
    both = jnp.concatenate([jnp.where(me % 2 == 0, sums, far), jnp.where(me % 2 == 0, far, sums)], axis=1)
    return held[0], held[1], grad_hidden, (both * scale).reshape(-1)


def solution(mesh):
    placed = (
        P("dp", None),
        P("dp", "seq"),
        P("dp", "seq"),
        P("dp", "seq"),
        P("seq"),
        P("dp", "seq"),
        P("dp", None),
    )
    return jax.shard_map(
        shards,
        mesh=mesh,
        in_specs=placed,
        out_specs=(P("dp", "seq"), P("dp", "seq"), P("dp", "seq"), P("seq")),
        check_vma=False,
    )
```

```python
import functools
import math

import jax
import jax.numpy as jnp
from jax import lax
from jax.experimental import pallas as pl
from jax.experimental.pallas import tpu as pltpu
from jax.sharding import PartitionSpec as P

COUNT = 384
HEAD = 128
GROUP = 4
BLOCK = 128
BLOCKS = COUNT // BLOCK
FACTOR = 1.0 / math.sqrt(HEAD)
LOG2E = math.log2(math.e)
BF16 = jnp.bfloat16
F32 = jnp.float32
VMEM_LIMIT = 16 * 1024 * 1024


def dot(a, b, dims):
    return lax.dot_general(a, b, ((dims[:1], dims[1:]), ((), ())), preferred_element_type=F32)

VMEM = pl.BlockSpec(memory_space=pltpu.VMEM)
SMEM = pl.BlockSpec(memory_space=pltpu.SMEM)
ANY = pl.BlockSpec(memory_space=pl.ANY)
HBM = pl.BlockSpec(memory_space=pltpu.HBM)
TOKEN = jax.ShapeDtypeStruct((8, 128), F32)
WIDE = GROUP * HEAD


def call(kernel, name, out_shape, ins, after=(), through=(), **kw):
    specs = [spec for spec, _ in ins]
    args = tuple(pltpu.with_memory_space_constraint(a, pltpu.HBM) if spec is HBM else a for spec, a in ins)
    n_in = len(args) + len(after)
    single = not isinstance(out_shape, (list, tuple))
    outs = [out_shape] if single else list(out_shape)
    kw.setdefault("out_specs", [VMEM] * len(outs))

    n_out = len(outs)
    if through:
        kw["input_output_aliases"] = {n_in + j: n_out + j for j in range(len(through))}
        outs += [jax.ShapeDtypeStruct(a.shape, a.dtype) for a in through]
        kw["out_specs"] = list(kw["out_specs"]) + [ANY] * len(through)
        single = False

    def run(*refs):
        first = n_in + len(through)
        kernel(*refs[: len(args)], *refs[first : first + n_out], *refs[first + n_out + len(through) :])

    got = pl.pallas_call(
        run,
        in_specs=list(specs) + [ANY] * (len(after) + len(through)),
        out_shape=outs,
        compiler_params=pltpu.CompilerParams(vmem_limit_bytes=VMEM_LIMIT),
        cost_estimate=pl.CostEstimate(flops=1000, bytes_accessed=1000, transcendentals=0),
        name=name,
        **kw,
    )(*args, *after, *through)
    return got[0] if single else got


def shape(*dims, dtype=BF16):
    return jax.ShapeDtypeStruct(dims, dtype)


def probs_kernel(at_ref, q_ref, k_ref, up_ref, p_ref, dv_ref, bias_ref, s_ref, dv_acc):
    row = lax.broadcasted_iota(jnp.int32, (COUNT, 1), 0)
    start = jnp.zeros((COUNT, 1), jnp.int32)
    end = jnp.int32(0)
    for doc in range(3):
        end = end + at_ref[5 + doc]
        start = jnp.where(row >= end, end, start)
    rows = lax.broadcasted_iota(jnp.int32, (COUNT, COUNT), 0)
    cols = lax.broadcasted_iota(jnp.int32, (COUNT, COUNT), 1)
    bias_ref[...] = jnp.where((cols <= rows) & (cols >= start), 0.0, -1e30).astype(F32)
    dv_acc[...] = jnp.zeros_like(dv_acc)
    for i in range(BLOCKS):
        width = BLOCK * (i + 1)
        at = pl.ds(BLOCK * i, BLOCK)
        qs = jnp.concatenate([q_ref[at, pl.ds(HEAD * h, HEAD)] for h in range(GROUP)], axis=0)
        s_ref[:, :width] = dot(qs, k_ref[:width, :], (1, 1))
        for h in range(GROUP):
            scores = s_ref[pl.ds(BLOCK * h, BLOCK), :width] * (FACTOR * LOG2E) + bias_ref[at, :width]
            expo = jnp.exp2(scores - jnp.max(scores, axis=1, keepdims=True))
            probs = expo * (1.0 / jnp.sum(expo, axis=1, keepdims=True))
            p_ref[h, at, :width] = probs.astype(BF16)
        low = jnp.concatenate([p_ref[h, at, :width] for h in range(GROUP)], axis=0)
        ups = jnp.concatenate([up_ref[at, pl.ds(HEAD * h, HEAD)] for h in range(GROUP)], axis=0)
        dv_acc[:, :width] += dot(ups, low, (0, 0))
    dv_ref[...] = dv_acc[...].T


PROBS_SCRATCH = [pltpu.VMEM((COUNT, COUNT), F32), pltpu.VMEM((GROUP * BLOCK, COUNT), F32), pltpu.VMEM((HEAD, COUNT), F32)]


def first_probs_kernel(
    at_ref, q_hbm, k_hbm, up_hbm, hidden_hbm, p_ref, dv_ref, hidden_out, q_ref, k_ref, up_ref, sems, *scratch
):
    copies = [
        pltpu.make_async_copy(a.at[:, pl.ds(0, b.shape[1])], b, sems.at[j])
        for j, (a, b) in enumerate(((q_hbm, q_ref), (k_hbm, k_ref), (up_hbm, up_ref)))
    ]
    for copy in copies:
        copy.start()
    whole = pltpu.make_async_copy(hidden_hbm, hidden_out, sems.at[3])
    whole.start()
    for copy in copies:
        copy.wait()
    probs_kernel(at_ref, q_ref, k_ref, up_ref, p_ref, dv_ref, *scratch)
    whole.wait()


def probs_part(g, at, queries, keys, upstream, dv, after, hidden=None):
    wide = pl.BlockSpec((COUNT, WIDE), lambda i: (0, g))
    narrow = pl.BlockSpec((COUNT, HEAD), lambda i: (0, g))
    outs = [shape(GROUP, COUNT, COUNT), shape(COUNT, 4 * HEAD, dtype=F32)]
    if hidden is not None:
        blocks = [pltpu.VMEM((COUNT, WIDE), BF16), pltpu.VMEM((COUNT, HEAD), BF16), pltpu.VMEM((COUNT, WIDE), BF16)]
        return call(
            first_probs_kernel, "probs_part", outs + [shape(*hidden.shape)],
            [(SMEM, at), (HBM, queries), (HBM, keys), (HBM, upstream), (HBM, hidden)], after, out_specs=[VMEM, narrow, ANY],
            grid=(1,), scratch_shapes=blocks + [pltpu.SemaphoreType.DMA((4,))] + PROBS_SCRATCH,
        )

    def kernel(*refs):
        probs_kernel(*refs[:4], *refs[5:])

    return call(
        kernel, "probs_part", outs, [(SMEM, at), (wide, queries), (narrow, keys), (wide, upstream), (ANY, dv)], after,
        out_specs=[VMEM, narrow], grid=(1,), scratch_shapes=PROBS_SCRATCH, input_output_aliases={4: 1},
    )


def grads_kernel(g, at_ref, q_ref, k_ref, up_ref, mine_ref, theirs_ref, p_ref, gq_ref, gk_ref, token_ref, dp_ref, ds_ref, dk_acc):
    token_ref[...] = jnp.zeros_like(token_ref)
    dk_acc[...] = jnp.zeros_like(dk_acc)
    col = pl.ds(HEAD * (g % 2), HEAD)
    all_values = jnp.where(at_ref[3] == g // 2, mine_ref[:, col], theirs_ref[:, col])
    for i in range(BLOCKS):
        width = BLOCK * (i + 1)
        at = pl.ds(BLOCK * i, BLOCK)
        ups = jnp.concatenate([up_ref[at, pl.ds(HEAD * h, HEAD)] for h in range(GROUP)], axis=0)
        dp_ref[:, :width] = dot(ups, all_values[:width], (1, 1))
        for h in range(GROUP):
            rows = pl.ds(BLOCK * h, BLOCK)
            dprobs = dp_ref[rows, :width]
            probs = p_ref[h, at, :width].astype(F32)
            delta = jnp.sum(probs * dprobs, axis=1, keepdims=True)
            ds_ref[rows, :width] = (probs * (dprobs - delta)).astype(BF16)
        dscores = ds_ref[:, :width]
        gq = dot(dscores, k_ref[:width, :], (1, 0)) * FACTOR
        for h in range(GROUP):
            gq_ref[at, pl.ds(HEAD * h, HEAD)] = gq[BLOCK * h : BLOCK * (h + 1)].astype(BF16)
        qs = jnp.concatenate([q_ref[at, pl.ds(HEAD * h, HEAD)] for h in range(GROUP)], axis=0)
        dk_acc[:, :width] += dot(qs, dscores, (0, 0))
    gk_ref[...] = (dk_acc[...] * FACTOR).T.astype(BF16)


def grads_part(g, at, queries, keys, upstream, mine, theirs, probs, held, after):
    wide = pl.BlockSpec((COUNT, WIDE), lambda i: (0, g))
    narrow = pl.BlockSpec((COUNT, HEAD), lambda i: (0, g))
    ins = [(SMEM, at), (wide, queries), (narrow, keys), (wide, upstream), (VMEM, mine), (VMEM, theirs), (VMEM, probs)]

    def kernel(*refs):
        grads_kernel(g, *refs[:7], *refs[len(refs) - 6 :])

    extra = {}
    if held is not None:
        ins += [(ANY, held[0]), (ANY, held[1])]
        extra["input_output_aliases"] = {7: 0, 8: 1}
    return call(
        kernel, "grads_part", [shape(*queries.shape), shape(*keys.shape), TOKEN], ins, after,
        out_specs=[wide, narrow, VMEM], grid=(1,),
        scratch_shapes=[pltpu.VMEM((GROUP * BLOCK, COUNT), F32), pltpu.VMEM((GROUP * BLOCK, COUNT), BF16), pltpu.VMEM((HEAD, COUNT), F32)], **extra,
    )


SHARD = 32
CHIP = 2 * SHARD
HALF = 256
DEPTH = 4096


def own_columns(at_ref):
    return pl.ds(pl.multiple_of(at_ref[3] * HALF, HALF), HALF)


def first_join(own_hbm, other_ref, out_ref, sem):
    c = lax.rem(lax.axis_index("dp"), 2)
    cols = pl.ds(pl.multiple_of(c * HALF, HALF), HALF)
    copy = pltpu.make_async_copy(
        own_hbm.at[:, cols], out_ref.at[pl.ds(pl.multiple_of(c * SHARD, SHARD), SHARD), :], sem
    )
    copy.start()
    out_ref[pl.ds(pl.multiple_of((1 - c) * SHARD, SHARD), SHARD), :] = other_ref[:, cols]
    copy.wait()


def join_kernel(own_ref, other_ref, out_ref):
    n = own_ref.shape[0]
    out_ref[:n, :] = own_ref[...]
    out_ref[n:, :] = other_ref[...]


def join_split_kernel(own_ref, other_ref, first_ref, second_ref):
    n = own_ref.shape[0]
    for j, out_ref in enumerate((first_ref, second_ref)):
        out_ref[:n, :] = own_ref[:, HEAD * j : HEAD * (j + 1)]
        out_ref[n:, :] = other_ref[:, HEAD * j : HEAD * (j + 1)]


def two_joins_kernel(at_ref, dv_ref, a0, a1, b0, b1, b2, b3, first_ref, second_ref, dv_out):
    dv_out[...] = dv_ref[:, pl.ds(pl.multiple_of((1 - at_ref[3]) * HALF, HALF), HALF)].astype(BF16)
    n = a0.shape[0]
    for j, part in enumerate((a0, a1)):
        first_ref[n * j : n * (j + 1), :] = part[...]
    for j, part in enumerate((b0, b1, b2, b3)):
        second_ref[n * j : n * (j + 1), :] = part[...]


def put_in_order(at_ref, pieces, codes_ref):
    z, y, x = at_ref[0], at_ref[1], at_ref[2]

    def place(piece, row, i, k, xi, col):
        zi = (i & 1) * 4 + (i & 2) + (i >> 2)
        to = ((z ^ zi) * 4 + ((y + 4 - k) & 3)) * 2 + (x ^ xi)
        rows = pl.ds(pl.multiple_of(to * CHIP, CHIP), CHIP)
        codes_ref[rows, pl.ds(col, HEAD)] = piece[pl.ds(row, CHIP), :]

    for k in range(4):
        for xi in range(2):
            for i in range(8):
                place(pieces[k], (xi * 8 + i) * CHIP, i, k, xi, 0)
                place(pieces[4 + xi], (k * 8 + i) * CHIP, i, k, xi, HEAD)


NEAR = 512
BESIDES = DEPTH // 2 - NEAR


def raw_kernel(at_ref, own_ref, other_ref, dv_own, dv_other, scale_ref, *refs):
    pieces, (mine_ref, theirs_ref, sums_ref, kept_ref, near_ref, beside_ref, codes_ref) = refs[:6], refs[6:]
    put_in_order(at_ref, pieces, codes_ref)
    cols = own_columns(at_ref)
    scale = scale_ref[:, cols]
    sums = jnp.zeros((1, HALF), F32)
    terms = ((other_ref, dv_other[...].astype(F32), theirs_ref), (own_ref, dv_own[:, cols], mine_ref))
    for hidden_ref, dv, values_ref in terms:
        raw = dot(hidden_ref[...], codes_ref[...], (1, 0))
        values_ref[...] = (raw * scale).astype(BF16)
        sums += jnp.sum(raw * dv, axis=0, keepdims=True)
    sums_ref[...] = sums
    s, half = at_ref[4], DEPTH // 2
    kept_ref[...] = codes_ref[pl.ds(pl.multiple_of(s * half, half), half), :]
    base = (1 - s) * half
    for j in range(2):
        part = pl.ds(j * HALF, HALF)
        near_ref[pl.ds(j * COUNT, COUNT), :] = (dv_own[:, part] * scale_ref[:, part]).astype(BF16)
    near_ref[2 * COUNT :, :] = codes_ref[pl.ds(pl.multiple_of(base, half), NEAR), :]
    beside_ref[...] = codes_ref[pl.ds(pl.multiple_of(base + NEAR, 128), BESIDES), :]


def raw_part(at, hidden, hidden_other, dv, dv_other, scale, pieces):
    outs = [shape(COUNT, HALF), shape(COUNT, HALF), shape(1, HALF, dtype=F32)]
    outs += [shape(DEPTH // 2, HALF), shape(2 * COUNT + NEAR, HALF), shape(BESIDES, HALF)]
    return call(
        raw_kernel, "raw_part", outs,
        [(SMEM, at)] + [(VMEM, a) for a in [hidden, hidden_other, dv, dv_other, scale] + pieces],
        scratch_shapes=[pltpu.VMEM((DEPTH, HALF), BF16)],
    )


BATCH = 512


def hidden_kernel(first, at_ref, dv_ref, scale_ref, near_ref, codes_ref, codes_far, kept_ref, kept_far, *refs):
    out_ref, token_ref, part_ref, sem = refs[-4:]
    token_ref[...] = jnp.zeros_like(token_ref)
    base, size, skip = (0, NEAR, 2 * COUNT) if first else (NEAR, BESIDES, 0)
    sides = []
    for other, codes, kept in ((0, codes_ref, kept_ref), (1, codes_far, kept_far)):
        c = at_ref[3] ^ other
        cols = pl.ds(pl.multiple_of(c * HALF, HALF), HALF)
        own = (dv_ref[:, cols] * scale_ref[:, cols]).astype(BF16)
        seq = near_ref[pl.ds(pl.multiple_of(c * COUNT, COUNT), COUNT), :]
        sides.append((own, seq, codes, kept))
    for at in range(0, size, BATCH):
        end = min(at + BATCH, size)
        total = 0.0
        for own, seq, codes, kept in sides:
            total += dot(own, kept[base + at : base + end, :], (1, 1))
            total += dot(seq, codes[skip + at : skip + end, :], (1, 1))
        part_ref[:, at:end] = total.astype(BF16)
    copy = pltpu.make_async_copy(part_ref, out_ref.at[:, pl.ds(base, size)], sem)
    copy.start()
    copy.wait()


def hidden_part(first, arrays, held, after):
    extra = {}
    ins = [(SMEM, arrays[0])] + [(VMEM, a) for a in arrays[1:]]
    if held is not None:
        extra["input_output_aliases"] = {len(ins): 0}
        ins.append((ANY, held))
    return call(
        functools.partial(hidden_kernel, first), "hidden_part", [shape(COUNT, DEPTH // 2), TOKEN], ins, after,
        out_specs=[ANY, VMEM],
        scratch_shapes=[pltpu.VMEM((COUNT, NEAR if first else BESIDES), BF16), pltpu.SemaphoreType.DMA], **extra,
    )


def add_kernel(a_ref, b_ref, out_ref):
    out_ref[...] = a_ref[...] + b_ref[...]


def pairs(move):
    out = []
    for i in range(128):
        z, y, x, c = move(i // 16, i // 4 % 4, i // 2 % 2, i % 2)
        out.append((i, ((z * 4 + y) * 2 + x) * 2 + c))
    return out


def z_swap(bit):
    return pairs(lambda z, y, x, c: (z ^ bit, y, x, c))


def y_shift(k):
    return pairs(lambda z, y, x, c: (z, (y + k) % 4, x, c))


def y_swap(bit):
    return pairs(lambda z, y, x, c: (z, y ^ bit, x, c))


X_SWAP = pairs(lambda z, y, x, c: (z, y, x ^ 1, c))
C_SWAP = pairs(lambda z, y, x, c: (z, y, x, c ^ 1))
SEQ_SWAP = [(0, 1), (1, 0)]
BESIDE = [(2 * a + s, 2 * b + 1 - s) for a, b in X_SWAP for s in range(2)]


def send(x, perm):
    return lax.ppermute(x, "dp", perm)


def shards(hidden, queries, keys, value_codes, value_scale, upstream, lengths):
    me, s = lax.axis_index("dp"), lax.axis_index("seq")
    place = jnp.stack([me // 16, me // 4 % 4, me // 2 % 2, me % 2, s]).astype(jnp.int32)
    at = jnp.concatenate([place, lengths[0, :3]])
    scale = value_scale.reshape(1, -1)

    rows = call(
        first_join, "join", shape(CHIP, HALF), [(HBM, value_codes), (VMEM, send(value_codes, C_SWAP))], (at,),
        scratch_shapes=[pltpu.SemaphoreType.DMA],
    )
    probs, dv = [], None
    for bit, heads in ((4, (0,)), (2, (1,)), (1, (2,))):
        got = send(rows, z_swap(bit))
        for g in heads:
            if g == 0:
                p, dv, hidden = probs_part(g, at, queries, keys, upstream, dv, (rows,), hidden)
            else:
                p, dv = probs_part(g, at, queries, keys, upstream, dv, (rows,))
            probs.append(p)
        n = rows.shape[0]
        ins = [(VMEM, rows), (VMEM, got)]
        if bit == 4:
            rows, hidden = call(join_kernel, "join", shape(2 * n, HALF), ins, (p,), (hidden,))
            hidden_other = send(hidden, C_SWAP)
        elif bit == 2:
            rows = call(join_kernel, "join", shape(2 * n, HALF), ins, (p,))
        else:
            first, second = call(join_split_kernel, "join", [shape(2 * n, HEAD)] * 2, ins, (hidden_other, p))
    first_x = send(first, X_SWAP)
    second_y = [send(second, y_shift(k)) for k in (1, 2, 3)]
    p, dv = probs_part(3, at, queries, keys, upstream, dv, (first,))
    probs.append(p)
    n = first.shape[0]
    first, second, dv_half = call(
        two_joins_kernel, "join", [shape(2 * n, HEAD), shape(4 * n, HEAD), shape(COUNT, HALF)],
        [(SMEM, at)] + [(VMEM, a) for a in [dv, first, first_x, second] + second_y],
    )
    pieces = [first] + [send(first, y_shift(k)) for k in (1, 2, 3)] + [second, send(second, X_SWAP)]
    dv_other = send(dv_half, C_SWAP)
    mine, theirs, sums, kept, near, beside = raw_part(at, hidden, hidden_other, dv, dv_other, scale, pieces)

    held = None
    for step, perm in enumerate((y_swap(1), y_swap(2), z_swap(1), z_swap(2), z_swap(4), X_SWAP)):
        got = send(sums, perm)
        after, through = (), ()
        if step == 0:
            values_far = send(theirs, C_SWAP)
            near = lax.ppermute(near, "seq", SEQ_SWAP)
            beside = lax.ppermute(beside, ("dp", "seq"), BESIDE)
            kept_far = send(kept, C_SWAP)
            after = (values_far, kept_far)
        elif step < 5:
            g = step - 1
            if step == 4:
                near_far = send(near, C_SWAP)
            *held, token = grads_part(g, at, queries, keys, upstream, mine, values_far, probs[g], held, (sums,))
            if step == 4:
                grad_hidden, token = hidden_part(
                    True, (at, dv, scale, near, near, near_far, kept, kept_far), None, (token,)
                )
            after = (token,)
        else:
            beside_far = send(beside, C_SWAP)
            grad_hidden, token = hidden_part(
                False, (at, dv, scale, near, beside, beside_far, kept, kept_far), grad_hidden, (sums,)
            )
            after = (token,)
        ins = [(VMEM, sums), (VMEM, got)]
        if step == 3:
            sums, near = call(add_kernel, "add", shape(1, HALF, dtype=F32), ins, after, (near,))
        elif step == 4:
            sums, beside = call(add_kernel, "add", shape(1, HALF, dtype=F32), ins, after, (beside,))
        else:
            sums = call(add_kernel, "add", shape(1, HALF, dtype=F32), ins, after)
    far = send(sums, C_SWAP)
    both = jnp.concatenate([jnp.where(me % 2 == 0, sums, far), jnp.where(me % 2 == 0, far, sums)], axis=1)
    return held[0], held[1], grad_hidden, (both * scale).reshape(-1)


def solution(mesh):
    placed = (
        P("dp", None),
        P("dp", "seq"),
        P("dp", "seq"),
        P("dp", "seq"),
        P("seq"),
        P("dp", "seq"),
        P("dp", None),
    )
    return jax.shard_map(
        shards,
        mesh=mesh,
        in_specs=placed,
        out_specs=(P("dp", "seq"), P("dp", "seq"), P("dp", "seq"), P("seq")),
        check_vma=False,
    )
```

```python
import functools
import math

import jax
import jax.numpy as jnp
from jax import lax
from jax.experimental import pallas as pl
from jax.experimental.pallas import tpu as pltpu
from jax.sharding import PartitionSpec as P

COUNT = 384
HEAD = 128
GROUP = 4
BLOCK = 128
BLOCKS = COUNT // BLOCK
FACTOR = 1.0 / math.sqrt(HEAD)
LOG2E = math.log2(math.e)
BF16 = jnp.bfloat16
F32 = jnp.float32
VMEM_LIMIT = 16 * 1024 * 1024


def dot(a, b, dims):
    return lax.dot_general(a, b, ((dims[:1], dims[1:]), ((), ())), preferred_element_type=F32)

VMEM = pl.BlockSpec(memory_space=pltpu.VMEM)
SMEM = pl.BlockSpec(memory_space=pltpu.SMEM)
ANY = pl.BlockSpec(memory_space=pl.ANY)
HBM = pl.BlockSpec(memory_space=pltpu.HBM)
TOKEN = jax.ShapeDtypeStruct((8, 128), F32)
WIDE = GROUP * HEAD


def call(kernel, name, out_shape, ins, after=(), through=(), **kw):
    specs = [spec for spec, _ in ins]
    args = tuple(pltpu.with_memory_space_constraint(a, pltpu.HBM) if spec is HBM else a for spec, a in ins)
    n_in = len(args) + len(after)
    single = not isinstance(out_shape, (list, tuple))
    outs = [out_shape] if single else list(out_shape)
    kw.setdefault("out_specs", [VMEM] * len(outs))

    n_out = len(outs)
    if through:
        kw["input_output_aliases"] = {n_in + j: n_out + j for j in range(len(through))}
        outs += [jax.ShapeDtypeStruct(a.shape, a.dtype) for a in through]
        kw["out_specs"] = list(kw["out_specs"]) + [ANY] * len(through)
        single = False

    def run(*refs):
        first = n_in + len(through)
        kernel(*refs[: len(args)], *refs[first : first + n_out], *refs[first + n_out + len(through) :])

    got = pl.pallas_call(
        run,
        in_specs=list(specs) + [ANY] * (len(after) + len(through)),
        out_shape=outs,
        compiler_params=pltpu.CompilerParams(vmem_limit_bytes=VMEM_LIMIT),
        cost_estimate=pl.CostEstimate(flops=1000, bytes_accessed=1000, transcendentals=0),
        name=name,
        **kw,
    )(*args, *after, *through)
    return got[0] if single else got


def shape(*dims, dtype=BF16):
    return jax.ShapeDtypeStruct(dims, dtype)


def probs_kernel(at_ref, q_ref, k_ref, up_ref, p_ref, dv_ref, bias_ref, s_ref, dv_acc):
    row = lax.broadcasted_iota(jnp.int32, (COUNT, 1), 0)
    start = jnp.zeros((COUNT, 1), jnp.int32)
    end = jnp.int32(0)
    for doc in range(3):
        end = end + at_ref[5 + doc]
        start = jnp.where(row >= end, end, start)
    rows = lax.broadcasted_iota(jnp.int32, (COUNT, COUNT), 0)
    cols = lax.broadcasted_iota(jnp.int32, (COUNT, COUNT), 1)
    bias_ref[...] = jnp.where((cols <= rows) & (cols >= start), 0.0, -1e30).astype(F32)
    dv_acc[...] = jnp.zeros_like(dv_acc)
    for i in range(BLOCKS):
        width = BLOCK * (i + 1)
        at = pl.ds(BLOCK * i, BLOCK)
        qs = jnp.concatenate([q_ref[at, pl.ds(HEAD * h, HEAD)] for h in range(GROUP)], axis=0)
        s_ref[:, :width] = dot(qs, k_ref[:width, :], (1, 1))
        for h in range(GROUP):
            scores = s_ref[pl.ds(BLOCK * h, BLOCK), :width] * (FACTOR * LOG2E) + bias_ref[at, :width]
            expo = jnp.exp2(scores - jnp.max(scores, axis=1, keepdims=True))
            probs = expo * (1.0 / jnp.sum(expo, axis=1, keepdims=True))
            p_ref[h, at, :width] = probs.astype(BF16)
        low = jnp.concatenate([p_ref[h, at, :width] for h in range(GROUP)], axis=0)
        ups = jnp.concatenate([up_ref[at, pl.ds(HEAD * h, HEAD)] for h in range(GROUP)], axis=0)
        dv_acc[:, :width] += dot(ups, low, (0, 0))
    dv_ref[...] = dv_acc[...].T


PROBS_SCRATCH = [pltpu.VMEM((COUNT, COUNT), F32), pltpu.VMEM((GROUP * BLOCK, COUNT), F32), pltpu.VMEM((HEAD, COUNT), F32)]


def first_probs_kernel(
    at_ref, q_hbm, k_hbm, up_hbm, hidden_hbm, p_ref, dv_ref, hidden_out, q_ref, k_ref, up_ref, sems, *scratch
):
    copies = [
        pltpu.make_async_copy(a.at[:, pl.ds(0, b.shape[1])], b, sems.at[j])
        for j, (a, b) in enumerate(((q_hbm, q_ref), (k_hbm, k_ref), (up_hbm, up_ref)))
    ]
    for copy in copies:
        copy.start()
    whole = pltpu.make_async_copy(hidden_hbm, hidden_out, sems.at[3])
    whole.start()
    for copy in copies:
        copy.wait()
    probs_kernel(at_ref, q_ref, k_ref, up_ref, p_ref, dv_ref, *scratch)
    whole.wait()


def probs_part(g, at, queries, keys, upstream, dv, after, hidden=None):
    wide = pl.BlockSpec((COUNT, WIDE), lambda i: (0, g))
    narrow = pl.BlockSpec((COUNT, HEAD), lambda i: (0, g))
    outs = [shape(GROUP, COUNT, COUNT), shape(COUNT, 4 * HEAD, dtype=F32)]
    if hidden is not None:
        blocks = [pltpu.VMEM((COUNT, WIDE), BF16), pltpu.VMEM((COUNT, HEAD), BF16), pltpu.VMEM((COUNT, WIDE), BF16)]
        return call(
            first_probs_kernel, "probs_part", outs + [shape(*hidden.shape)],
            [(SMEM, at), (HBM, queries), (HBM, keys), (HBM, upstream), (HBM, hidden)], after, out_specs=[VMEM, narrow, ANY],
            grid=(1,), scratch_shapes=blocks + [pltpu.SemaphoreType.DMA((4,))] + PROBS_SCRATCH,
        )

    def kernel(*refs):
        probs_kernel(*refs[:4], *refs[5:])

    return call(
        kernel, "probs_part", outs, [(SMEM, at), (wide, queries), (narrow, keys), (wide, upstream), (ANY, dv)], after,
        out_specs=[VMEM, narrow], grid=(1,), scratch_shapes=PROBS_SCRATCH, input_output_aliases={4: 1},
    )


def grads_kernel(g, at_ref, q_ref, k_ref, up_ref, mine_ref, theirs_ref, p_ref, gq_ref, gk_ref, token_ref, dp_ref, ds_ref, dk_acc):
    token_ref[...] = jnp.zeros_like(token_ref)
    dk_acc[...] = jnp.zeros_like(dk_acc)
    col = pl.ds(HEAD * (g % 2), HEAD)
    all_values = jnp.where(at_ref[3] == g // 2, mine_ref[:, col], theirs_ref[:, col])
    for i in range(BLOCKS):
        width = BLOCK * (i + 1)
        at = pl.ds(BLOCK * i, BLOCK)
        ups = jnp.concatenate([up_ref[at, pl.ds(HEAD * h, HEAD)] for h in range(GROUP)], axis=0)
        dp_ref[:, :width] = dot(ups, all_values[:width], (1, 1))
        for h in range(GROUP):
            rows = pl.ds(BLOCK * h, BLOCK)
            dprobs = dp_ref[rows, :width]
            probs = p_ref[h, at, :width].astype(F32)
            delta = jnp.sum(probs * dprobs, axis=1, keepdims=True)
            ds_ref[rows, :width] = (probs * (dprobs - delta)).astype(BF16)
        dscores = ds_ref[:, :width]
        gq = dot(dscores, k_ref[:width, :], (1, 0)) * FACTOR
        for h in range(GROUP):
            gq_ref[at, pl.ds(HEAD * h, HEAD)] = gq[BLOCK * h : BLOCK * (h + 1)].astype(BF16)
        qs = jnp.concatenate([q_ref[at, pl.ds(HEAD * h, HEAD)] for h in range(GROUP)], axis=0)
        dk_acc[:, :width] += dot(qs, dscores, (0, 0))
    gk_ref[...] = (dk_acc[...] * FACTOR).T.astype(BF16)


def grads_part(g, at, queries, keys, upstream, mine, theirs, probs, held, after):
    wide = pl.BlockSpec((COUNT, WIDE), lambda i: (0, g))
    narrow = pl.BlockSpec((COUNT, HEAD), lambda i: (0, g))
    ins = [(SMEM, at), (wide, queries), (narrow, keys), (wide, upstream), (VMEM, mine), (VMEM, theirs), (VMEM, probs)]

    def kernel(*refs):
        grads_kernel(g, *refs[:7], *refs[len(refs) - 6 :])

    extra = {}
    if held is not None:
        ins += [(ANY, held[0]), (ANY, held[1])]
        extra["input_output_aliases"] = {7: 0, 8: 1}
    return call(
        kernel, "grads_part", [shape(*queries.shape), shape(*keys.shape), TOKEN], ins, after,
        out_specs=[wide, narrow, VMEM], grid=(1,),
        scratch_shapes=[pltpu.VMEM((GROUP * BLOCK, COUNT), F32), pltpu.VMEM((GROUP * BLOCK, COUNT), BF16), pltpu.VMEM((HEAD, COUNT), F32)], **extra,
    )


SHARD = 32
CHIP = 2 * SHARD
HALF = 256
DEPTH = 4096


def own_columns(at_ref):
    return pl.ds(pl.multiple_of(at_ref[3] * HALF, HALF), HALF)


def first_join(own_hbm, other_ref, out_ref, sem):
    c = lax.rem(lax.axis_index("dp"), 2)
    cols = pl.ds(pl.multiple_of(c * HALF, HALF), HALF)
    copy = pltpu.make_async_copy(
        own_hbm.at[:, cols], out_ref.at[pl.ds(pl.multiple_of(c * SHARD, SHARD), SHARD), :], sem
    )
    copy.start()
    out_ref[pl.ds(pl.multiple_of((1 - c) * SHARD, SHARD), SHARD), :] = other_ref[:, cols]
    copy.wait()


def join_kernel(own_ref, other_ref, out_ref):
    n = own_ref.shape[0]
    out_ref[:n, :] = own_ref[...]
    out_ref[n:, :] = other_ref[...]


def join_split_kernel(own_ref, other_ref, first_ref, second_ref):
    n = own_ref.shape[0]
    for j, out_ref in enumerate((first_ref, second_ref)):
        out_ref[:n, :] = own_ref[:, HEAD * j : HEAD * (j + 1)]
        out_ref[n:, :] = other_ref[:, HEAD * j : HEAD * (j + 1)]


def two_joins_kernel(at_ref, dv_ref, a0, a1, b0, b1, b2, b3, first_ref, second_ref, dv_out):
    dv_out[...] = dv_ref[:, pl.ds(pl.multiple_of((1 - at_ref[3]) * HALF, HALF), HALF)].astype(BF16)
    n = a0.shape[0]
    for j, part in enumerate((a0, a1)):
        first_ref[n * j : n * (j + 1), :] = part[...]
    for j, part in enumerate((b0, b1, b2, b3)):
        second_ref[n * j : n * (j + 1), :] = part[...]


def put_in_order(at_ref, pieces, codes_ref):
    z, y, x = at_ref[0], at_ref[1], at_ref[2]

    def place(piece, row, i, k, xi, col):
        zi = (i & 1) * 4 + (i & 2) + (i >> 2)
        to = ((z ^ zi) * 4 + ((y + 4 - k) & 3)) * 2 + (x ^ xi)
        rows = pl.ds(pl.multiple_of(to * CHIP, CHIP), CHIP)
        codes_ref[rows, pl.ds(col, HEAD)] = piece[pl.ds(row, CHIP), :]

    for k in range(4):
        for xi in range(2):
            for i in range(8):
                place(pieces[k], (xi * 8 + i) * CHIP, i, k, xi, 0)
                place(pieces[4 + xi], (k * 8 + i) * CHIP, i, k, xi, HEAD)


NEAR = 512
BESIDES = DEPTH // 2 - NEAR


def raw_kernel(at_ref, own_ref, other_ref, dv_own, dv_other, scale_ref, *refs):
    pieces, (mine_ref, theirs_ref, sums_ref, kept_ref, near_ref, beside_ref, codes_ref) = refs[:6], refs[6:]
    put_in_order(at_ref, pieces, codes_ref)
    cols = own_columns(at_ref)
    scale = scale_ref[:, cols]
    sums = jnp.zeros((1, HALF), F32)
    terms = ((other_ref, dv_other[...].astype(F32), theirs_ref), (own_ref, dv_own[:, cols], mine_ref))
    for hidden_ref, dv, values_ref in terms:
        raw = dot(hidden_ref[...], codes_ref[...], (1, 0))
        values_ref[...] = (raw * scale).astype(BF16)
        sums += jnp.sum(raw * dv, axis=0, keepdims=True)
    sums_ref[...] = sums
    s, half = at_ref[4], DEPTH // 2
    kept_ref[...] = codes_ref[pl.ds(pl.multiple_of(s * half, half), half), :]
    base = (1 - s) * half
    for j in range(2):
        part = pl.ds(j * HALF, HALF)
        near_ref[pl.ds(j * COUNT, COUNT), :] = (dv_own[:, part] * scale_ref[:, part]).astype(BF16)
    near_ref[2 * COUNT :, :] = codes_ref[pl.ds(pl.multiple_of(base, half), NEAR), :]
    beside_ref[...] = codes_ref[pl.ds(pl.multiple_of(base + NEAR, 128), BESIDES), :]


def raw_part(at, hidden, hidden_other, dv, dv_other, scale, pieces):
    outs = [shape(COUNT, HALF), shape(COUNT, HALF), shape(1, HALF, dtype=F32)]
    outs += [shape(DEPTH // 2, HALF), shape(2 * COUNT + NEAR, HALF), shape(BESIDES, HALF)]
    return call(
        raw_kernel, "raw_part", outs,
        [(SMEM, at)] + [(VMEM, a) for a in [hidden, hidden_other, dv, dv_other, scale] + pieces],
        scratch_shapes=[pltpu.VMEM((DEPTH, HALF), BF16)],
    )


BATCH = 512


def hidden_kernel(first, at_ref, dv_ref, scale_ref, near_ref, codes_ref, codes_far, kept_ref, kept_far, *refs):
    out_ref, token_ref, part_ref, sem = refs[-4:]
    token_ref[...] = jnp.zeros_like(token_ref)
    base, size, skip = (0, NEAR, 2 * COUNT) if first else (NEAR, BESIDES, 0)
    sides = []
    for other, codes, kept in ((0, codes_ref, kept_ref), (1, codes_far, kept_far)):
        c = at_ref[3] ^ other
        cols = pl.ds(pl.multiple_of(c * HALF, HALF), HALF)
        own = (dv_ref[:, cols] * scale_ref[:, cols]).astype(BF16)
        seq = near_ref[pl.ds(pl.multiple_of(c * COUNT, COUNT), COUNT), :]
        sides.append((own, seq, codes, kept))
    for at in range(0, size, BATCH):
        end = min(at + BATCH, size)
        total = 0.0
        for own, seq, codes, kept in sides:
            total += dot(own, kept[base + at : base + end, :], (1, 1))
            total += dot(seq, codes[skip + at : skip + end, :], (1, 1))
        part_ref[:, at:end] = total.astype(BF16)
    copy = pltpu.make_async_copy(part_ref, out_ref.at[:, pl.ds(base, size)], sem)
    copy.start()
    copy.wait()


def hidden_part(first, arrays, held, after):
    extra = {}
    ins = [(SMEM, arrays[0])] + [(VMEM, a) for a in arrays[1:]]
    if held is not None:
        extra["input_output_aliases"] = {len(ins): 0}
        ins.append((ANY, held))
    return call(
        functools.partial(hidden_kernel, first), "hidden_part", [shape(COUNT, DEPTH // 2), TOKEN], ins, after,
        out_specs=[ANY, VMEM],
        scratch_shapes=[pltpu.VMEM((COUNT, NEAR if first else BESIDES), BF16), pltpu.SemaphoreType.DMA], **extra,
    )


def add_kernel(a_ref, b_ref, out_ref):
    out_ref[...] = a_ref[...] + b_ref[...]


def pairs(move):
    out = []
    for i in range(128):
        z, y, x, c = move(i // 16, i // 4 % 4, i // 2 % 2, i % 2)
        out.append((i, ((z * 4 + y) * 2 + x) * 2 + c))
    return out


def z_swap(bit):
    return pairs(lambda z, y, x, c: (z ^ bit, y, x, c))


def y_shift(k):
    return pairs(lambda z, y, x, c: (z, (y + k) % 4, x, c))


def y_swap(bit):
    return pairs(lambda z, y, x, c: (z, y ^ bit, x, c))


X_SWAP = pairs(lambda z, y, x, c: (z, y, x ^ 1, c))
C_SWAP = pairs(lambda z, y, x, c: (z, y, x, c ^ 1))
SEQ_SWAP = [(0, 1), (1, 0)]
BESIDE = [(2 * a + s, 2 * b + 1 - s) for a, b in X_SWAP for s in range(2)]


def send(x, perm):
    return lax.ppermute(x, "dp", perm)


def shards(hidden, queries, keys, value_codes, value_scale, upstream, lengths):
    me, s = lax.axis_index("dp"), lax.axis_index("seq")
    place = jnp.stack([me // 16, me // 4 % 4, me // 2 % 2, me % 2, s]).astype(jnp.int32)
    at = jnp.concatenate([place, lengths[0, :3]])
    scale = value_scale.reshape(1, -1)

    rows = call(
        first_join, "join", shape(CHIP, HALF), [(HBM, value_codes), (VMEM, send(value_codes, C_SWAP))], (at,),
        scratch_shapes=[pltpu.SemaphoreType.DMA],
    )
    probs, dv = [], None
    for bit, heads in ((4, (0,)), (2, (1,)), (1, (2,))):
        got = send(rows, z_swap(bit))
        for g in heads:
            if g == 0:
                p, dv, hidden = probs_part(g, at, queries, keys, upstream, dv, (rows,), hidden)
            else:
                p, dv = probs_part(g, at, queries, keys, upstream, dv, (rows,))
            probs.append(p)
        n = rows.shape[0]
        ins = [(VMEM, rows), (VMEM, got)]
        if bit == 4:
            rows, hidden = call(join_kernel, "join", shape(2 * n, HALF), ins, (p,), (hidden,))
            hidden_other = send(hidden, C_SWAP)
        elif bit == 2:
            rows = call(join_kernel, "join", shape(2 * n, HALF), ins, (p,))
        else:
            first, second = call(join_split_kernel, "join", [shape(2 * n, HEAD)] * 2, ins, (hidden_other, p))
    first_x = send(first, X_SWAP)
    second_y = [send(second, y_shift(k)) for k in (1, 2, 3)]
    p, dv = probs_part(3, at, queries, keys, upstream, dv, (first,))
    probs.append(p)
    n = first.shape[0]
    first, second, dv_half = call(
        two_joins_kernel, "join", [shape(2 * n, HEAD), shape(4 * n, HEAD), shape(COUNT, HALF)],
        [(SMEM, at)] + [(VMEM, a) for a in [dv, first, first_x, second] + second_y],
    )
    pieces = [first] + [send(first, y_shift(k)) for k in (1, 2, 3)] + [second, send(second, X_SWAP)]
    dv_other = send(dv_half, C_SWAP)
    mine, theirs, sums, kept, near, beside = raw_part(at, hidden, hidden_other, dv, dv_other, scale, pieces)

    held = None
    for step, perm in enumerate((y_swap(1), y_swap(2), z_swap(1), z_swap(2), z_swap(4), X_SWAP)):
        got = send(sums, perm)
        after = ()
        if step == 0:
            values_far = send(theirs, C_SWAP)
            near = lax.ppermute(near, "seq", SEQ_SWAP)
            beside = lax.ppermute(beside, ("dp", "seq"), BESIDE)
            kept_far = send(kept, C_SWAP)
            after = (kept_far,)
        if step < 4:
            *held, token = grads_part(
                step, at, queries, keys, upstream, mine, values_far, probs[step], held, (sums,)
            )
            after += (token,)
        elif step == 4:
            near_far = send(near, C_SWAP)
            grad_hidden, token = hidden_part(
                True, (at, dv, scale, near, near, near_far, kept, kept_far), None, (sums,)
            )
            after = (token,)
        else:
            beside_far = send(beside, C_SWAP)
            grad_hidden, token = hidden_part(
                False, (at, dv, scale, near, beside, beside_far, kept, kept_far), grad_hidden, (sums,)
            )
            after = (token,)
        ins = [(VMEM, sums), (VMEM, got)]
        if step == 3:
            sums, near = call(add_kernel, "add", shape(1, HALF, dtype=F32), ins, after, (near,))
        elif step == 4:
            sums, beside = call(add_kernel, "add", shape(1, HALF, dtype=F32), ins, after, (beside,))
        else:
            sums = call(add_kernel, "add", shape(1, HALF, dtype=F32), ins, after)
    far = send(sums, C_SWAP)
    both = jnp.concatenate([jnp.where(me % 2 == 0, sums, far), jnp.where(me % 2 == 0, far, sums)], axis=1)
    return held[0], held[1], grad_hidden, (both * scale).reshape(-1)


def solution(mesh):
    placed = (
        P("dp", None),
        P("dp", "seq"),
        P("dp", "seq"),
        P("dp", "seq"),
        P("seq"),
        P("dp", "seq"),
        P("dp", None),
    )
    return jax.shard_map(
        shards,
        mesh=mesh,
        in_specs=placed,
        out_specs=(P("dp", "seq"), P("dp", "seq"), P("dp", "seq"), P("seq")),
        check_vma=False,
    )
```
